32 devices in a mesh: dp: 8 (over z, core), fsdp: 4 (over y, x).
Axes of the slice: x: 2, y: 2, z: 4, core: 2. Of those that a mesh axis runs over, the one named last changes fastest.
Arguments:
- tokens: bfloat16 [16384, 1024], P(('dp', 'fsdp')), may hold values from -6 to 6
- first_values: bfloat16 [16384, 1024], P(('dp', 'fsdp')), may hold values from -12 to 12
- lengths: int32 [32], P(('dp', 'fsdp')), may hold values from 256 to 512, as said below
- gain_one: bfloat16 [1024], P('fsdp'), may hold values from 0.099609375 to 1.8984375
- w_qkv: bfloat16 [1024, 3072], P('fsdp'), may hold values from -0.1875 to 0.1875
- w_out: bfloat16 [1024, 1024], P('fsdp'), may hold values from -3 to 3
- gain_two: bfloat16 [1024], P('fsdp'), may hold values from 0.099609375 to 1.8984375
- w_gate: bfloat16 [1024, 2816], P('fsdp'), may hold values from -0.1875 to 0.1875
- w_up: bfloat16 [1024, 2816], P('fsdp'), may hold values from -0.1875 to 0.1875
- w_down: bfloat16 [2816, 1024], P('fsdp'), may hold values from -0.4375 to 0.4375
- cotangent: bfloat16 [16384, 1024], P(('dp', 'fsdp')), may hold values from -6 to 6
Outputs:
- output: bfloat16 [16384, 1024], P(('dp', 'fsdp'))
- grad_tokens: float32 [16384, 1024], P(('dp', 'fsdp'))
- grad_first_values: float32 [16384, 1024], P(('dp', 'fsdp'))
- grad_gain_one: float32 [1024], P('fsdp')
- grad_w_qkv: float32 [1024, 3072], P('fsdp')
- grad_w_out: float32 [1024, 1024], P('fsdp')
- grad_gain_two: float32 [1024], P('fsdp')
- grad_w_gate: float32 [1024, 2816], P('fsdp')
- grad_w_up: float32 [1024, 2816], P('fsdp')
- grad_w_down: float32 [2816, 1024], P('fsdp')
- first_norm: float32 [], replicated
- value_norm: float32 [], replicated
The draws below stay inside these ranges and needn't reach their ends.
Inputs may be any that keep to these rules, and one draw needn't show every extreme that they name: `lengths`: each device holds one whole sequence in its 512 rows; rows from its length on are padding that no query reads.
All inputs are finite; a program needn't handle non-finite values.
Results may differ from the reference program's by a relative error of at most 0.015.
Values may be sent and summed in bfloat16 or wider, within the bound.
A program may use at most 192 MiB of HBM per device.

```python
import math
import jax
import jax.numpy as jnp
from jax import lax

D = 1024
HEAD_DIM = 64
FF = 2816
TOK_DEV = 512
SEQS = 32
TOKENS = 16384


def draw_first_values(key, part):
    key = jax.random.fold_in(key, 11)
    ramp_rows = jnp.arange(TOKENS, dtype=jnp.float32) / max(TOKENS - 1, 1)
    base = jnp.clip(jax.random.normal(key, (TOKENS, D), jnp.float32), -4.0, 4.0)
    ramp = 1.0 + 2.0 * ramp_rows
    return (base * ramp[:, None]).astype(jnp.bfloat16)


def draw_lengths(key, part):
    key = jax.random.fold_in(key, 23)
    key_one, key_two, key_three = jax.random.split(key, 3)
    drawn = jax.random.randint(key_one, (SEQS,), TOK_DEV // 2, TOK_DEV + 1)
    longest = jax.random.randint(key_two, (), 0, SEQS)
    shortest = (longest + 1 + jax.random.randint(key_three, (), 0, SEQS - 1)) % SEQS
    drawn = drawn.at[longest].set(TOK_DEV).at[shortest].set(TOK_DEV // 2)
    return drawn.astype(jnp.int32)


def steps_of(own_key, shape, cuts, low, high):
    loudness, own = 1.0, jax.random.fold_in(own_key, 6)
    for dim, shards_of in cuts:
        steps = jnp.exp(jax.random.uniform(jax.random.fold_in(own, dim), (shards_of,), jnp.float32, low / len(cuts), high / len(cuts)))
        loudness = loudness * jnp.repeat(steps, shape[dim] // shards_of).reshape([-1 if axis == dim else 1 for axis in range(len(shape))])
    return loudness


def normal_values(key, shape, scale, bound, cuts=(), kind=jnp.bfloat16):
    array = scale * jax.random.normal(key, shape, jnp.float32)
    if cuts:
        array = array * steps_of(key, shape, cuts, -0.22, 0.18)
    return jnp.clip(array, -bound, bound).astype(kind)


def setup_inputs(seed: int = 0) -> dict:
    streams_of = jax.random.split(jax.random.key(seed), 12)
    return {
        "tokens": normal_values(streams_of[0], (TOKENS, D), 1.0, 6.0, ((0, 32),)),
        "first_values": draw_first_values(jax.random.fold_in(streams_of[11], 71), 0),
        "lengths": draw_lengths(jax.random.fold_in(streams_of[11], 71), 0),
        "gain_one": jnp.clip(1.0 + 0.18 * jax.random.normal(streams_of[3], (D,), jnp.float32), 0.099609375, 1.8984375).astype(jnp.bfloat16),
        "w_qkv": normal_values(streams_of[4], (D, 3 * D), D ** -0.5, 0.1875, ((0, 4),)),
        "w_out": normal_values(streams_of[5], (D, D), (max(2, D // 256)) ** -0.5, 3.0, ((0, 4),)),
        "gain_two": jnp.clip(1.0 + 0.18 * jax.random.normal(streams_of[6], (D,), jnp.float32), 0.099609375, 1.8984375).astype(jnp.bfloat16),
        "w_gate": normal_values(streams_of[7], (D, FF), D ** -0.5, 0.1875, ((0, 4),)),
        "w_up": normal_values(streams_of[8], (D, FF), D ** -0.5, 0.1875, ((0, 4),)),
        "w_down": normal_values(streams_of[9], (FF, D), (max(2, FF // 16)) ** -0.5, 0.4375, ((0, 4),)),
        "cotangent": normal_values(streams_of[10], (TOKENS, D), 1.0, 6.0, ((0, 32),)),
    }


norm_eps = 1e-06

@jax.custom_vjp
def low(v):
    return lax.optimization_barrier(v.astype(jnp.bfloat16)).astype(jnp.float32)

@jax.custom_vjp
def low_back(v):
    return v

def low_keep(v):
    return (low(v), None)

def low_pass(kept, grad):
    return (grad,)

def back_keep(v):
    return (v, None)

def back_low(kept, grad):
    return (low(grad),)
low.defvjp(low_keep, low_pass)
low_back.defvjp(back_keep, back_low)

def rotary_tables(count, width):
    half_width = width // 2
    frequency = jnp.exp(-(jnp.arange(half_width, dtype=jnp.float32) * 2.0 / width) * math.log(10000.0))
    angles = jnp.arange(count, dtype=jnp.float32)[:, None] * frequency[None, :]
    cosine = jnp.concatenate([jnp.cos(angles), jnp.cos(angles)], axis=1)
    sine_table = jnp.concatenate([jnp.sin(angles), jnp.sin(angles)], axis=1)
    return (cosine[:, None, :], sine_table[:, None, :])

def rotate(values, cosine, sine_table):
    half_width = values.shape[-1] // 2
    turned = jnp.concatenate([-values[..., half_width:], values[..., :half_width]], axis=-1)
    return values * cosine + turned * sine_table

def mat_high(form, left, right):
    return jnp.einsum(form, left, right, precision=lax.Precision.HIGHEST)

def layer_group(params, pieces):
    gain_first, qkv_weight, out_weight, gain_second, gate_weight, up_weight, down_weight = params
    inputs, first_float, group_lengths = pieces
    groups, count, width = inputs.shape
    head_count = width // HEAD_DIM
    normed_one = inputs * lax.rsqrt(lax.optimization_barrier(jnp.mean(inputs * inputs, axis=-1, keepdims=True)) + norm_eps)
    hidden_one = low(normed_one * gain_first)
    projected = low_back(mat_high('gnd,de->gne', hidden_one, qkv_weight))
    shaped = projected.reshape(groups, count, 3, head_count, HEAD_DIM)
    cosine, sine_table = rotary_tables(count, HEAD_DIM)
    queries = low(rotate(shaped[:, :, 0], cosine, sine_table))
    keys_low = low(rotate(shaped[:, :, 1], cosine, sine_table))
    mixed = 0.5 * shaped[:, :, 2] + 0.5 * first_float.reshape(groups, count, head_count, HEAD_DIM)
    values_low = low(mixed)
    scores = low_back(mat_high('gqhd,gkhd->ghqk', queries, keys_low) * HEAD_DIM ** (-0.5))
    position = jnp.arange(count).astype(jnp.int32)
    causal = position[None, :] <= position[:, None]
    allowed = causal[None, None, :, :] & (position[None, None, None, :] < group_lengths[:, None, None, None])
    scores = jnp.where(allowed, scores, -1e+30)
    soft_low = low(jax.nn.softmax(scores, axis=-1))
    heads_out = mat_high('ghqk,gkhd->gqhd', soft_low, values_low)
    attended = low(low_back(heads_out.reshape(groups, count, width)))
    after_attn = inputs + low_back(mat_high('gnd,de->gne', attended, out_weight))
    normed_two = after_attn * lax.rsqrt(lax.optimization_barrier(jnp.mean(after_attn * after_attn, axis=-1, keepdims=True)) + norm_eps)
    hidden_two = low(normed_two * gain_second)
    gate_pre = low_back(mat_high('gnd,df->gnf', hidden_two, gate_weight))
    up_proj = low_back(mat_high('gnd,df->gnf', hidden_two, up_weight))
    product = low(jax.nn.silu(gate_pre) * up_proj)
    layered = after_attn + mat_high('gnf,fd->gnd', product, down_weight)
    return (layered, mixed.reshape(groups, count, width))

def reference(tokens, first_values, lengths, gain_one, w_qkv, w_out, gain_two, w_gate, w_up, w_down, cotangent):
    group_size = math.gcd(SEQS, max(1, 4096 // TOK_DEV))
    group_count = SEQS // group_size
    grouped_lengths = lengths.reshape(group_count, group_size).astype(jnp.int32)
    floats = tuple((item.astype(jnp.float32) for item in (tokens, first_values, gain_one, w_qkv, w_out, gain_two, w_gate, w_up, w_down)))

    def forward(inputs, first_float, gain_first, qkv_weight, out_weight, gain_second, gate_weight, up_weight, down_weight):
        params = (gain_first, qkv_weight, out_weight, gain_second, gate_weight, up_weight, down_weight)

        def one_group(pieces):
            return jax.checkpoint(layer_group)(params, pieces)
        layered, mixed = lax.map(one_group, (inputs.reshape(group_count, group_size, TOK_DEV, D), first_float.reshape(group_count, group_size, TOK_DEV, D), grouped_lengths))
        return (layered.reshape(TOKENS, D), mixed.reshape(TOKENS, D))
    result, pull_back, mixed = jax.vjp(forward, *floats, has_aux=True)
    grads = pull_back(cotangent.astype(jnp.float32))
    first_norm = jnp.mean(floats[1] * floats[1])
    value_norm = jnp.mean(mixed * mixed)
    return (result.astype(jnp.bfloat16), grads[0], grads[1], grads[2], grads[3], grads[4], grads[5], grads[6], grads[7], grads[8], first_norm, value_norm)
```

```python
import functools
import math

import jax
import jax.numpy as jnp
import numpy as np
from jax import lax
from jax.experimental import pallas as pl
from jax.experimental.pallas import tpu as pltpu
from jax.sharding import PartitionSpec as P

HEAD_DIM = 64
PAIR = 2 * HEAD_DIM
TILE = 256
GAIN_ROWS = 16
norm_eps = 1e-06
F32 = jnp.float32
BF16 = jnp.bfloat16
AXES = ("dp", "fsdp")
ANY = pl.BlockSpec(memory_space=pl.ANY)


def dot_nn(a, b):
    return lax.dot_general(a, b, (((1,), (0,)), ((), ())), preferred_element_type=F32)


def dot_nt(a, b):
    return lax.dot_general(a, b, (((1,), (1,)), ((), ())), preferred_element_type=F32)


def rotary_tables(count):
    half = HEAD_DIM // 2
    frequency = np.exp(
        -(np.arange(half, dtype=np.float32) * np.float32(2.0) / np.float32(HEAD_DIM))
        * np.float32(math.log(10000.0))
    ).astype(np.float32)
    angles = np.arange(count, dtype=np.float32)[:, None] * frequency[None, :]
    cosine = np.cos(angles.astype(np.float64)).astype(np.float32)
    sine = np.sin(angles.astype(np.float64)).astype(np.float32)
    cosine = np.concatenate([cosine] * 4, axis=1)
    sine = np.concatenate([-sine, sine, -sine, sine], axis=1)
    return cosine, sine


def swap_halves(x):
    half = HEAD_DIM // 2
    lane = lax.broadcasted_iota(jnp.int32, x.shape, 1)
    up = pltpu.roll(x, PAIR - half, 1)
    down = pltpu.roll(x, half, 1)
    return jnp.where((lane % HEAD_DIM) < half, up, down)


def bit_reverse(value, bits):
    out = 0
    for i in range(bits):
        out = out + ((value >> i) & 1) * (1 << (bits - 1 - i))
    return out


class Layout:
    def __init__(self, dp, fs):
        self.dp, self.fs = dp, fs
        self.bits = fs.bit_length() - 1
        self.line = dp // 2

    def perm(self, move):
        pairs = []
        for d in range(self.dp):
            for f in range(self.fs):
                target = move(d, f)
                if target is not None:
                    pairs.append((d * self.fs + f, target[0] * self.fs + target[1]))
        return pairs

    def send(self, x, move):
        return lax.ppermute(x, AXES, self.perm(move))

    def core(self, x):
        return self.send(x, lambda d, f: (d ^ 1, f))

    def step(self, x, i):
        bits = self.bits
        return self.send(x, lambda d, f: (d, f ^ (1 << (i if d % 2 == 0 else bits - 1 - i))))

    def index(self, length):
        d, f = lax.axis_index("dp"), lax.axis_index("fsdp")
        c = d % 2
        masks = jnp.arange(self.fs, dtype=jnp.int32)
        turned = bit_reverse(masks, self.bits)
        straight = c == 0
        mine = f ^ jnp.where(straight, masks, turned)
        other = f ^ jnp.where(straight, turned, masks)
        order = f ^ jnp.where(straight, turned, masks)
        head = jnp.stack([c, 1 - c, length, f]).astype(jnp.int32)
        return jnp.concatenate([head, mine, other, order]).astype(jnp.int32)

    def gather(self, half):
        pieces = [half]
        for i in range(self.bits):
            pieces = pieces + [self.step(piece, i) for piece in pieces]
        return pieces, [self.core(piece) for piece in pieces[1:]]

    def line_sum(self, total):
        size = self.line
        if size == 1:
            return total
        half = size // 2
        r = lax.axis_index("dp") // 2

        def hop(x, table):
            return self.send(
                x, lambda d, f: (table[d // 2] * 2 + d % 2, f) if d // 2 in table else None
            )

        for i in range(half - 1):
            got = hop(total, {i: i + 1, size - 1 - i: size - 2 - i})
            total = add_low(total, got)
        got = hop(total, {half - 1: half, half: half - 1})
        total = add_low(total, got)
        for i in range(half - 1):
            low, high = half - 1 - i, half + i
            got = hop(total, {low: low - 1, high: high + 1})
            total = jnp.where((r == low - 1) | (r == high + 1), got, total)
        return total

    def reduce(self, keep, send):
        for i in range(self.bits):
            got = self.step(send, i)
            total = add_low(keep, got)
            blocks = total.shape[0]
            if blocks > 1:
                keep, send = total[: blocks // 2], total[blocks // 2 :]
        return self.line_sum(total[0])

    def small_sum(self, x):
        x = x + self.core(x)
        for i in range(self.bits):
            x = x + self.step(x, i)
        reach = 1
        while reach < self.line:
            x = x + self.send(x, lambda d, f: ((((d // 2) ^ reach) * 2 + d % 2), f))
            reach *= 2
        return x


def add_low(a, b):
    return (a.astype(F32) + b.astype(F32)).astype(BF16)


IDX_HEAD = 4


def piece_copies(idx, own, mine, other, target, sems, first, column, width, rows, count):
    copies = [
        pltpu.make_async_copy(own, target.at[pl.ds(idx[3] * rows, rows), :], sems.at[first])
    ]
    for m in range(1, count):
        for which, (pieces, base) in enumerate(((mine, 0), (other, count))):
            shard = idx[IDX_HEAD + base + m]
            side = pl.multiple_of(idx[which] * width, 128)
            copies.append(
                pltpu.make_async_copy(
                    pieces[m - 1].at[pl.ds(0, rows), pl.ds(column, width)],
                    target.at[pl.ds(shard * rows, rows), pl.ds(side, width)],
                    sems.at[first + 2 * m - 1 + which],
                )
            )
    return copies


def start(copies):
    for copy in copies:
        copy.start()


def wait(copies):
    for copy in copies:
        copy.wait()


def call(body, grid, in_specs, out_specs, out_shape, scratch, name, flops, nbytes, limit=56):
    return pl.pallas_call(
        body,
        grid_spec=pltpu.PrefetchScalarGridSpec(
            num_scalar_prefetch=1,
            grid=grid,
            in_specs=in_specs,
            out_specs=out_specs,
            scratch_shapes=scratch,
        ),
        out_shape=out_shape,
        compiler_params=pltpu.CompilerParams(vmem_limit_bytes=limit * 2**20),
        cost_estimate=pl.CostEstimate(
            flops=int(flops), bytes_accessed=int(nbytes), transcendentals=0
        ),
        name=name,
    )


def whole(shape):
    zeros = (0,) * len(shape)
    return pl.BlockSpec(shape, lambda *_: zeros)


def struct(shape, dtype):
    return jax.ShapeDtypeStruct(shape, dtype)


def qkv_body(count, idx, tokens, first, cosine, sine, own, *rest):
    pieces, rest = rest[: 2 * count - 1], rest[2 * count - 1 :]
    queries, keys, values, hidden_t, gains, sums, weight, hidden, gain, sems = rest
    half_own, mine, other = pieces[0], pieces[1:count], pieces[count:]
    rows = own.shape[0]
    width = tokens.shape[1]
    side = own.shape[1] // 2
    copies = piece_copies(idx, own, mine, other, weight, sems, 0, 0, side, rows, count)
    start(copies)
    gain_copies = []
    for m in range(count):
        piece = half_own if m == 0 else mine[m - 1]
        shard = idx[IDX_HEAD + m]
        for which in range(2):
            gain_copies.append(
                pltpu.make_async_copy(
                    piece.at[pl.ds(rows, GAIN_ROWS), pl.ds(which * rows, rows)],
                    gain.at[which, :, pl.ds(pl.multiple_of(shard * rows, 128), rows)],
                    sems.at[2 * count - 1 + 2 * m + which],
                )
            )
    start(gain_copies)
    inputs = tokens[...].astype(F32)
    inverse = lax.rsqrt(jnp.mean(inputs * inputs, axis=-1, keepdims=True) + norm_eps)
    wait(gain_copies)
    gain_one = gain[0, 0:1, :].astype(F32)
    gains[0:1, :] = gain_one
    gains[1:2, :] = gain[1, 0:1, :].astype(F32)
    gains[2:8, :] = jnp.zeros((6, width), F32)
    normed = inputs * inverse * gain_one
    hidden[...] = normed.astype(BF16)
    hidden_t[...] = normed.astype(BF16).T
    wait(copies)
    cos, sin = cosine[...], sine[...]

    def rotated(base, out, scale):
        @pl.loop(0, width // TILE)
        def _(t):
            at = pl.multiple_of(t * TILE, TILE)
            raw = dot_nn(hidden[...], weight[:, pl.ds(base + at, TILE)])
            for part in range(TILE // PAIR):
                x = raw[:, part * PAIR : (part + 1) * PAIR]
                turned = x * cos + swap_halves(x) * sin
                out[:, pl.ds(at + part * PAIR, PAIR)] = turned.astype(BF16) * scale

    rotated(0, queries, jnp.asarray(HEAD_DIM**-0.5, BF16))
    rotated(width, keys, jnp.asarray(1.0, BF16))

    def mix(t, carry):
        at = pl.multiple_of(t * TILE, TILE)
        raw = dot_nn(hidden[...], weight[:, pl.ds(2 * width + at, TILE)])
        kept = first[:, pl.ds(at, TILE)].astype(F32)
        mixed = 0.5 * raw + 0.5 * kept
        values[:, pl.ds(at, TILE)] = mixed.astype(BF16)
        return (
            carry[0] + jnp.sum(kept * kept, axis=0, keepdims=True),
            carry[1] + jnp.sum(mixed * mixed, axis=0, keepdims=True),
        )

    zero = jnp.zeros((1, TILE), F32)
    one, two = lax.fori_loop(0, width // TILE, mix, (zero, zero))
    sums[...] = jnp.zeros(sums.shape, F32)
    sums[0:1, :] = one
    sums[1:2, :] = two


def qkv_kernel(lay, idx, tokens, first, tables, own, half_own, mine, other):
    count = lay.fs
    rows, width = tokens.shape
    n = own.shape[1]
    operands = (tokens, first, tables[0], tables[1], own, half_own, *mine, *other)
    return call(
        functools.partial(qkv_body, count),
        (1,),
        [whole(tokens.shape), whole(first.shape), whole(tables[0].shape), whole(tables[1].shape)]
        + [ANY] * (2 * count),
        [
            whole((rows, width)),
            whole((rows, width)),
            whole((rows, width)),
            whole((width, rows)),
            whole((8, width)),
            whole((8, TILE)),
        ],
        [
            struct((rows, width), BF16),
            struct((rows, width), BF16),
            struct((rows, width), BF16),
            struct((width, rows), BF16),
            struct((8, width), F32),
            struct((8, TILE), F32),
        ],
        [
            pltpu.VMEM((width, n), BF16),
            pltpu.VMEM((rows, width), BF16),
            pltpu.VMEM((2, GAIN_ROWS, width), BF16),
            pltpu.SemaphoreType.DMA((4 * count - 1,)),
        ],
        "qkv",
        2 * rows * width * n,
        2 * width * n + 12 * rows * width,
    )(idx, *operands)


def attend_body(idx, queries, keys, values, attended, attended_t, logs, turned):
    rows = queries.shape[0]
    block = min(TILE, rows)
    length = idx[2]
    lane = lax.broadcasted_iota(jnp.int32, (rows, PAIR), 1)
    q, k = queries[...], keys[...]
    v_t = values[...].T
    logs[...] = jnp.zeros(logs.shape, F32)
    for head in range(2):
        inside = (lane // HEAD_DIM) == head
        k_head = jnp.where(inside, k, jnp.zeros_like(k))
        v_head = v_t[head * HEAD_DIM : (head + 1) * HEAD_DIM]
        for b in range(rows // block):
            upto = (b + 1) * block
            scores = dot_nt(k_head[:upto], q[b * block : upto])
            key = lax.broadcasted_iota(jnp.int32, scores.shape, 0)
            query = lax.broadcasted_iota(jnp.int32, (1, block), 1) + b * block
            scores = jnp.where(key <= jnp.minimum(query, length - 1), scores, -1e30)
            peak = jnp.max(scores, axis=0, keepdims=True)
            expo = jnp.exp(scores - peak)
            total = jnp.sum(expo, axis=0, keepdims=True)
            soft = (expo * (1.0 / total)).astype(BF16)
            logs[0, head : head + 1, b * block : upto] = peak + jnp.log(total)
            turned[head * HEAD_DIM : (head + 1) * HEAD_DIM, b * block : upto] = dot_nn(
                v_head[:, :upto], soft
            )
    out = turned[...]
    attended_t[...] = out.astype(BF16)
    attended[...] = out.T.astype(BF16)


def attend_kernel(idx, queries, keys, values):
    rows, width = queries.shape
    pairs = width // PAIR
    column = pl.BlockSpec((rows, PAIR), lambda p, _: (0, p))
    return call(
        attend_body,
        (pairs,),
        [column] * 3,
        [
            column,
            pl.BlockSpec((PAIR, rows), lambda p, _: (p, 0)),
            pl.BlockSpec((1, 8, rows), lambda p, _: (p, 0, 0)),
        ],
        [
            struct((rows, width), BF16),
            struct((width, rows), BF16),
            struct((pairs, 8, rows), F32),
        ],
        [pltpu.VMEM((PAIR, rows), F32)],
        "attend",
        8 * rows * rows * width,
        10 * rows * width,
        32,
    )(idx, queries, keys, values)


def attend_back_body(
    idx, queries, keys, values, grads, logs, cosine, sine, grad_q, grad_k, grad_v, grad_first, turned
):
    rows = queries.shape[0]
    block = min(TILE, rows)
    length = idx[2]
    lane = lax.broadcasted_iota(jnp.int32, (rows, PAIR), 1)
    q, k, v, g = queries[...], keys[...], values[...], grads[...]
    k_t = k.T
    sums_k, sums_v = [], []
    for head in range(2):
        inside = (lane // HEAD_DIM) == head
        k_head = jnp.where(inside, k, jnp.zeros_like(k))
        v_head = jnp.where(inside, v, jnp.zeros_like(v))
        k_turned = k_t[head * HEAD_DIM : (head + 1) * HEAD_DIM]
        parts_k, parts_v = [], []
        for b in range(rows // block):
            upto = (b + 1) * block
            q_block, g_block = q[b * block : upto], g[b * block : upto]
            scores = dot_nt(k_head[:upto], q_block)
            key = lax.broadcasted_iota(jnp.int32, scores.shape, 0)
            query = lax.broadcasted_iota(jnp.int32, (1, block), 1) + b * block
            log_total = logs[0, head : head + 1, b * block : upto]
            soft = jnp.where(
                key <= jnp.minimum(query, length - 1), jnp.exp(scores - log_total), 0.0
            )
            grad_soft = dot_nt(v_head[:upto], g_block)
            inner = jnp.sum(soft * grad_soft, axis=0, keepdims=True)
            grad_scores = (soft * (grad_soft - inner)).astype(BF16)
            turned[head * HEAD_DIM : (head + 1) * HEAD_DIM, b * block : upto] = dot_nn(
                k_turned[:, :upto], grad_scores
            )
            parts_k.append(dot_nn(grad_scores, q_block))
            parts_v.append(dot_nn(soft.astype(BF16), g_block))
        for parts, sums in ((parts_k, sums_k), (parts_v, sums_v)):
            rows_of = []
            for r in range(rows // block):
                piece = parts[r][r * block : (r + 1) * block]
                for later in parts[r + 1 :]:
                    piece = piece + later[r * block : (r + 1) * block]
                rows_of.append(piece)
            sums.append(jnp.concatenate(rows_of, axis=0))
    first_head = lane < HEAD_DIM
    cos, sin = cosine[...], sine[...]

    def back(x):
        return (x * cos - swap_halves(x) * sin).astype(BF16)

    grad_q[...] = back(turned[...].T * HEAD_DIM**-0.5)
    grad_k[...] = back(jnp.where(first_head, sums_k[0], sums_k[1]))
    half_v = 0.5 * jnp.where(first_head, sums_v[0], sums_v[1])
    grad_first[...] = half_v
    grad_v[...] = half_v.astype(BF16)


def attend_back_kernel(idx, queries, keys, values, grads, logs, tables):
    rows, width = queries.shape
    pairs = width // PAIR
    column = pl.BlockSpec((rows, PAIR), lambda p, _: (0, p))
    return call(
        attend_back_body,
        (pairs,),
        [column] * 4
        + [
            pl.BlockSpec((1, 8, rows), lambda p, _: (p, 0, 0)),
            whole(tables[0].shape),
            whole(tables[1].shape),
        ],
        [column] * 4,
        [struct((rows, width), BF16)] * 3 + [struct((rows, width), F32)],
        [pltpu.VMEM((PAIR, rows), F32)],
        "attend_back",
        20 * rows * rows * width,
        18 * rows * width,
        40,
    )(idx, queries, keys, values, grads, logs, *tables)


def gate_body(count, idx, attended, tokens, gains, own_out, own_gate, own_up, *rest):
    pieces, rest = rest[: 2 * count - 2], rest[2 * count - 2 :]
    (after, hidden_two, hidden_t, gate, up, product, product_t) = rest[:7]
    w_out, w_gate, w_up, sems = rest[7:]
    mine, other = pieces[: count - 1], pieces[count - 1 :]
    rows = own_out.shape[0]
    per = 2 * count - 1

    @pl.when(pl.program_id(0) == 0)
    def _():
        side_out, side = own_out.shape[1] // 2, own_gate.shape[1] // 2
        load = functools.partial(piece_copies, idx, rows=rows, count=count, sems=sems)
        first = load(own_out, mine, other, w_out, first=0, column=0, width=side_out)
        second = load(own_gate, mine, other, w_gate, first=per, column=side_out, width=side)
        third = load(own_up, mine, other, w_up, first=2 * per, column=side_out + side, width=side)
        start(first + second + third)
        wait(first)

        @pl.loop(0, w_out.shape[1] // TILE)
        def _(t):
            at = pl.multiple_of(t * TILE, TILE)
            after[:, pl.ds(at, TILE)] = tokens[:, pl.ds(at, TILE)].astype(F32) + dot_nn(
                attended[...], w_out[:, pl.ds(at, TILE)]
            )

        x = after[...]
        inverse = lax.rsqrt(jnp.mean(x * x, axis=-1, keepdims=True) + norm_eps)
        low = (x * inverse * gains[1:2, :]).astype(BF16)
        hidden_two[...] = low
        hidden_t[...] = low.T
        wait(second + third)

    at = pl.multiple_of(pl.program_id(0) * TILE, TILE)
    gate_pre = dot_nn(hidden_two[...], w_gate[:, pl.ds(at, TILE)])
    up_proj = dot_nn(hidden_two[...], w_up[:, pl.ds(at, TILE)])
    low = (gate_pre * jax.nn.sigmoid(gate_pre) * up_proj).astype(BF16)
    gate[...] = gate_pre.astype(gate.dtype)
    up[...] = up_proj.astype(up.dtype)
    product[...] = low
    product_t[...] = low.T


def gate_kernel(lay, idx, attended, tokens, gains, own_out, own_gate, own_up, mine, other):
    count = lay.fs
    rows, width = tokens.shape
    hidden = own_gate.shape[1]
    tile = pl.BlockSpec((rows, TILE), lambda t, _: (0, t))
    return call(
        functools.partial(gate_body, count),
        (hidden // TILE,),
        [whole(attended.shape), whole(tokens.shape), whole(gains.shape)] + [ANY] * (2 * count + 1),
        [
            whole((rows, width)),
            whole((rows, width)),
            whole((width, rows)),
            tile,
            tile,
            tile,
            pl.BlockSpec((TILE, rows), lambda t, _: (t, 0)),
        ],
        [
            struct((rows, width), F32),
            struct((rows, width), BF16),
            struct((width, rows), BF16),
            struct((rows, hidden), BF16),
            struct((rows, hidden), BF16),
            struct((rows, hidden), BF16),
            struct((hidden, rows), BF16),
        ],
        [
            pltpu.VMEM((width, width), BF16),
            pltpu.VMEM((width, hidden), BF16),
            pltpu.VMEM((width, hidden), BF16),
            pltpu.SemaphoreType.DMA((3 * (2 * count - 1),)),
        ],
        "gate",
        2 * rows * width * (width + 2 * hidden),
        2 * width * (width + 2 * hidden) + 8 * rows * hidden,
    )(idx, attended, tokens, gains, own_out, own_gate, own_up, *mine, *other)


def down_body(count, idx, cotangent, after, gate, up, product, own, *rest):
    pieces, rest = rest[: 2 * count - 2], rest[2 * count - 2 :]
    grad_gate, grad_up, output, weight, total, sems = rest
    mine, other = pieces[: count - 1], pieces[count - 1 :]
    t = pl.program_id(0)

    @pl.when(t == 0)
    def _():
        copies = piece_copies(
            idx, own, mine, other, weight, sems, 0, 0, own.shape[1] // 2, own.shape[0], count
        )
        start(copies)
        total[...] = after[...]
        wait(copies)

    rows_of = weight[pl.ds(pl.multiple_of(t * TILE, TILE), TILE), :]
    grad_product = dot_nt(cotangent[...], rows_of)
    gate_pre = gate[...].astype(F32)
    up_proj = up[...].astype(F32)
    sigma = jax.nn.sigmoid(gate_pre)
    grad_gate[...] = (
        grad_product * up_proj * sigma * (1.0 + gate_pre * (1.0 - sigma))
    ).astype(BF16)
    grad_up[...] = (grad_product * (gate_pre * sigma)).astype(BF16)
    total[...] += dot_nn(product[...], rows_of)

    @pl.when(t == pl.num_programs(0) - 1)
    def _():
        output[...] = total[...].astype(BF16)


def down_kernel(lay, idx, cotangent, after, gate, up, product, own, mine, other):
    count = lay.fs
    rows, width = cotangent.shape
    hidden = gate.shape[1]
    tile = pl.BlockSpec((rows, TILE), lambda t, _: (0, t))
    return call(
        functools.partial(down_body, count),
        (hidden // TILE,),
        [whole(cotangent.shape), whole(after.shape), tile, tile, tile] + [ANY] * (2 * count - 1),
        [tile, tile, whole((rows, width))],
        [
            struct((rows, hidden), BF16),
            struct((rows, hidden), BF16),
            struct((rows, width), BF16),
        ],
        [
            pltpu.VMEM((hidden, width), BF16),
            pltpu.VMEM((rows, width), F32),
            pltpu.SemaphoreType.DMA((2 * count - 1,)),
        ],
        "down",
        4 * rows * width * hidden,
        2 * width * hidden + 10 * rows * hidden,
    )(idx, cotangent, after, gate, up, product, own, *mine, *other)


def rms_back(grad, normed, inverse):
    return inverse * (grad - normed * jnp.mean(grad * normed, axis=-1, keepdims=True))


def mlp_back_body(count, idx, grad_gate, grad_up, after, cotangent, gains, own_out, own_gate, own_up, *rest):
    pieces, rest = rest[: 2 * count - 2], rest[2 * count - 2 :]
    grad_after, grad_low, grad_attended, grad_gain = rest[:4]
    w_out, w_gate, w_up, total, sems = rest[4:]
    mine, other = pieces[: count - 1], pieces[count - 1 :]
    rows = own_out.shape[0]
    per = 2 * count - 1
    side_out, side = own_out.shape[1] // 2, own_gate.shape[1] // 2
    load = functools.partial(piece_copies, idx, rows=rows, count=count, sems=sems)
    first = load(own_out, mine, other, w_out, first=0, column=0, width=side_out)
    second = load(own_gate, mine, other, w_gate, first=per, column=side_out, width=side)
    third = load(own_up, mine, other, w_up, first=2 * per, column=side_out + side, width=side)
    start(second + third + first)
    wait(second + third)
    width = w_gate.shape[0]

    @pl.loop(0, width // TILE)
    def _(t):
        at = pl.multiple_of(t * TILE, TILE)
        total[:, pl.ds(at, TILE)] = dot_nt(grad_gate[...], w_gate[pl.ds(at, TILE), :]) + dot_nt(
            grad_up[...], w_up[pl.ds(at, TILE), :]
        )

    x = after[...]
    inverse = lax.rsqrt(jnp.mean(x * x, axis=-1, keepdims=True) + norm_eps)
    normed = x * inverse
    grad_hidden = total[...]
    grad_gain[...] = jnp.zeros(grad_gain.shape, F32)
    grad_gain[0:1, :] = jnp.sum(grad_hidden * normed, axis=0, keepdims=True)
    result = cotangent[...].astype(F32) + rms_back(grad_hidden * gains[1:2, :], normed, inverse)
    grad_after[...] = result
    grad_low[...] = result.astype(BF16)
    wait(first)

    @pl.loop(0, width // TILE)
    def _(t):
        at = pl.multiple_of(t * TILE, TILE)
        grad_attended[:, pl.ds(at, TILE)] = dot_nt(
            grad_low[...], w_out[pl.ds(at, TILE), :]
        ).astype(BF16)


def mlp_back_kernel(lay, idx, grad_gate, grad_up, after, cotangent, gains, own_out, own_gate, own_up, mine, other):
    count = lay.fs
    rows, width = cotangent.shape
    hidden = grad_gate.shape[1]
    return call(
        functools.partial(mlp_back_body, count),
        (1,),
        [whole(grad_gate.shape), whole(grad_up.shape), whole(after.shape), whole(cotangent.shape), whole(gains.shape)]
        + [ANY] * (2 * count + 1),
        [whole((rows, width)), whole((rows, width)), whole((rows, width)), whole((8, width))],
        [
            struct((rows, width), F32),
            struct((rows, width), BF16),
            struct((rows, width), BF16),
            struct((8, width), F32),
        ],
        [
            pltpu.VMEM((width, width), BF16),
            pltpu.VMEM((width, hidden), BF16),
            pltpu.VMEM((width, hidden), BF16),
            pltpu.VMEM((rows, width), F32),
            pltpu.SemaphoreType.DMA((3 * (2 * count - 1),)),
        ],
        "mlp_back",
        2 * rows * width * (width + 2 * hidden),
        2 * width * (width + 2 * hidden) + 4 * rows * hidden + 12 * rows * width,
    )(idx, grad_gate, grad_up, after, cotangent, gains, own_out, own_gate, own_up, *mine, *other)


def qkv_back_body(count, idx, grad_q, grad_k, grad_v, tokens, grad_after, gains, own, *rest):
    pieces, rest = rest[: 2 * count - 2], rest[2 * count - 2 :]
    grad_tokens, grad_gain, weight, total, sems = rest
    mine, other = pieces[: count - 1], pieces[count - 1 :]
    copies = piece_copies(
        idx, own, mine, other, weight, sems, 0, 0, own.shape[1] // 2, own.shape[0], count
    )
    start(copies)
    x = tokens[...].astype(F32)
    inverse = lax.rsqrt(jnp.mean(x * x, axis=-1, keepdims=True) + norm_eps)
    width = weight.shape[0]
    wait(copies)

    @pl.loop(0, width // TILE)
    def _(t):
        at = pl.multiple_of(t * TILE, TILE)
        block = pl.ds(at, TILE)
        total[:, block] = (
            dot_nt(grad_q[...], weight[block, 0:width])
            + dot_nt(grad_k[...], weight[block, width : 2 * width])
            + dot_nt(grad_v[...], weight[block, 2 * width : 3 * width])
        )

    normed = x * inverse
    grad_hidden = total[...]
    grad_gain[...] = jnp.zeros(grad_gain.shape, F32)
    grad_gain[0:1, :] = jnp.sum(grad_hidden * normed, axis=0, keepdims=True)
    grad_tokens[...] = grad_after[...] + rms_back(grad_hidden * gains[0:1, :], normed, inverse)


def qkv_back_kernel(lay, idx, grad_q, grad_k, grad_v, tokens, grad_after, gains, own, mine, other):
    count = lay.fs
    rows, width = tokens.shape
    n = own.shape[1]
    operands = (grad_q, grad_k, grad_v, tokens, grad_after, gains)
    return call(
        functools.partial(qkv_back_body, count),
        (1,),
        [whole(item.shape) for item in operands] + [ANY] * (2 * count - 1),
        [whole((rows, width)), whole((8, width))],
        [struct((rows, width), F32), struct((8, width), F32)],
        [
            pltpu.VMEM((width, n), BF16),
            pltpu.VMEM((rows, width), F32),
            pltpu.SemaphoreType.DMA((2 * count - 1,)),
        ],
        "qkv_back",
        2 * rows * width * n,
        2 * width * n + 16 * rows * width,
    )(idx, *operands, own, *mine, *other)


def grad_sibling_body(parts, idx, turned, *rest):
    lefts, out = rest[:parts], rest[parts]
    side = lefts[0].shape[1]
    for i, left in enumerate(lefts):
        out[0, :, i * side : (i + 1) * side] = dot_nn(turned[...], left[...]).astype(BF16)


def grad_own_body(parts, blocks, idx, turned, *rest):
    lefts, got, keep, send = rest[:parts], rest[parts], rest[parts + 1], rest[parts + 2]
    side = lefts[0].shape[1]
    place = pl.program_id(0)

    def block(out):
        for i, left in enumerate(lefts):
            columns = slice(i * side, (i + 1) * side)
            summed = dot_nn(turned[...], left[...]) + got[0, :, columns].astype(F32)
            out[0, :, columns] = summed.astype(BF16)

    @pl.when(place < blocks // 2)
    def _():
        block(keep)

    @pl.when(place >= blocks // 2)
    def _():
        block(send)


def weight_grad(lay, idx, turned, lefts, name):
    blocks = lay.fs
    total, rows = turned.shape
    block = total // blocks
    half = [left.shape[1] // 2 for left in lefts]
    wide = sum(half)
    cost = (2 * rows * total * wide, 2 * rows * (total + wide) + 2 * total * wide)
    base = IDX_HEAD + 2 * blocks

    def shard(p, idx):
        return (idx[base + p], 0)

    sibling = call(
        functools.partial(grad_sibling_body, len(lefts)),
        (blocks,),
        [pl.BlockSpec((block, rows), lambda p, idx: (p, 0))]
        + [pl.BlockSpec((rows, side), lambda p, idx: (0, idx[1])) for side in half],
        [pl.BlockSpec((1, block, wide), lambda p, idx: (p, 0, 0))],
        [struct((blocks, block, wide), BF16)],
        [],
        name + "_sibling",
        *cost,
    )(idx, turned, *lefts)[0]
    got = lay.core(sibling)
    return call(
        functools.partial(grad_own_body, len(lefts), blocks),
        (blocks,),
        [pl.BlockSpec((block, rows), shard)]
        + [pl.BlockSpec((rows, side), lambda p, idx: (0, idx[0])) for side in half]
        + [pl.BlockSpec((1, block, wide), lambda p, idx: (idx[base + p], 0, 0))],
        [
            pl.BlockSpec((1, block, wide), lambda p, idx: (jnp.minimum(p, blocks // 2 - 1), 0, 0)),
            pl.BlockSpec((1, block, wide), lambda p, idx: (jnp.maximum(p - blocks // 2, 0), 0, 0)),
        ],
        [struct((blocks // 2, block, wide), BF16)] * 2,
        [],
        name + "_own",
        *cost,
    )(idx, turned, *lefts, got)


def finish_body(parts, idx, mine, other, *outs):
    low = idx[0] == 0
    at = 0
    for out in outs:
        side = out.shape[1] // 2
        a = mine[:, at : at + side].astype(F32)
        b = other[:, at : at + side].astype(F32)
        out[:, 0:side] = jnp.where(low, a, b)
        out[:, side:] = jnp.where(low, b, a)
        at += side


def finish(lay, idx, mine, widths, name):
    other = lay.core(mine)
    rows, wide = mine.shape
    block = rows // 4 if rows % 64 == 0 else rows
    return call(
        functools.partial(finish_body, len(widths)),
        (rows // block,),
        [pl.BlockSpec((block, wide), lambda p, _: (p, 0))] * 2,
        [pl.BlockSpec((block, 2 * side), lambda p, _: (p, 0)) for side in widths],
        [struct((rows, 2 * side), F32) for side in widths],
        [],
        name,
        0,
        12 * rows * wide,
    )(idx, mine, other)


def body(
    lay,
    tokens,
    first_values,
    lengths,
    gain_one,
    w_qkv,
    w_out,
    gain_two,
    w_gate,
    w_up,
    w_down,
    cotangent,
):
    rows, width = tokens.shape
    hidden = w_gate.shape[1]
    shard_rows = w_qkv.shape[0]
    idx = lay.index(lengths[0])
    tables = tuple(jnp.asarray(table) for table in rotary_tables(rows))
    c = lax.axis_index("dp") % 2

    def half_of(weight):
        side = weight.shape[1] // 2
        return lax.dynamic_slice_in_dim(weight, c * side, side, axis=1)

    gain_block = jnp.concatenate([gain_one, gain_two])
    half_qkv = half_of(w_qkv)
    gain_block = jnp.pad(
        gain_block[None], ((0, GAIN_ROWS - 1), (0, half_qkv.shape[1] - 2 * shard_rows))
    )
    half_a = jnp.concatenate([half_qkv, gain_block], axis=0)
    half_b = jnp.concatenate([half_of(w_out), half_of(w_gate), half_of(w_up)], axis=1)
    half_c = half_of(w_down)
    mine_a, other_a = lay.gather(half_a)
    mine_b, other_b = lay.gather(half_b)
    mine_c, other_c = lay.gather(half_c)

    queries, keys, values, hidden_one_t, gains, sums = qkv_kernel(
        lay, idx, tokens, first_values, tables, w_qkv, half_a, mine_a[1:], other_a
    )
    attended, attended_t, logs = attend_kernel(idx, queries, keys, values)
    after, hidden_two, hidden_two_t, gate, up, product, product_t = gate_kernel(
        lay, idx, attended, tokens, gains, w_out, w_gate, w_up, mine_b[1:], other_b
    )
    keep, send = weight_grad(lay, idx, product_t, [cotangent], "grad_down")
    total_down = lay.reduce(keep, send)
    grad_gate, grad_up, output = down_kernel(
        lay, idx, cotangent, after, gate, up, product, w_down, mine_c[1:], other_c
    )
    keep, send = weight_grad(lay, idx, hidden_two_t, [grad_gate, grad_up], "grad_gate_up")
    total_gate_up = lay.reduce(keep, send)
    grad_after, grad_after_low, grad_attended, grad_gain_two = mlp_back_kernel(
        lay, idx, grad_gate, grad_up, after, cotangent, gains, w_out, w_gate, w_up, mine_b[1:], other_b
    )
    keep, send = weight_grad(lay, idx, attended_t, [grad_after_low], "grad_out")
    total_out = lay.reduce(keep, send)
    grad_q, grad_k, grad_v, grad_first = attend_back_kernel(
        idx, queries, keys, values, grad_attended, logs, tables
    )
    keep, send = weight_grad(lay, idx, hidden_one_t, [grad_q, grad_k, grad_v], "grad_qkv")
    total_qkv = lay.reduce(keep, send)
    grad_tokens, grad_gain_one = qkv_back_kernel(
        lay, idx, grad_q, grad_k, grad_v, tokens, grad_after, gains, w_qkv, mine_a[1:], other_a
    )

    small = jnp.concatenate(
        [
            grad_gain_one[0:1],
            grad_gain_two[0:1],
            jnp.pad(jnp.sum(sums, axis=1)[None], ((0, 5), (0, width - 8))),
        ]
    )
    small = lay.small_sum(small)
    at = lax.axis_index("fsdp") * shard_rows
    entry_count = rows * width * lay.dp * lay.fs
    shard_gain_one = lax.dynamic_slice(small[0], (at,), (shard_rows,))
    shard_gain_two = lax.dynamic_slice(small[1], (at,), (shard_rows,))
    first_norm = small[2, 0] / entry_count
    value_norm = small[2, 1] / entry_count

    (shard_down,) = finish(lay, idx, total_down, [width // 2], "finish_down")
    shard_gate, shard_up = finish(lay, idx, total_gate_up, [hidden // 2] * 2, "finish_gate_up")
    (shard_out,) = finish(lay, idx, total_out, [width // 2], "finish_out")
    third = width // 2
    other_qkv = lay.core(total_qkv)
    low = c == 0
    blocks = []
    for i in range(3):
        a = total_qkv[:, i * third : (i + 1) * third].astype(F32)
        b = other_qkv[:, i * third : (i + 1) * third].astype(F32)
        blocks += [jnp.where(low, a, b), jnp.where(low, b, a)]
    shard_qkv = jnp.concatenate(blocks, axis=1)
    return (
        output,
        grad_tokens,
        grad_first,
        shard_gain_one,
        shard_qkv,
        shard_out,
        shard_gain_two,
        shard_gate,
        shard_up,
        shard_down,
        first_norm,
        value_norm,
    )


def solution(mesh):
    both = P(AXES, None)
    rows = P("fsdp", None)
    in_specs = (both, both, P(AXES), P("fsdp"), rows, rows, P("fsdp"), rows, rows, rows, both)
    out_specs = (both, both, both, P("fsdp"), rows, rows, P("fsdp"), rows, rows, rows, P(), P())
    lay = Layout(mesh.shape["dp"], mesh.shape["fsdp"])
    return jax.shard_map(
        functools.partial(body, lay),
        mesh=mesh,
        in_specs=in_specs,
        out_specs=out_specs,
        check_vma=False,
    )
```

```python
import functools
import math

import jax
import jax.numpy as jnp
import numpy as np
from jax import lax
from jax.experimental import pallas as pl
from jax.experimental.pallas import tpu as pltpu
from jax.sharding import PartitionSpec as P

HEAD_DIM = 64
PAIR = 2 * HEAD_DIM
TILE = 256
GAIN_ROWS = 16
norm_eps = 1e-06
F32 = jnp.float32
BF16 = jnp.bfloat16
AXES = ("dp", "fsdp")
ANY = pl.BlockSpec(memory_space=pl.ANY)


def dot_nn(a, b):
    return lax.dot_general(a, b, (((1,), (0,)), ((), ())), preferred_element_type=F32)


def dot_nt(a, b):
    return lax.dot_general(a, b, (((1,), (1,)), ((), ())), preferred_element_type=F32)


def dot_tn(a, b):
    return lax.dot_general(a, b, (((0,), (0,)), ((), ())), preferred_element_type=F32)


def rotary_tables(count):
    half = HEAD_DIM // 2
    frequency = np.exp(
        -(np.arange(half, dtype=np.float32) * np.float32(2.0) / np.float32(HEAD_DIM))
        * np.float32(math.log(10000.0))
    ).astype(np.float32)
    angles = np.arange(count, dtype=np.float32)[:, None] * frequency[None, :]
    cosine = np.cos(angles.astype(np.float64)).astype(np.float32)
    sine = np.sin(angles.astype(np.float64)).astype(np.float32)
    cosine = np.concatenate([cosine] * 4, axis=1)
    sine = np.concatenate([-sine, sine, -sine, sine], axis=1)
    return cosine, sine


def swap_halves(x):
    half = HEAD_DIM // 2
    lane = lax.broadcasted_iota(jnp.int32, x.shape, 1)
    up = pltpu.roll(x, PAIR - half, 1)
    down = pltpu.roll(x, half, 1)
    return jnp.where((lane % HEAD_DIM) < half, up, down)


def bit_reverse(value, bits):
    out = 0
    for i in range(bits):
        out = out + ((value >> i) & 1) * (1 << (bits - 1 - i))
    return out


class Layout:
    def __init__(self, dp, fs):
        self.dp, self.fs = dp, fs
        self.bits = fs.bit_length() - 1
        self.line = dp // 2

    def perm(self, move):
        pairs = []
        for d in range(self.dp):
            for f in range(self.fs):
                target = move(d, f)
                if target is not None:
                    pairs.append((d * self.fs + f, target[0] * self.fs + target[1]))
        return pairs

    def send(self, x, move):
        return lax.ppermute(x, AXES, self.perm(move))

    def core(self, x):
        return self.send(x, lambda d, f: (d ^ 1, f))

    def step(self, x, i):
        bits = self.bits
        return self.send(x, lambda d, f: (d, f ^ (1 << (i if d % 2 == 0 else bits - 1 - i))))

    def index(self, length):
        d, f = lax.axis_index("dp"), lax.axis_index("fsdp")
        c = d % 2
        masks = jnp.arange(self.fs, dtype=jnp.int32)
        turned = bit_reverse(masks, self.bits)
        straight = c == 0
        mine = f ^ jnp.where(straight, masks, turned)
        other = f ^ jnp.where(straight, turned, masks)
        order = f ^ jnp.where(straight, turned, masks)
        head = jnp.stack([c, 1 - c, length, f]).astype(jnp.int32)
        return jnp.concatenate([head, mine, other, order]).astype(jnp.int32)

    def gather(self, half):
        pieces = [half]
        for i in range(self.bits):
            pieces = pieces + [self.step(piece, i) for piece in pieces]
        return pieces, [self.core(piece) for piece in pieces[1:]]

    def line_sum(self, total):
        size = self.line
        if size == 1:
            return total
        half = size // 2
        r = lax.axis_index("dp") // 2

        def hop(x, table):
            return self.send(
                x, lambda d, f: (table[d // 2] * 2 + d % 2, f) if d // 2 in table else None
            )

        for i in range(half - 1):
            got = hop(total, {i: i + 1, size - 1 - i: size - 2 - i})
            total = add_low(total, got)
        got = hop(total, {half - 1: half, half: half - 1})
        total = add_low(total, got)
        for i in range(half - 1):
            low, high = half - 1 - i, half + i
            got = hop(total, {low: low - 1, high: high + 1})
            total = jnp.where((r == low - 1) | (r == high + 1), got, total)
        return total

    def reduce(self, keep, send):
        for i in range(self.bits):
            got = self.step(send, i)
            total = add_low(keep, got)
            blocks = total.shape[0]
            if blocks > 1:
                keep, send = total[: blocks // 2], total[blocks // 2 :]
        return self.line_sum(total[0])

    def small_sum(self, x):
        x = x + self.core(x)
        for i in range(self.bits):
            x = x + self.step(x, i)
        reach = 1
        while reach < self.line:
            x = x + self.send(x, lambda d, f: ((((d // 2) ^ reach) * 2 + d % 2), f))
            reach *= 2
        return x


def add_low(a, b):
    return (a.astype(F32) + b.astype(F32)).astype(BF16)


IDX_HEAD = 4


def start(copies):
    for copy in copies:
        copy.start()


def wait(copies):
    for copy in copies:
        copy.wait()


def call(body, grid, in_specs, out_specs, out_shape, scratch, name, flops, nbytes, limit=56):
    return pl.pallas_call(
        body,
        grid_spec=pltpu.PrefetchScalarGridSpec(
            num_scalar_prefetch=1,
            grid=grid,
            in_specs=in_specs,
            out_specs=out_specs,
            scratch_shapes=scratch,
        ),
        out_shape=out_shape,
        compiler_params=pltpu.CompilerParams(vmem_limit_bytes=limit * 2**20),
        cost_estimate=pl.CostEstimate(
            flops=int(flops), bytes_accessed=int(nbytes), transcendentals=0
        ),
        name=name,
    )


def whole(shape):
    zeros = (0,) * len(shape)
    return pl.BlockSpec(shape, lambda *_: zeros)


def struct(shape, dtype):
    return jax.ShapeDtypeStruct(shape, dtype)


class Place:
    def __init__(self, lay):
        self.bits, self.count = lay.bits, lay.fs
        self.d, self.f = lax.axis_index("dp"), lax.axis_index("fsdp")
        self.c = lax.rem(self.d, 2)
        self.flips = []
        for i in range(self.bits):
            ahead, back = 1 << i, 1 << (self.bits - 1 - i)
            one = ahead * (1 - 2 * lax.rem(self.f // ahead, 2))
            two = back * (1 - 2 * lax.rem(self.f // back, 2))
            self.flips.append(one + self.c * (two - one))

    def shard(self, m):
        return self.f + sum(self.flips[i] for i in range(self.bits) if (m >> i) & 1)

    def partner(self, i):
        return (self.d, self.f + self.flips[i])

    def sibling(self):
        return (self.d + 1 - 2 * self.c, self.f)

    def group(self):
        others = []
        for m in range(1, self.count):
            others.append((self.d, self.shard(m)))
        return others


def remote(src, dst, send, recv, device):
    return pltpu.make_async_remote_copy(
        src_ref=src,
        dst_ref=dst,
        send_sem=send,
        recv_sem=recv,
        device_id=device,
        device_id_type=pl.DeviceIdType.MESH,
    )


class Gather:
    def __init__(self, place, own, full, sems, slot):
        self.place = place
        send, recv, cross_send, cross_recv, local = sems
        count = place.count
        rows, side = own.shape[0], own.shape[1] // 2
        column = pl.multiple_of(place.c * side, 128)
        self.link, self.cross = [None], [None]
        self.local = pltpu.make_async_copy(
            own, full.at[pl.ds(pl.multiple_of(place.f * rows, rows), rows), :], local.at[slot]
        )
        for m in range(1, count):
            step = m.bit_length() - 1
            before = m - (1 << step)

            def spot(piece):
                at = pl.multiple_of(place.shard(piece) * rows, rows)
                return full.at[pl.ds(at, rows), pl.ds(column, side)]

            source = own.at[:, pl.ds(column, side)] if before == 0 else spot(before)
            self.link.append(
                remote(
                    source,
                    spot(before),
                    send.at[slot * count + m],
                    recv.at[slot * count + m],
                    place.partner(step),
                )
            )
            self.cross.append(
                remote(
                    spot(m),
                    spot(m),
                    cross_send.at[slot * count + m],
                    cross_recv.at[slot * count + m],
                    place.sibling(),
                )
            )

    def begin(self):
        for i in range(self.place.bits):
            self.link[1 << i].start()

    def arrived(self, m):
        self.link[m].wait_recv()
        for i in range(m.bit_length(), self.place.bits):
            self.link[m + (1 << i)].start()
        self.cross[m].start()

    def complete(self):
        for copy in self.cross[1:]:
            copy.wait_recv()

    def drain(self):
        for copy in self.link[1:] + self.cross[1:]:
            copy.wait_send()


def forward_body(
    lay,
    lengths,
    tokens,
    first,
    cosine,
    sine,
    gain_in,
    cotangent,
    in_qkv,
    in_out,
    in_gate,
    in_up,
    in_down,
    full_qkv,
    full_out,
    full_gate,
    full_up,
    full_down,
    out_q,
    out_k,
    out_v,
    logs,
    hidden_one2,
    attended2,
    hidden_two2,
    out_after,
    out_gate,
    out_up,
    out_product,
    grad_down,
    gains,
    sums,
    w_qkv,
    w_out,
    w_gate,
    w_up,
    gain,
    hidden,
    queries,
    keys,
    values,
    attended,
    after,
    gate_pre,
    low_gate,
    low_up,
    product2,
    cot2,
    grad_low,
    turned,
    send,
    recv,
    cross_send,
    cross_recv,
    local,
    gain_send,
    gain_recv,
    swap_send,
    swap_recv,
    write,
):
    place = Place(lay)
    count, c = place.count, place.c
    rows, width = tokens.shape
    shard_rows = in_qkv.shape[0]
    ff = in_gate.shape[1]
    sibling = place.sibling()

    barrier = pltpu.get_barrier_semaphore()
    for device in [sibling] + place.group():
        pl.semaphore_signal(barrier, inc=1, device_id=device, device_id_type=pl.DeviceIdType.MESH)
    pl.semaphore_wait(barrier, count)

    sems = (send, recv, cross_send, cross_recv, local)
    g_qkv = Gather(place, in_qkv, w_qkv, sems, 0)
    g_out = Gather(place, in_out, w_out, sems, 1)
    g_gate = Gather(place, in_gate, w_gate, sems, 2)
    g_up = Gather(place, in_up, w_up, sems, 3)
    g_down = Gather(place, in_down, full_down, sems, 4)
    gathers = [g_qkv, g_out, g_gate, g_up, g_down]
    g_qkv.begin()
    gain_at = pl.multiple_of(place.f * shard_rows, shard_rows)
    gain_copies = []
    for m, device in enumerate(place.group()):
        gain_copies.append(
            remote(
                gain_in,
                gain.at[:, pl.ds(gain_at, shard_rows)],
                gain_send.at[m],
                gain_recv.at[m],
                device,
            )
        )
    gain_own = pltpu.make_async_copy(
        gain_in, gain.at[:, pl.ds(gain_at, shard_rows)], local.at[5]
    )
    start(gain_copies + [gain_own])
    for gather in gathers:
        gather.local.start()
    g_out.begin()

    writes = []

    def put(source, target):
        copy = pltpu.make_async_copy(source, target, write.at[len(writes)])
        copy.start()
        writes.append(copy)

    swaps = []

    def swap(source, target):
        slot = len(swaps)
        copy = remote(source, target, swap_send.at[slot], swap_recv.at[slot], sibling)
        copy.start()
        swaps.append(copy)
        return copy

    def share(source, target):
        put(source, target.at[pl.ds(0, rows), :])
        return swap(source, target.at[pl.ds(rows, rows), :])

    half = width // 2
    theirs = pl.multiple_of((1 - c) * half, 128)
    ours = pl.multiple_of(c * half, 128)
    cot_swap = swap(cotangent.at[:, pl.ds(theirs, half)], cot2.at[pl.ds(rows, rows), :])
    cot_own = pltpu.make_async_copy(
        cotangent.at[:, pl.ds(ours, half)], cot2.at[pl.ds(0, rows), :], local.at[6]
    )
    cot_own.start()

    inputs = tokens[...].astype(F32)
    inverse = lax.rsqrt(jnp.mean(inputs * inputs, axis=-1, keepdims=True) + norm_eps)
    for copy in gain_copies:
        copy.wait_recv()
    gain_own.wait()
    gains[0:1, :] = gain[0:1, :].astype(F32)
    gains[1:2, :] = gain[1:2, :].astype(F32)
    gains[2:8, :] = jnp.zeros((6, width), F32)
    hidden[...] = (inputs * inverse * gains[0:1, :]).astype(BF16)
    share(hidden, hidden_one2)
    for m in range(1, count):
        g_qkv.arrived(m)
        if m == count // 2:
            g_gate.begin()
    for m in range(1, count):
        g_out.arrived(m)
    g_qkv.local.wait()
    g_qkv.complete()
    put(w_qkv, full_qkv)
    g_up.begin()
    g_out.local.wait()
    g_out.complete()
    put(w_out, full_out)

    block = min(TILE, rows)

    @pl.loop(0, rows // block)
    def _(i):
        at = pl.ds(pl.multiple_of(i * block, block), block)
        cos, sin = cosine[at, :], sine[at, :]
        for which, out, scale in ((0, queries, HEAD_DIM**-0.5), (1, keys, 1.0)):
            raw = dot_nn(hidden[at, :], w_qkv[:, which * width : (which + 1) * width])
            for p in range(width // PAIR):
                x = raw[:, p * PAIR : (p + 1) * PAIR]
                low = (x * cos + swap_halves(x) * sin).astype(BF16)
                out[at, p * PAIR : (p + 1) * PAIR] = low * jnp.asarray(scale, BF16)

    sums[...] = jnp.zeros(sums.shape, F32)

    @pl.loop(0, rows // block)
    def _(i):
        at = pl.ds(pl.multiple_of(i * block, block), block)
        raw = dot_nn(hidden[at, :], w_qkv[:, 2 * width : 3 * width])
        kept = first[at, :].astype(F32)
        mixed = 0.5 * raw + 0.5 * kept
        values[at, :] = mixed.astype(BF16)
        sums[0:1, :] += jnp.sum(kept * kept, axis=0, keepdims=True)
        sums[1:2, :] += jnp.sum(mixed * mixed, axis=0, keepdims=True)

    put(queries, out_q)
    put(keys, out_k)
    put(values, out_v)
    length = lengths[0]

    def attend(begin, end):
        @pl.loop(begin, end)
        def _(p):
            at = pl.ds(pl.multiple_of(p * PAIR, PAIR), PAIR)
            q, k = queries[:, at], keys[:, at]
            v_t = values[:, at].T
            lane = lax.broadcasted_iota(jnp.int32, (rows, PAIR), 1)
            for head in range(2):
                inside = (lane // HEAD_DIM) == head
                k_head = jnp.where(inside, k, jnp.zeros_like(k))
                v_head = v_t[head * HEAD_DIM : (head + 1) * HEAD_DIM]
                for b in range(rows // block):
                    upto = (b + 1) * block
                    scores = dot_nt(k_head[:upto], q[b * block : upto])
                    key = lax.broadcasted_iota(jnp.int32, scores.shape, 0)
                    query = lax.broadcasted_iota(jnp.int32, (1, block), 1) + b * block
                    allowed = key <= jnp.minimum(query, length - 1)
                    scores = jnp.where(allowed, scores, -1e30)
                    peak = jnp.max(scores, axis=0, keepdims=True)
                    expo = jnp.exp(scores - peak)
                    total = jnp.sum(expo, axis=0, keepdims=True)
                    soft = (expo * (1.0 / total)).astype(BF16)
                    logs[p, head : head + 1, b * block : upto] = peak + jnp.log(total)
                    turned[head * HEAD_DIM : (head + 1) * HEAD_DIM, b * block : upto] = dot_nn(
                        v_head[:, :upto], soft
                    )
            attended[:, at] = turned[...].T.astype(BF16)

    pairs = width // PAIR
    logs[...] = jnp.zeros(logs.shape, F32)
    attend(0, pairs // 4)
    for m in range(1, count // 2):
        g_gate.arrived(m)
    attend(pairs // 4, pairs // 2)
    for m in range(count // 2, count):
        g_gate.arrived(m)
    g_down.begin()
    attend(pairs // 2, 3 * pairs // 4)
    for m in range(1, count // 2):
        g_up.arrived(m)
    attend(3 * pairs // 4, pairs)
    for m in range(count // 2, count):
        g_up.arrived(m)

    share(attended, attended2)

    @pl.loop(0, rows // block)
    def _(i):
        at = pl.ds(pl.multiple_of(i * block, block), block)
        x = tokens[at, :].astype(F32) + dot_nn(attended[at, :], w_out[...])
        after[at, :] = x
        scale = lax.rsqrt(jnp.mean(x * x, axis=-1, keepdims=True) + norm_eps)
        low_up[at, 0:width] = (x * scale * gains[1:2, :]).astype(BF16)

    put(after, out_after)
    hidden_two = low_up.at[:, pl.ds(0, width)]
    second = share(hidden_two, hidden_two2)
    second_put = writes[-1]
    g_gate.local.wait()
    g_gate.complete()
    put(w_gate, full_gate)

    @pl.loop(0, rows // block)
    def _(i):
        at = pl.ds(pl.multiple_of(i * block, block), block)
        gate_pre[at, :] = dot_nn(low_up[at, 0:width], w_gate[...])
        low_gate[at, :] = gate_pre[at, :].astype(BF16)

    put(low_gate, out_gate)
    g_up.local.wait()
    g_up.complete()
    put(w_up, full_up)
    for m in range(1, count // 2):
        g_down.arrived(m)
    second.wait_send()
    second_put.wait()

    @pl.loop(0, rows // block)
    def _(i):
        at = pl.ds(pl.multiple_of(i * block, block), block)
        up_proj = dot_nn(low_up[at, 0:width], w_up[...])
        gate_of = gate_pre[at, :]
        product2[at, :] = (gate_of * jax.nn.sigmoid(gate_of) * up_proj).astype(BF16)
        low_up[at, :] = up_proj.astype(BF16)

    put(low_up, out_up)
    own_product = product2.at[pl.ds(0, rows), :]
    put(own_product, out_product)
    product_swap = swap(own_product, product2.at[pl.ds(rows, rows), :])
    for m in range(count // 2, count):
        g_down.arrived(m)
    cot_own.wait()
    cot_swap.wait_recv()
    product_swap.wait_recv()

    @pl.loop(0, ff // TILE)
    def _(i):
        at = pl.ds(pl.multiple_of(i * TILE, TILE), TILE)
        grad_low[at, :] = dot_tn(product2[:, at], cot2[...]).astype(BF16)

    put(grad_low, grad_down)
    g_down.local.wait()
    g_down.complete()
    for gather in gathers:
        gather.drain()
    for copy in gain_copies:
        copy.wait_send()
    for copy in swaps:
        if copy is not cot_swap and copy is not product_swap:
            copy.wait_recv()
        if copy is not second:
            copy.wait_send()
    for copy in writes:
        if copy is not second_put:
            copy.wait()


def forward_kernel(lay, lengths, tokens, first, tables, gain_in, cotangent, w_qkv, w_out, w_gate, w_up, w_down):
    count = lay.fs
    rows, width = tokens.shape
    n, ff = w_qkv.shape[1], w_gate.shape[1]
    half = width // 2
    pairs = width // PAIR
    big = struct((rows, width), BF16)
    wide = struct((rows, ff), BF16)
    two = struct((2 * rows, width), BF16)
    dma = pltpu.SemaphoreType.DMA
    vmem = pl.BlockSpec(memory_space=pltpu.VMEM)
    weights = [(width, n), (width, width), (width, ff), (width, ff), (ff, width)]
    out_shape = (
        [struct(shape, BF16) for shape in weights]
        + [big, big, big, struct((pairs, 8, rows), F32)]
        + [two, two, two, struct((rows, width), F32), wide, wide, wide]
        + [struct((ff, half), BF16), struct((8, width), F32), struct((8, width), F32)]
    )
    out_specs = [ANY] * 8 + [vmem] + [ANY] * 8 + [vmem, vmem]
    return pl.pallas_call(
        functools.partial(forward_body, lay),
        in_specs=[pl.BlockSpec(memory_space=pltpu.SMEM)] + [vmem] * 4 + [vmem] + [ANY] * 6,
        out_specs=out_specs,
        out_shape=out_shape,
        scratch_shapes=[
            pltpu.VMEM((width, n), BF16),
            pltpu.VMEM((width, width), BF16),
            pltpu.VMEM((width, ff), BF16),
            pltpu.VMEM((width, ff), BF16),
            pltpu.VMEM((GAIN_ROWS, width), BF16),
            pltpu.VMEM((rows, width), BF16),
            pltpu.VMEM((rows, width), BF16),
            pltpu.VMEM((rows, width), BF16),
            pltpu.VMEM((rows, width), BF16),
            pltpu.VMEM((rows, width), BF16),
            pltpu.VMEM((rows, width), F32),
            pltpu.VMEM((rows, ff), F32),
            pltpu.VMEM((rows, ff), BF16),
            pltpu.VMEM((rows, ff), BF16),
            pltpu.VMEM((2 * rows, ff), BF16),
            pltpu.VMEM((2 * rows, half), BF16),
            pltpu.VMEM((ff, half), BF16),
            pltpu.VMEM((PAIR, rows), F32),
            dma((5 * count,)),
            dma((5 * count,)),
            dma((5 * count,)),
            dma((5 * count,)),
            dma((7,)),
            dma((count - 1,)),
            dma((count - 1,)),
            dma((5,)),
            dma((5,)),
            dma((16,)),
        ],
        compiler_params=pltpu.CompilerParams(
            collective_id=0, has_side_effects=True, vmem_limit_bytes=62 * 2**20
        ),
        cost_estimate=pl.CostEstimate(
            flops=2 * rows * width * (n + width + 3 * ff),
            bytes_accessed=60 * 2**20,
            transcendentals=0,
        ),
        name="forward",
    )(lengths, tokens, first, *tables, gain_in, cotangent, w_qkv, w_out, w_gate, w_up, w_down)


def attend_back_body(
    idx, queries, keys, values, grads, logs, cosine, sine, grad_q, grad_k, grad_v, grad_first, turned
):
    rows = queries.shape[0]
    block = min(TILE, rows)
    length = idx[2]
    lane = lax.broadcasted_iota(jnp.int32, (rows, PAIR), 1)
    q, k, v, g = queries[...], keys[...], values[...], grads[...]
    k_t = k.T
    sums_k, sums_v = [], []
    for head in range(2):
        inside = (lane // HEAD_DIM) == head
        k_head = jnp.where(inside, k, jnp.zeros_like(k))
        v_head = jnp.where(inside, v, jnp.zeros_like(v))
        k_turned = k_t[head * HEAD_DIM : (head + 1) * HEAD_DIM]
        parts_k, parts_v = [], []
        for b in range(rows // block):
            upto = (b + 1) * block
            q_block, g_block = q[b * block : upto], g[b * block : upto]
            scores = dot_nt(k_head[:upto], q_block)
            key = lax.broadcasted_iota(jnp.int32, scores.shape, 0)
            query = lax.broadcasted_iota(jnp.int32, (1, block), 1) + b * block
            log_total = logs[0, head : head + 1, b * block : upto]
            soft = jnp.where(
                key <= jnp.minimum(query, length - 1), jnp.exp(scores - log_total), 0.0
            )
            grad_soft = dot_nt(v_head[:upto], g_block)
            inner = jnp.sum(soft * grad_soft, axis=0, keepdims=True)
            grad_scores = (soft * (grad_soft - inner)).astype(BF16)
            turned[head * HEAD_DIM : (head + 1) * HEAD_DIM, b * block : upto] = dot_nn(
                k_turned[:, :upto], grad_scores
            )
            parts_k.append(dot_nn(grad_scores, q_block))
            parts_v.append(dot_nn(soft.astype(BF16), g_block))
        for parts, sums in ((parts_k, sums_k), (parts_v, sums_v)):
            rows_of = []
            for r in range(rows // block):
                piece = parts[r][r * block : (r + 1) * block]
                for later in parts[r + 1 :]:
                    piece = piece + later[r * block : (r + 1) * block]
                rows_of.append(piece)
            sums.append(jnp.concatenate(rows_of, axis=0))
    first_head = lane < HEAD_DIM
    cos, sin = cosine[...], sine[...]

    def back(x):
        return (x * cos - swap_halves(x) * sin).astype(BF16)

    grad_q[...] = back(turned[...].T * HEAD_DIM**-0.5)
    grad_k[...] = back(jnp.where(first_head, sums_k[0], sums_k[1]))
    half_v = 0.5 * jnp.where(first_head, sums_v[0], sums_v[1])
    grad_first[...] = half_v
    grad_v[...] = half_v.astype(BF16)


def attend_back_kernel(idx, queries, keys, values, grads, logs, tables):
    rows, width = queries.shape
    pairs = width // PAIR
    column = pl.BlockSpec((rows, PAIR), lambda p, _: (0, p))
    return call(
        attend_back_body,
        (pairs,),
        [column] * 4
        + [
            pl.BlockSpec((1, 8, rows), lambda p, _: (p, 0, 0)),
            whole(tables[0].shape),
            whole(tables[1].shape),
        ],
        [column] * 4,
        [struct((rows, width), BF16)] * 3 + [struct((rows, width), F32)],
        [pltpu.VMEM((PAIR, rows), F32)],
        "attend_back",
        20 * rows * rows * width,
        18 * rows * width,
        40,
    )(idx, queries, keys, values, grads, logs, *tables)


def down_body(idx, cotangent, after, gate, up, product, weight, grad_gate, grad_up, output, total):
    t = pl.program_id(0)

    @pl.when(t == 0)
    def _():
        total[...] = after[...]

    rows_of = weight[...]
    grad_product = dot_nt(cotangent[...], rows_of)
    gate_pre = gate[...].astype(F32)
    up_proj = up[...].astype(F32)
    sigma = jax.nn.sigmoid(gate_pre)
    grad_gate[...] = (
        grad_product * up_proj * sigma * (1.0 + gate_pre * (1.0 - sigma))
    ).astype(BF16)
    grad_up[...] = (grad_product * (gate_pre * sigma)).astype(BF16)
    total[...] += dot_nn(product[...], rows_of)

    @pl.when(t == pl.num_programs(0) - 1)
    def _():
        output[...] = total[...].astype(BF16)


def down_kernel(idx, cotangent, after, gate, up, product, weight):
    rows, width = cotangent.shape
    hidden = gate.shape[1]
    tile = pl.BlockSpec((rows, TILE), lambda t, _: (0, t))
    return call(
        down_body,
        (hidden // TILE,),
        [whole(cotangent.shape), whole(after.shape), tile, tile, tile]
        + [pl.BlockSpec((TILE, width), lambda t, _: (t, 0))],
        [tile, tile, whole((rows, width))],
        [
            struct((rows, hidden), BF16),
            struct((rows, hidden), BF16),
            struct((rows, width), BF16),
        ],
        [pltpu.VMEM((rows, width), F32)],
        "down",
        4 * rows * width * hidden,
        2 * width * hidden + 10 * rows * hidden,
    )(idx, cotangent, after, gate, up, product, weight)


def rms_back(grad, normed, inverse):
    return inverse * (grad - normed * jnp.mean(grad * normed, axis=-1, keepdims=True))


def mlp_back_body(idx, grad_gate, grad_up, after, cotangent, gains, w_out, w_gate, w_up, *rest):
    grad_after, grad_low, grad_attended, grad_gain, total = rest
    width = w_gate.shape[0]

    @pl.loop(0, width // TILE)
    def _(t):
        at = pl.multiple_of(t * TILE, TILE)
        total[:, pl.ds(at, TILE)] = dot_nt(grad_gate[...], w_gate[pl.ds(at, TILE), :]) + dot_nt(
            grad_up[...], w_up[pl.ds(at, TILE), :]
        )

    x = after[...]
    inverse = lax.rsqrt(jnp.mean(x * x, axis=-1, keepdims=True) + norm_eps)
    normed = x * inverse
    grad_hidden = total[...]
    grad_gain[...] = jnp.zeros(grad_gain.shape, F32)
    grad_gain[0:1, :] = jnp.sum(grad_hidden * normed, axis=0, keepdims=True)
    result = cotangent[...].astype(F32) + rms_back(grad_hidden * gains[1:2, :], normed, inverse)
    grad_after[...] = result
    grad_low[...] = result.astype(BF16)

    @pl.loop(0, width // TILE)
    def _(t):
        at = pl.multiple_of(t * TILE, TILE)
        grad_attended[:, pl.ds(at, TILE)] = dot_nt(
            grad_low[...], w_out[pl.ds(at, TILE), :]
        ).astype(BF16)


def mlp_back_kernel(idx, *operands):
    cotangent = operands[3]
    rows, width = cotangent.shape
    hidden = operands[0].shape[1]
    return call(
        mlp_back_body,
        (1,),
        [whole(item.shape) for item in operands],
        [whole((rows, width)), whole((rows, width)), whole((rows, width)), whole((8, width))],
        [
            struct((rows, width), F32),
            struct((rows, width), BF16),
            struct((rows, width), BF16),
            struct((8, width), F32),
        ],
        [pltpu.VMEM((rows, width), F32)],
        "mlp_back",
        2 * rows * width * (width + 2 * hidden),
        2 * width * (width + 2 * hidden) + 4 * rows * hidden + 12 * rows * width,
        62,
    )(idx, *operands)


def qkv_back_body(idx, grad_q, grad_k, grad_v, tokens, grad_after, gains, weight, grad_tokens, grad_gain, total):
    x = tokens[...].astype(F32)
    inverse = lax.rsqrt(jnp.mean(x * x, axis=-1, keepdims=True) + norm_eps)
    width = weight.shape[0]

    @pl.loop(0, width // TILE)
    def _(t):
        at = pl.multiple_of(t * TILE, TILE)
        block = pl.ds(at, TILE)
        total[:, block] = (
            dot_nt(grad_q[...], weight[block, 0:width])
            + dot_nt(grad_k[...], weight[block, width : 2 * width])
            + dot_nt(grad_v[...], weight[block, 2 * width : 3 * width])
        )

    normed = x * inverse
    grad_hidden = total[...]
    grad_gain[...] = jnp.zeros(grad_gain.shape, F32)
    grad_gain[0:1, :] = jnp.sum(grad_hidden * normed, axis=0, keepdims=True)
    grad_tokens[...] = grad_after[...] + rms_back(grad_hidden * gains[0:1, :], normed, inverse)


def qkv_back_kernel(idx, *operands):
    rows, width = operands[0].shape
    n = operands[-1].shape[1]
    return call(
        qkv_back_body,
        (1,),
        [whole(item.shape) for item in operands],
        [whole((rows, width)), whole((8, width))],
        [struct((rows, width), F32), struct((8, width), F32)],
        [pltpu.VMEM((rows, width), F32)],
        "qkv_back",
        2 * rows * width * n,
        2 * width * n + 16 * rows * width,
    )(idx, *operands)


def grad_sibling_body(parts, idx, turned, *rest):
    lefts, out = rest[:parts], rest[parts]
    side = lefts[0].shape[1]
    for i, left in enumerate(lefts):
        out[0, :, i * side : (i + 1) * side] = dot_tn(turned[...], left[...]).astype(BF16)


def grad_own_body(parts, blocks, idx, turned, *rest):
    lefts, got, keep, send = rest[:parts], rest[parts], rest[parts + 1], rest[parts + 2]
    side = lefts[0].shape[1]
    place = pl.program_id(0)

    def block(out):
        for i, left in enumerate(lefts):
            columns = slice(i * side, (i + 1) * side)
            summed = dot_tn(turned[...], left[...]) + got[0, :, columns].astype(F32)
            out[0, :, columns] = summed.astype(BF16)

    @pl.when(place < blocks // 2)
    def _():
        block(keep)

    @pl.when(place >= blocks // 2)
    def _():
        block(send)


def weight_grad(lay, idx, turned, lefts, name):
    blocks = lay.fs
    rows, total = lefts[0].shape[0], turned.shape[1]
    block = total // blocks
    half = [left.shape[1] // 2 for left in lefts]
    wide = sum(half)
    cost = (2 * rows * total * wide, 2 * rows * (total + wide) + 2 * total * wide)
    base = IDX_HEAD + 2 * blocks

    def shard(p, idx):
        return (0, idx[base + p])

    sibling = call(
        functools.partial(grad_sibling_body, len(lefts)),
        (blocks,),
        [pl.BlockSpec((rows, block), lambda p, idx: (0, p))]
        + [pl.BlockSpec((rows, side), lambda p, idx: (0, idx[1])) for side in half],
        [pl.BlockSpec((1, block, wide), lambda p, idx: (p, 0, 0))],
        [struct((blocks, block, wide), BF16)],
        [],
        name + "_sibling",
        *cost,
    )(idx, turned, *lefts)[0]
    got = lay.core(sibling)
    return call(
        functools.partial(grad_own_body, len(lefts), blocks),
        (blocks,),
        [pl.BlockSpec((rows, block), shard)]
        + [pl.BlockSpec((rows, side), lambda p, idx: (0, idx[0])) for side in half]
        + [pl.BlockSpec((1, block, wide), lambda p, idx: (idx[base + p], 0, 0))],
        [
            pl.BlockSpec((1, block, wide), lambda p, idx: (jnp.minimum(p, blocks // 2 - 1), 0, 0)),
            pl.BlockSpec((1, block, wide), lambda p, idx: (jnp.maximum(p - blocks // 2, 0), 0, 0)),
        ],
        [struct((blocks // 2, block, wide), BF16)] * 2,
        [],
        name + "_own",
        *cost,
    )(idx, turned, *lefts, got)


def finish_body(parts, idx, mine, other, *outs):
    low = idx[0] == 0
    at = 0
    for out in outs:
        side = out.shape[1] // 2
        a = mine[:, at : at + side].astype(F32)
        b = other[:, at : at + side].astype(F32)
        out[:, 0:side] = jnp.where(low, a, b)
        out[:, side:] = jnp.where(low, b, a)
        at += side


def finish(lay, idx, mine, widths, name):
    other = lay.core(mine)
    rows, wide = mine.shape
    block = rows // 4 if rows % 64 == 0 else rows
    return call(
        functools.partial(finish_body, len(widths)),
        (rows // block,),
        [pl.BlockSpec((block, wide), lambda p, _: (p, 0))] * 2,
        [pl.BlockSpec((block, 2 * side), lambda p, _: (p, 0)) for side in widths],
        [struct((rows, 2 * side), F32) for side in widths],
        [],
        name,
        0,
        12 * rows * wide,
    )(idx, mine, other)


def body(
    lay,
    tokens,
    first_values,
    lengths,
    gain_one,
    w_qkv,
    w_out,
    gain_two,
    w_gate,
    w_up,
    w_down,
    cotangent,
):
    rows, width = tokens.shape
    hidden = w_gate.shape[1]
    shard_rows = w_qkv.shape[0]
    idx = lay.index(lengths[0])
    tables = tuple(jnp.asarray(table) for table in rotary_tables(rows))
    c = lax.axis_index("dp") % 2
    gain_block = jnp.pad(jnp.stack([gain_one, gain_two]), ((0, GAIN_ROWS - 2), (0, 0)))
    (
        full_qkv,
        full_out,
        full_gate,
        full_up,
        full_down,
        queries,
        keys,
        values,
        logs,
        hidden_one,
        attended,
        hidden_two,
        after,
        gate,
        up,
        product,
        down_sum,
        gains,
        sums,
    ) = forward_kernel(
        lay, lengths, tokens, first_values, tables, gain_block, cotangent, w_qkv, w_out, w_gate, w_up, w_down
    )
    blocks = jnp.take(
        down_sum.reshape(lay.fs, -1, width // 2), idx[IDX_HEAD + 2 * lay.fs :], axis=0
    )
    total_down = lay.reduce(blocks[: lay.fs // 2], blocks[lay.fs // 2 :])
    grad_gate, grad_up, output = down_kernel(idx, cotangent, after, gate, up, product, full_down)
    keep, send = weight_grad(lay, idx, hidden_two, [grad_gate, grad_up], "grad_gate_up")
    total_gate_up = lay.reduce(keep, send)
    grad_after, grad_after_low, grad_attended, grad_gain_two = mlp_back_kernel(
        idx, grad_gate, grad_up, after, cotangent, gains, full_out, full_gate, full_up
    )
    keep, send = weight_grad(lay, idx, attended, [grad_after_low], "grad_out")
    total_out = lay.reduce(keep, send)
    grad_q, grad_k, grad_v, grad_first = attend_back_kernel(
        idx, queries, keys, values, grad_attended, logs, tables
    )
    keep, send = weight_grad(lay, idx, hidden_one, [grad_q, grad_k, grad_v], "grad_qkv")
    total_qkv = lay.reduce(keep, send)
    grad_tokens, grad_gain_one = qkv_back_kernel(
        idx, grad_q, grad_k, grad_v, tokens, grad_after, gains, full_qkv
    )

    small = jnp.concatenate(
        [
            grad_gain_one[0:1],
            grad_gain_two[0:1],
            jnp.pad(jnp.sum(sums, axis=1)[None], ((0, 5), (0, width - 8))),
        ]
    )
    small = lay.small_sum(small)
    at = lax.axis_index("fsdp") * shard_rows
    entry_count = rows * width * lay.dp * lay.fs
    shard_gain_one = lax.dynamic_slice(small[0], (at,), (shard_rows,))
    shard_gain_two = lax.dynamic_slice(small[1], (at,), (shard_rows,))
    first_norm = small[2, 0] / entry_count
    value_norm = small[2, 1] / entry_count

    (shard_down,) = finish(lay, idx, total_down, [width // 2], "finish_down")
    shard_gate, shard_up = finish(lay, idx, total_gate_up, [hidden // 2] * 2, "finish_gate_up")
    (shard_out,) = finish(lay, idx, total_out, [width // 2], "finish_out")
    third = width // 2
    other_qkv = lay.core(total_qkv)
    low = c == 0
    blocks = []
    for i in range(3):
        a = total_qkv[:, i * third : (i + 1) * third].astype(F32)
        b = other_qkv[:, i * third : (i + 1) * third].astype(F32)
        blocks += [jnp.where(low, a, b), jnp.where(low, b, a)]
    shard_qkv = jnp.concatenate(blocks, axis=1)
    return (
        output,
        grad_tokens,
        grad_first,
        shard_gain_one,
        shard_qkv,
        shard_out,
        shard_gain_two,
        shard_gate,
        shard_up,
        shard_down,
        first_norm,
        value_norm,
    )


def solution(mesh):
    both = P(AXES, None)
    rows = P("fsdp", None)
    in_specs = (both, both, P(AXES), P("fsdp"), rows, rows, P("fsdp"), rows, rows, rows, both)
    out_specs = (both, both, both, P("fsdp"), rows, rows, P("fsdp"), rows, rows, rows, P(), P())
    lay = Layout(mesh.shape["dp"], mesh.shape["fsdp"])
    return jax.shard_map(
        functools.partial(body, lay),
        mesh=mesh,
        in_specs=in_specs,
        out_specs=out_specs,
        check_vma=False,
    )
```

```python
import functools
import math

import jax
import jax.numpy as jnp
import numpy as np
from jax import lax
from jax.experimental import pallas as pl
from jax.experimental.pallas import tpu as pltpu
from jax.sharding import PartitionSpec as P

HEAD_DIM = 64
PAIR = 2 * HEAD_DIM
TILE = 256
GAIN_ROWS = 16
norm_eps = 1e-06
F32 = jnp.float32
BF16 = jnp.bfloat16
AXES = ("dp", "fsdp")
ANY = pl.BlockSpec(memory_space=pl.ANY)


def dot_nn(a, b):
    return lax.dot_general(a, b, (((1,), (0,)), ((), ())), preferred_element_type=F32)


def dot_nt(a, b):
    return lax.dot_general(a, b, (((1,), (1,)), ((), ())), preferred_element_type=F32)


def dot_tn(a, b):
    return lax.dot_general(a, b, (((0,), (0,)), ((), ())), preferred_element_type=F32)


def rotary_tables(count):
    half = HEAD_DIM // 2
    frequency = np.exp(
        -(np.arange(half, dtype=np.float32) * np.float32(2.0) / np.float32(HEAD_DIM))
        * np.float32(math.log(10000.0))
    ).astype(np.float32)
    angles = np.arange(count, dtype=np.float32)[:, None] * frequency[None, :]
    cosine = np.cos(angles.astype(np.float64)).astype(np.float32)
    sine = np.sin(angles.astype(np.float64)).astype(np.float32)
    cosine = np.concatenate([cosine] * 4, axis=1)
    sine = np.concatenate([-sine, sine, -sine, sine], axis=1)
    return cosine, sine


def swap_halves(x):
    half = HEAD_DIM // 2
    lane = lax.broadcasted_iota(jnp.int32, x.shape, 1)
    up = pltpu.roll(x, PAIR - half, 1)
    down = pltpu.roll(x, half, 1)
    return jnp.where((lane % HEAD_DIM) < half, up, down)


class Layout:
    def __init__(self, dp, fs):
        self.dp, self.fs = dp, fs
        self.bits = fs.bit_length() - 1
        self.line = dp // 2


def add_low(a, b):
    return (a.astype(F32) + b.astype(F32)).astype(BF16)


def start(copies):
    for copy in copies:
        copy.start()


def wait(copies):
    for copy in copies:
        copy.wait()


def struct(shape, dtype):
    return jax.ShapeDtypeStruct(shape, dtype)


class Place:
    def __init__(self, lay):
        self.bits, self.count = lay.bits, lay.fs
        self.d, self.f = lax.axis_index("dp"), lax.axis_index("fsdp")
        self.c = lax.rem(self.d, 2)
        self.flips = []
        for i in range(self.bits):
            ahead, back = 1 << i, 1 << (self.bits - 1 - i)
            one = ahead * (1 - 2 * lax.rem(self.f // ahead, 2))
            two = back * (1 - 2 * lax.rem(self.f // back, 2))
            self.flips.append(one + self.c * (two - one))

    def shard(self, m):
        return self.f + sum(self.flips[i] for i in range(self.bits) if (m >> i) & 1)

    def partner(self, i):
        return (self.d, self.f + self.flips[i])

    def sibling(self):
        return (self.d + 1 - 2 * self.c, self.f)

    def group(self):
        others = []
        for m in range(1, self.count):
            others.append((self.d, self.shard(m)))
        return others


def remote(src, dst, send, recv, device):
    return pltpu.make_async_remote_copy(
        src_ref=src,
        dst_ref=dst,
        send_sem=send,
        recv_sem=recv,
        device_id=device,
        device_id_type=pl.DeviceIdType.MESH,
    )


class Gather:
    def __init__(self, place, own, full, sems, slot):
        self.place = place
        send, recv, cross_send, cross_recv, local = sems
        count = place.count
        rows, side = own.shape[0], own.shape[1] // 2
        column = pl.multiple_of(place.c * side, 128)
        self.link, self.cross = [None], [None]
        self.local = pltpu.make_async_copy(
            own, full.at[pl.ds(pl.multiple_of(place.f * rows, rows), rows), :], local.at[slot]
        )
        for m in range(1, count):
            step = m.bit_length() - 1
            before = m - (1 << step)

            def spot(piece):
                at = pl.multiple_of(place.shard(piece) * rows, rows)
                return full.at[pl.ds(at, rows), pl.ds(column, side)]

            source = own.at[:, pl.ds(column, side)] if before == 0 else spot(before)
            self.link.append(
                remote(
                    source,
                    spot(before),
                    send.at[slot * count + m],
                    recv.at[slot * count + m],
                    place.partner(step),
                )
            )
            self.cross.append(
                remote(
                    spot(m),
                    spot(m),
                    cross_send.at[slot * count + m],
                    cross_recv.at[slot * count + m],
                    place.sibling(),
                )
            )

    def begin(self):
        for i in range(self.place.bits):
            self.link[1 << i].start()

    def arrived(self, m):
        self.link[m].wait_recv()
        for i in range(m.bit_length(), self.place.bits):
            self.link[m + (1 << i)].start()
        self.cross[m].start()

    def complete(self):
        for copy in self.cross[1:]:
            copy.wait_recv()

    def drain(self):
        for copy in self.link[1:] + self.cross[1:]:
            copy.wait_send()


def forward_body(
    lay,
    lengths,
    tokens,
    first,
    cosine,
    sine,
    gain_in,
    cotangent,
    in_qkv,
    in_out,
    in_gate,
    in_up,
    in_down,
    full_qkv,
    full_out,
    full_gate,
    full_up,
    full_down,
    out_q,
    out_k,
    out_v,
    logs,
    hidden_one2,
    attended2,
    hidden_two2,
    out_after,
    out_gate,
    out_up,
    out_product,
    grad_down,
    gains,
    sums,
    w_qkv,
    w_out,
    w_gate,
    w_up,
    gain,
    hidden,
    queries,
    keys,
    values,
    attended,
    after,
    gate_pre,
    low_gate,
    low_up,
    product2,
    cot2,
    grad_low,
    turned,
    send,
    recv,
    cross_send,
    cross_recv,
    local,
    gain_send,
    gain_recv,
    swap_send,
    swap_recv,
    write,
):
    place = Place(lay)
    count, c = place.count, place.c
    rows, width = tokens.shape
    shard_rows = in_qkv.shape[0]
    ff = in_gate.shape[1]
    sibling = place.sibling()

    barrier = pltpu.get_barrier_semaphore()
    for device in [sibling] + place.group():
        pl.semaphore_signal(barrier, inc=1, device_id=device, device_id_type=pl.DeviceIdType.MESH)
    pl.semaphore_wait(barrier, count)

    sems = (send, recv, cross_send, cross_recv, local)
    g_qkv = Gather(place, in_qkv, w_qkv, sems, 0)
    g_out = Gather(place, in_out, w_out, sems, 1)
    g_gate = Gather(place, in_gate, w_gate, sems, 2)
    g_up = Gather(place, in_up, w_up, sems, 3)
    g_down = Gather(place, in_down, full_down, sems, 4)
    gathers = [g_qkv, g_out, g_gate, g_up, g_down]
    g_qkv.begin()
    gain_at = pl.multiple_of(place.f * shard_rows, shard_rows)
    gain_copies = []
    for m, device in enumerate(place.group()):
        gain_copies.append(
            remote(
                gain_in,
                gain.at[:, pl.ds(gain_at, shard_rows)],
                gain_send.at[m],
                gain_recv.at[m],
                device,
            )
        )
    gain_own = pltpu.make_async_copy(
        gain_in, gain.at[:, pl.ds(gain_at, shard_rows)], local.at[5]
    )
    start(gain_copies + [gain_own])
    for gather in gathers:
        gather.local.start()
    g_out.begin()

    writes = []

    def put(source, target):
        copy = pltpu.make_async_copy(source, target, write.at[len(writes)])
        copy.start()
        writes.append(copy)

    swaps = []

    def swap(source, target):
        slot = len(swaps)
        copy = remote(source, target, swap_send.at[slot], swap_recv.at[slot], sibling)
        copy.start()
        swaps.append(copy)
        return copy

    def share(source, target):
        put(source, target.at[pl.ds(0, rows), :])
        return swap(source, target.at[pl.ds(rows, rows), :])

    half = width // 2
    theirs = pl.multiple_of((1 - c) * half, 128)
    ours = pl.multiple_of(c * half, 128)
    cot_swap = swap(cotangent.at[:, pl.ds(theirs, half)], cot2.at[pl.ds(rows, rows), :])
    cot_own = pltpu.make_async_copy(
        cotangent.at[:, pl.ds(ours, half)], cot2.at[pl.ds(0, rows), :], local.at[6]
    )
    cot_own.start()

    inputs = tokens[...].astype(F32)
    inverse = lax.rsqrt(jnp.mean(inputs * inputs, axis=-1, keepdims=True) + norm_eps)
    for copy in gain_copies:
        copy.wait_recv()
    gain_own.wait()
    gains[0:1, :] = gain[0:1, :].astype(F32)
    gains[1:2, :] = gain[1:2, :].astype(F32)
    gains[2:8, :] = jnp.zeros((6, width), F32)
    hidden[...] = (inputs * inverse * gains[0:1, :]).astype(BF16)
    share(hidden, hidden_one2)
    for m in range(1, count):
        g_qkv.arrived(m)
        if m == count // 2:
            g_gate.begin()
    for m in range(1, count):
        g_out.arrived(m)
    g_qkv.local.wait()
    g_qkv.complete()
    put(w_qkv, full_qkv)
    g_up.begin()
    g_out.local.wait()
    g_out.complete()
    put(w_out, full_out)

    block = min(TILE, rows)

    @pl.loop(0, rows // block)
    def _(i):
        at = pl.ds(pl.multiple_of(i * block, block), block)
        cos, sin = cosine[at, :], sine[at, :]
        for which, out, scale in ((0, queries, HEAD_DIM**-0.5), (1, keys, 1.0)):
            raw = dot_nn(hidden[at, :], w_qkv[:, which * width : (which + 1) * width])
            for p in range(width // PAIR):
                x = raw[:, p * PAIR : (p + 1) * PAIR]
                low = (x * cos + swap_halves(x) * sin).astype(BF16)
                out[at, p * PAIR : (p + 1) * PAIR] = low * jnp.asarray(scale, BF16)

    sums[...] = jnp.zeros(sums.shape, F32)

    @pl.loop(0, rows // block)
    def _(i):
        at = pl.ds(pl.multiple_of(i * block, block), block)
        raw = dot_nn(hidden[at, :], w_qkv[:, 2 * width : 3 * width])
        kept = first[at, :].astype(F32)
        mixed = 0.5 * raw + 0.5 * kept
        values[at, :] = mixed.astype(BF16)
        sums[0:1, :] += jnp.sum(kept * kept, axis=0, keepdims=True)
        sums[1:2, :] += jnp.sum(mixed * mixed, axis=0, keepdims=True)

    put(queries, out_q)
    put(keys, out_k)
    put(values, out_v)
    length = lengths[0]

    def attend(begin, end):
        @pl.loop(begin, end)
        def _(p):
            at = pl.ds(pl.multiple_of(p * PAIR, PAIR), PAIR)
            q, k = queries[:, at], keys[:, at]
            v_t = values[:, at].T
            lane = lax.broadcasted_iota(jnp.int32, (rows, PAIR), 1)
            for head in range(2):
                inside = (lane // HEAD_DIM) == head
                k_head = jnp.where(inside, k, jnp.zeros_like(k))
                v_head = v_t[head * HEAD_DIM : (head + 1) * HEAD_DIM]
                for b in range(rows // block):
                    upto = (b + 1) * block
                    scores = dot_nt(k_head[:upto], q[b * block : upto])
                    key = lax.broadcasted_iota(jnp.int32, scores.shape, 0)
                    query = lax.broadcasted_iota(jnp.int32, (1, block), 1) + b * block
                    allowed = key <= jnp.minimum(query, length - 1)
                    scores = jnp.where(allowed, scores, -1e30)
                    peak = jnp.max(scores, axis=0, keepdims=True)
                    expo = jnp.exp(scores - peak)
                    total = jnp.sum(expo, axis=0, keepdims=True)
                    soft = (expo * (1.0 / total)).astype(BF16)
                    logs[p, head : head + 1, b * block : upto] = peak + jnp.log(total)
                    turned[head * HEAD_DIM : (head + 1) * HEAD_DIM, b * block : upto] = dot_nn(
                        v_head[:, :upto], soft
                    )
            attended[:, at] = turned[...].T.astype(BF16)

    pairs = width // PAIR
    logs[...] = jnp.zeros(logs.shape, F32)
    attend(0, pairs // 4)
    for m in range(1, count // 2):
        g_gate.arrived(m)
    attend(pairs // 4, pairs // 2)
    for m in range(count // 2, count):
        g_gate.arrived(m)
    g_down.begin()
    attend(pairs // 2, 3 * pairs // 4)
    for m in range(1, count // 2):
        g_up.arrived(m)
    attend(3 * pairs // 4, pairs)
    for m in range(count // 2, count):
        g_up.arrived(m)

    share(attended, attended2)

    @pl.loop(0, rows // block)
    def _(i):
        at = pl.ds(pl.multiple_of(i * block, block), block)
        x = tokens[at, :].astype(F32) + dot_nn(attended[at, :], w_out[...])
        after[at, :] = x
        scale = lax.rsqrt(jnp.mean(x * x, axis=-1, keepdims=True) + norm_eps)
        low_up[at, 0:width] = (x * scale * gains[1:2, :]).astype(BF16)

    put(after, out_after)
    hidden_two = low_up.at[:, pl.ds(0, width)]
    second = share(hidden_two, hidden_two2)
    second_put = writes[-1]
    g_gate.local.wait()
    g_gate.complete()
    put(w_gate, full_gate)

    @pl.loop(0, rows // block)
    def _(i):
        at = pl.ds(pl.multiple_of(i * block, block), block)
        gate_pre[at, :] = dot_nn(low_up[at, 0:width], w_gate[...])
        low_gate[at, :] = gate_pre[at, :].astype(BF16)

    put(low_gate, out_gate)
    g_up.local.wait()
    g_up.complete()
    put(w_up, full_up)
    for m in range(1, count // 2):
        g_down.arrived(m)
    second.wait_send()
    second_put.wait()

    @pl.loop(0, rows // block)
    def _(i):
        at = pl.ds(pl.multiple_of(i * block, block), block)
        up_proj = dot_nn(low_up[at, 0:width], w_up[...])
        gate_of = gate_pre[at, :]
        product2[at, :] = (gate_of * jax.nn.sigmoid(gate_of) * up_proj).astype(BF16)
        low_up[at, :] = up_proj.astype(BF16)

    put(low_up, out_up)
    own_product = product2.at[pl.ds(0, rows), :]
    put(own_product, out_product)
    product_swap = swap(own_product, product2.at[pl.ds(rows, rows), :])
    for m in range(count // 2, count):
        g_down.arrived(m)
    cot_own.wait()
    cot_swap.wait_recv()
    product_swap.wait_recv()

    @pl.loop(0, ff // TILE)
    def _(i):
        at = pl.ds(pl.multiple_of(i * TILE, TILE), TILE)
        grad_low[at, :] = dot_tn(product2[:, at], cot2[...]).astype(BF16)

    put(grad_low, grad_down)
    g_down.local.wait()
    g_down.complete()
    for gather in gathers:
        gather.drain()
    for copy in gain_copies:
        copy.wait_send()
    for copy in swaps:
        if copy is not cot_swap and copy is not product_swap:
            copy.wait_recv()
        if copy is not second:
            copy.wait_send()
    for copy in writes:
        if copy is not second_put:
            copy.wait()


def forward_kernel(lay, lengths, tokens, first, tables, gain_in, cotangent, w_qkv, w_out, w_gate, w_up, w_down):
    count = lay.fs
    rows, width = tokens.shape
    n, ff = w_qkv.shape[1], w_gate.shape[1]
    half = width // 2
    pairs = width // PAIR
    big = struct((rows, width), BF16)
    wide = struct((rows, ff), BF16)
    two = struct((2 * rows, width), BF16)
    dma = pltpu.SemaphoreType.DMA
    vmem = pl.BlockSpec(memory_space=pltpu.VMEM)
    weights = [(width, n), (width, width), (width, ff), (width, ff), (ff, width)]
    out_shape = (
        [struct(shape, BF16) for shape in weights]
        + [big, big, big, struct((pairs, 8, rows), F32)]
        + [two, two, two, struct((rows, width), F32), wide, wide, wide]
        + [struct((ff, half), BF16), struct((8, width), F32), struct((8, width), F32)]
    )
    out_specs = [ANY] * 8 + [vmem] + [ANY] * 8 + [vmem, vmem]
    return pl.pallas_call(
        functools.partial(forward_body, lay),
        in_specs=[pl.BlockSpec(memory_space=pltpu.SMEM)] + [vmem] * 4 + [vmem] + [ANY] * 6,
        out_specs=out_specs,
        out_shape=out_shape,
        scratch_shapes=[
            pltpu.VMEM((width, n), BF16),
            pltpu.VMEM((width, width), BF16),
            pltpu.VMEM((width, ff), BF16),
            pltpu.VMEM((width, ff), BF16),
            pltpu.VMEM((GAIN_ROWS, width), BF16),
            pltpu.VMEM((rows, width), BF16),
            pltpu.VMEM((rows, width), BF16),
            pltpu.VMEM((rows, width), BF16),
            pltpu.VMEM((rows, width), BF16),
            pltpu.VMEM((rows, width), BF16),
            pltpu.VMEM((rows, width), F32),
            pltpu.VMEM((rows, ff), F32),
            pltpu.VMEM((rows, ff), BF16),
            pltpu.VMEM((rows, ff), BF16),
            pltpu.VMEM((2 * rows, ff), BF16),
            pltpu.VMEM((2 * rows, half), BF16),
            pltpu.VMEM((ff, half), BF16),
            pltpu.VMEM((PAIR, rows), F32),
            dma((5 * count,)),
            dma((5 * count,)),
            dma((5 * count,)),
            dma((5 * count,)),
            dma((7,)),
            dma((count - 1,)),
            dma((count - 1,)),
            dma((5,)),
            dma((5,)),
            dma((16,)),
        ],
        compiler_params=pltpu.CompilerParams(
            collective_id=0, has_side_effects=True, vmem_limit_bytes=62 * 2**20
        ),
        cost_estimate=pl.CostEstimate(
            flops=2 * rows * width * (n + width + 3 * ff),
            bytes_accessed=60 * 2**20,
            transcendentals=0,
        ),
        name="forward",
    )(lengths, tokens, first, *tables, gain_in, cotangent, w_qkv, w_out, w_gate, w_up, w_down)


def rms_back(grad, normed, inverse):
    return inverse * (grad - normed * jnp.mean(grad * normed, axis=-1, keepdims=True))


class Line:
    def __init__(self, lay, place):
        size = lay.line
        r = place.d // 2
        self.half = size // 2
        upper = r // self.half
        toward = 1 - 2 * upper
        self.depth = r * toward + upper * (size - 1)
        self.next = (place.d + 2 * toward, place.f)
        self.prev = (place.d - 2 * toward, place.f)
        self.middle = self.depth == self.half - 1
        self.inner = self.depth > 0
        self.others = []
        reach = 1
        while reach < size:
            self.others.append((place.d + 2 * reach * (1 - 2 * lax.rem(r // reach, 2)), place.f))
            reach *= 2


def signal(sem, device):
    pl.semaphore_signal(sem, inc=1, device_id=device, device_id_type=pl.DeviceIdType.MESH)


class Reduce:
    def __init__(self, place, line, slot, held, sources, first, later, final, column, sems):
        send, recv, z_send, z_recv, credit, f_local, f_send, f_recv = sems
        self.place, self.line, self.held, self.first = place, line, held, first
        self.bits, count = place.bits, place.count
        self.count = count
        base = slot * count
        half = count // 2
        self.steps, self.lands = [], []
        at = 0
        for i in range(self.bits):
            blocks = count >> (i + 1)
            copies, lands = [], []
            for q in range(blocks):
                source = sources[q] if i == 0 else held.at[blocks + q]
                land = first.at[q] if i == 0 else later.at[at + q]
                index = base + q if i == 0 else base + half + at + q
                lands.append(land)
                copies.append(remote(source, land, send.at[index], recv.at[index], place.partner(i)))
            if i > 0:
                at += blocks
            self.steps.append(copies)
            self.lands.append(lands)
        mine = held.at[0]
        self.total_in, self.total_out = first.at[0], first.at[1]
        self.to_in = remote(mine, first.at[0], z_send.at[2 * slot], z_recv.at[2 * slot], line.next)
        self.to_middle = remote(
            mine, first.at[1], z_send.at[2 * slot], z_recv.at[2 * slot + 1], line.next
        )
        self.back_middle = remote(
            first.at[0], first.at[1], z_send.at[2 * slot + 1], z_recv.at[2 * slot + 1], line.prev
        )
        self.back_out = remote(
            first.at[1], first.at[1], z_send.at[2 * slot + 1], z_recv.at[2 * slot + 1], line.prev
        )
        self.from_next, self.from_prev = credit.at[2 * slot], credit.at[2 * slot + 1]
        spot = final.at[:, column]
        self.ends = []
        for source in (self.total_in, self.total_out):
            self.ends.append(
                (
                    pltpu.make_async_copy(source, spot, f_local.at[slot]),
                    remote(source, spot, f_send.at[slot], f_recv.at[slot], place.sibling()),
                )
            )

    def begin(self, q):
        self.steps[0][q].start()

    def take(self, i):
        blocks = self.count >> (i + 1)
        for q in reversed(range(blocks)):
            self.steps[i][q].wait_recv()
            self.held[q] = add_low(self.held[q], self.lands[i][q][...])
            if i + 1 < self.bits and q >= blocks // 2:
                self.steps[i + 1][q - blocks // 2].start()
        line = self.line
        if i == 0:

            @pl.when(line.middle)
            def _():
                signal(self.from_next, line.next)

            @pl.when(jnp.logical_not(line.middle))
            def _():
                signal(self.from_prev, line.next)

            @pl.when(line.inner)
            def _():
                signal(self.from_next, line.prev)

        if i == self.bits - 1:

            @pl.when(jnp.logical_not(line.inner))
            def _():
                self.onward()

    def onward(self):
        line = self.line
        pl.semaphore_wait(self.from_next, 1)

        @pl.when(line.middle)
        def _():
            self.to_middle.start()

        @pl.when(jnp.logical_not(line.middle))
        def _():
            self.to_in.start()

    def inward(self):
        @pl.when(self.line.inner)
        def _():
            self.to_in.wait_recv()
            self.held[0] = add_low(self.held[0], self.total_in[...])
            self.onward()

    def finish(self, which):
        local, cross = self.ends[which]
        local.start()
        cross.start()

    def across(self):
        line = self.line

        @pl.when(line.middle)
        def _():
            self.to_middle.wait_recv()
            self.total_in[...] = add_low(self.held[0], self.total_out[...])

            @pl.when(line.inner)
            def _():
                pl.semaphore_wait(self.from_prev, 1)
                self.back_middle.start()

            self.finish(0)

    def outward(self):
        line = self.line
        if line.half == 1:
            return

        @pl.when(jnp.logical_not(line.middle))
        def _():
            self.back_out.wait_recv()

            @pl.when(line.inner)
            def _():
                pl.semaphore_wait(self.from_prev, 1)
                self.back_out.start()

            self.finish(1)

    def drain(self):
        line = self.line
        for copies in self.steps:
            for copy in copies:
                copy.wait_send()
        self.to_in.wait_send()

        @pl.when(line.inner)
        def _():
            self.back_out.wait_send()

        local, cross = self.ends[0]
        local.wait()
        cross.wait_send()
        cross.wait_recv()


def backward_body(
    lay,
    lengths,
    cosine,
    sine,
    gains,
    sums,
    logs,
    full_qkv,
    full_out,
    full_gate,
    full_up,
    full_down,
    in_q,
    in_k,
    in_v,
    hidden_one2,
    attended2,
    hidden_two2,
    in_after,
    in_gate,
    in_up,
    in_product,
    in_grad_down,
    tokens,
    cotangent,
    output,
    grad_tokens,
    grad_first,
    sum_qkv,
    sum_out,
    sum_gate,
    sum_up,
    sum_down,
    small,
    gate,
    up,
    product,
    ring,
    w_out,
    one,
    two,
    three,
    cot,
    left,
    right,
    low,
    attend_grad,
    gate_sib,
    up_sib,
    low_sib,
    q_sib,
    k_sib,
    v_sib,
    held_down,
    held_gate,
    held_up,
    held_narrow,
    first_down,
    first_gate,
    first_up,
    first_narrow,
    later_down,
    later_gate,
    later_up,
    later_narrow,
    small_land,
    turned,
    load_sem,
    ring_sem,
    swap_send,
    swap_recv,
    write_sem,
    send,
    recv,
    z_send,
    z_recv,
    credit,
    f_local,
    f_send,
    f_recv,
    small_send,
    small_recv,
):
    place = Place(lay)
    line = Line(lay, place)
    count, c = place.count, place.c
    sibling = place.sibling()
    rows, width = cot.shape
    ff = gate.shape[1]
    side, narrow = ff // 2, width // 2
    block = min(TILE, rows)
    bits = place.bits

    barrier = pltpu.get_barrier_semaphore()
    partners = [place.partner(i) for i in range(bits)]
    known = [sibling] + partners + line.others + [line.next]
    for device in known:
        signal(barrier, device)

    @pl.when(line.inner)
    def _():
        signal(barrier, line.prev)
        pl.semaphore_wait(barrier, len(known) + 1)

    @pl.when(jnp.logical_not(line.inner))
    def _():
        pl.semaphore_wait(barrier, len(known))

    loads = {}

    def load(name, source, target):
        copy = pltpu.make_async_copy(source, target, load_sem.at[len(loads)])
        copy.start()
        loads[name] = copy

    writes = []

    def put(source, target):
        copy = pltpu.make_async_copy(source, target, write_sem.at[len(writes)])
        copy.start()
        writes.append(copy)
        return copy

    swaps = []

    def swap(source, target):
        slot = len(swaps)
        copy = remote(source, target, swap_send.at[slot], swap_recv.at[slot], sibling)
        copy.start()
        swaps.append(copy)
        return copy

    def shard_of(p):
        m = sum(((p >> i) & 1) << (bits - 1 - i) for i in range(bits))
        return place.shard(m)

    sems = (send, recv, z_send, z_recv, credit, f_local, f_send, f_recv)
    half = count // 2
    down_rows = in_grad_down.shape[0] // count
    shard_rows = sum_qkv.shape[0]

    def down_block(p):
        at = pl.multiple_of(shard_of(p) * down_rows, down_rows)
        return in_grad_down.at[pl.ds(at, down_rows), :]

    def columns(offset, size):
        return pl.ds(pl.multiple_of(offset + c * size, 128), size)

    def reduce_of(slot, held, first, later, final, offset, size):
        sources = [held.at[half + q] for q in range(half)]
        return Reduce(place, line, slot, held, sources, first, later, final, columns(offset, size), sems)

    r_down = Reduce(
        place,
        line,
        0,
        held_down,
        [down_block(half + q) for q in range(half)],
        first_down,
        later_down,
        sum_down,
        columns(0, narrow),
        sems,
    )
    r_gate = reduce_of(1, held_gate, first_gate, later_gate, sum_gate, 0, side)
    r_up = reduce_of(2, held_up, first_up, later_up, sum_up, 0, side)

    def narrow_of(index, slot, final, offset):
        at = index * count
        return reduce_of(
            slot,
            held_narrow.at[pl.ds(at, count)],
            first_narrow.at[pl.ds(index * half, half)],
            later_narrow.at[pl.ds(index * (half - 1), half - 1)],
            final,
            offset,
            narrow,
        )

    r_out = narrow_of(0, 3, sum_out, 0)
    r_v = narrow_of(1, 4, sum_qkv, 2 * width)
    r_k = narrow_of(2, 5, sum_qkv, width)
    r_q = narrow_of(3, 6, sum_qkv, 0)
    reduces = [r_down, r_gate, r_up, r_out, r_v, r_k, r_q]

    for q in range(half):
        r_down.begin(q)

    tile = min(TILE, side)
    whole_tiles, rest = side // tile, side % tile

    def ring_copy(row, slot, size):
        return pltpu.make_async_copy(
            full_down.at[pl.ds(row, size), :],
            ring.at[slot, pl.ds(0, size), pl.ds(0, width)],
            ring_sem.at[slot],
        )

    theirs = pl.multiple_of((1 - c) * side, 128)
    ours = pl.multiple_of(c * side, 128)
    ring_copy(theirs, 0, tile).start()
    load("gate", in_gate, gate)
    load("up", in_up, up)
    load("cot", cotangent, cot)
    load("product", in_product, product)
    load("after", in_after, one)
    load("left", hidden_two2, left)
    for q in range(half):
        load("down%d" % q, down_block(q), held_down.at[q])
    load("out", full_out, w_out)
    load("right", attended2, right)
    for name in ("gate", "up", "cot", "product", "after"):
        loads[name].wait()
    two[...] = one[...]

    def down_tile(at, slot, size):
        rows_of = ring[slot, 0:size, 0:width]
        grad_product = dot_nt(cot[...], rows_of)
        gate_pre = gate[:, pl.ds(at, size)].astype(F32)
        up_proj = up[:, pl.ds(at, size)].astype(F32)
        sigma = jax.nn.sigmoid(gate_pre)
        gate[:, pl.ds(at, size)] = (
            grad_product * up_proj * sigma * (1.0 + gate_pre * (1.0 - sigma))
        ).astype(BF16)
        up[:, pl.ds(at, size)] = (grad_product * (gate_pre * sigma)).astype(BF16)
        two[...] += dot_nn(product[:, pl.ds(at, size)], rows_of)

    def half_down(base, following):
        @pl.loop(0, whole_tiles)
        def _(t):
            slot = lax.rem(t, 2)
            at = pl.multiple_of(base + t * tile, 128)
            ring_copy(at, slot, tile).wait()

            @pl.when(t + 1 < whole_tiles)
            def _():
                ring_copy(pl.multiple_of(at + tile, 128), 1 - slot, tile).start()

            if rest:

                @pl.when(t + 1 == whole_tiles)
                def _():
                    ring_copy(pl.multiple_of(at + tile, 128), 2, rest).start()

            down_tile(at, slot, tile)

        if following is not None:
            ring_copy(following, 0, tile).start()
        if rest:
            at = pl.multiple_of(base + whole_tiles * tile, 128)
            ring_copy(at, 2, rest).wait()
            down_tile(at, 2, rest)

    half_down(theirs, ours)
    gate_swap = swap(gate.at[:, pl.ds(theirs, side)], gate_sib)
    up_swap = swap(up.at[:, pl.ds(theirs, side)], up_sib)
    half_down(ours, None)
    low[...] = two[...].astype(BF16)
    output_put = put(low, output)
    load("q", in_q, product.at[:, pl.ds(0, width)])
    load("k", in_k, product.at[:, pl.ds(width, width)])

    def tile_copies(i):
        at = pl.ds(i * block_w, block_w)
        return (
            pltpu.make_async_copy(
                full_gate.at[at, :], ring.at[i % 2, :, pl.ds(0, ff)], ring_sem.at[i % 2]
            ),
            pltpu.make_async_copy(
                full_up.at[at, :], ring.at[2 + i % 2, :, pl.ds(0, ff)], ring_sem.at[2 + i % 2]
            ),
        )

    block_w = min(TILE, width)
    start(tile_copies(0))
    start(tile_copies(1))
    loads["left"].wait()

    def grad_block(held, p, both, own, other):
        at = pl.ds(pl.multiple_of(shard_of(p) * shard_rows, 128), shard_rows)
        held[p] = (
            dot_tn(both[0:rows, at], own) + dot_tn(both[rows : 2 * rows, at], other)
        ).astype(BF16)

    def grad_of(reduce, both, own, other):
        for p in list(range(half, count)) + list(range(half)):
            grad_block(reduce.held, p, both, own(), other())
            if p >= half:
                reduce.begin(p - half)

    gate_swap.wait_recv()
    grad_of(r_gate, left, lambda: gate[:, pl.ds(ours, side)], lambda: gate_sib[...])
    up_swap.wait_recv()
    grad_of(r_up, left, lambda: up[:, pl.ds(ours, side)], lambda: up_sib[...])
    for q in range(half):
        loads["down%d" % q].wait()
    load("one", hidden_one2, left)
    tiles = width // block_w

    def back_tile(i):
        wait(tile_copies(i))
        at = slice(i * block_w, (i + 1) * block_w)
        two[:, at] = dot_nt(gate[...], ring[i % 2, :, 0:ff]) + dot_nt(up[...], ring[2 + i % 2, :, 0:ff])
        if i + 2 < tiles:
            start(tile_copies(i + 2))

    r_down.take(0)
    for i in range(tiles // 2):
        back_tile(i)
    for i in range(1, bits):
        r_down.take(i)
    for i in range(tiles // 2, tiles):
        back_tile(i)
    output_put.wait()
    small[...] = jnp.zeros(small.shape, F32)
    small[2:4, :] = sums[0:2, :]

    @pl.loop(0, rows // block)
    def _(i):
        at = pl.ds(pl.multiple_of(i * block, block), block)
        x = one[at, :]
        inverse = lax.rsqrt(jnp.mean(x * x, axis=-1, keepdims=True) + norm_eps)
        normed = x * inverse
        grad_hidden = two[at, :]
        small[1:2, :] += jnp.sum(grad_hidden * normed, axis=0, keepdims=True)
        result = cot[at, :].astype(F32) + rms_back(grad_hidden * gains[1:2, :], normed, inverse)
        three[at, :] = result
        low[at, :] = result.astype(BF16)

    theirs_narrow = pl.multiple_of((1 - c) * narrow, 128)
    ours_narrow = pl.multiple_of(c * narrow, 128)
    low_swap = swap(low.at[:, pl.ds(theirs_narrow, narrow)], low_sib)
    gate_swap.wait_send()
    up_swap.wait_send()
    load("v", in_v, up.at[:, pl.ds(width, width)])
    load("tokens", tokens, cot)
    loads["out"].wait()

    @pl.loop(0, rows // block)
    def _(i):
        at = pl.ds(pl.multiple_of(i * block, block), block)
        attend_grad[at, :] = dot_nt(low[at, :], w_out[...]).astype(BF16)

    def qkv_copy(i):
        return pltpu.make_async_copy(
            full_qkv.at[pl.ds(i * block_w, block_w), :], ring.at[i % 4], ring_sem.at[i % 4]
        )

    for i in range(min(4, tiles)):
        qkv_copy(i).start()
    loads["right"].wait()
    low_swap.wait_recv()
    grad_of(r_out, right, lambda: low[:, pl.ds(ours_narrow, narrow)], lambda: low_sib[...])
    r_gate.take(0)
    for name in ("q", "k", "v"):
        loads[name].wait()
    length = lengths[0]
    pairs = width // PAIR
    q_grad, k_grad = gate.at[:, pl.ds(0, width)], gate.at[:, pl.ds(width, width)]
    v_grad = up.at[:, pl.ds(0, width)]

    def attend_back(base, begin, end):
        @pl.loop(begin, end)
        def _(i):
            p = base + i
            at = pl.ds(pl.multiple_of(p * PAIR, PAIR), PAIR)
            shift = pl.ds(pl.multiple_of(width + p * PAIR, PAIR), PAIR)
            q, k, v, g = product[:, at], product[:, shift], up[:, shift], attend_grad[:, at]
            lane = lax.broadcasted_iota(jnp.int32, (rows, PAIR), 1)
            k_t = k.T
            sums_k, sums_v = [], []
            for head in range(2):
                inside = (lane // HEAD_DIM) == head
                k_head = jnp.where(inside, k, jnp.zeros_like(k))
                v_head = jnp.where(inside, v, jnp.zeros_like(v))
                k_turned = k_t[head * HEAD_DIM : (head + 1) * HEAD_DIM]
                parts_k, parts_v = [], []
                for b in range(rows // block):
                    upto = (b + 1) * block
                    q_block, g_block = q[b * block : upto], g[b * block : upto]
                    scores = dot_nt(k_head[:upto], q_block)
                    key = lax.broadcasted_iota(jnp.int32, scores.shape, 0)
                    query = lax.broadcasted_iota(jnp.int32, (1, block), 1) + b * block
                    log_total = logs[p, head : head + 1, b * block : upto]
                    allowed = key <= jnp.minimum(query, length - 1)
                    soft = jnp.where(allowed, jnp.exp(scores - log_total), 0.0)
                    grad_soft = dot_nt(v_head[:upto], g_block)
                    inner = jnp.sum(soft * grad_soft, axis=0, keepdims=True)
                    grad_scores = (soft * (grad_soft - inner)).astype(BF16)
                    turned[head * HEAD_DIM : (head + 1) * HEAD_DIM, b * block : upto] = dot_nn(
                        k_turned[:, :upto], grad_scores
                    )
                    parts_k.append(dot_nn(grad_scores, q_block))
                    parts_v.append(dot_nn(soft.astype(BF16), g_block))
                for parts, gathered in ((parts_k, sums_k), (parts_v, sums_v)):
                    rows_of = []
                    for r in range(rows // block):
                        piece = parts[r][r * block : (r + 1) * block]
                        for later in parts[r + 1 :]:
                            piece = piece + later[r * block : (r + 1) * block]
                        rows_of.append(piece)
                    gathered.append(jnp.concatenate(rows_of, axis=0))
            first_head = lane < HEAD_DIM
            cos, sin = cosine[...], sine[...]

            def back(x):
                return (x * cos - swap_halves(x) * sin).astype(BF16)

            gate[:, at] = back(turned[...].T * HEAD_DIM**-0.5)
            gate[:, shift] = back(jnp.where(first_head, sums_k[0], sums_k[1]))
            half_v = 0.5 * jnp.where(first_head, sums_v[0], sums_v[1])
            two[:, at] = half_v
            up[:, at] = half_v.astype(BF16)

    their_pairs, our_pairs = (1 - c) * (pairs // 2), c * (pairs // 2)
    attend_back(their_pairs, 0, pairs // 4)
    r_up.take(0)
    r_down.inward()
    attend_back(their_pairs, pairs // 4, pairs // 2)
    v_swap = swap(v_grad.at[:, pl.ds(theirs_narrow, narrow)], v_sib)
    k_swap = swap(k_grad.at[:, pl.ds(theirs_narrow, narrow)], k_sib)
    q_swap = swap(q_grad.at[:, pl.ds(theirs_narrow, narrow)], q_sib)
    for i in range(1, bits):
        r_gate.take(i)
    r_down.across()
    attend_back(our_pairs, 0, pairs // 4)
    for i in range(1, bits):
        r_up.take(i)
    r_out.take(0)
    r_gate.inward()
    attend_back(our_pairs, pairs // 4, pairs // 2)
    put(two, grad_first)
    r_down.outward()
    loads["one"].wait()

    def ours_of(ref, offset):
        at = pl.ds(pl.multiple_of(offset + c * narrow, 128), narrow)
        return lambda: ref[:, at]

    v_swap.wait_recv()
    grad_of(r_v, left, ours_of(up, 0), lambda: v_sib[...])
    k_swap.wait_recv()
    grad_of(r_k, left, ours_of(gate, width), lambda: k_sib[...])
    q_swap.wait_recv()
    grad_of(r_q, left, ours_of(gate, 0), lambda: q_sib[...])
    for i in range(1, bits):
        r_out.take(i)
    r_gate.across()
    r_up.inward()
    for i in range(tiles):
        qkv_copy(i).wait()
        slot = i % 4
        one[:, i * block_w : (i + 1) * block_w] = (
            dot_nt(gate[:, 0:width], ring[slot, :, 0:width])
            + dot_nt(gate[:, width : 2 * width], ring[slot, :, width : 2 * width])
            + dot_nt(up[:, 0:width], ring[slot, :, 2 * width : 3 * width])
        )
        if i + 4 < tiles:
            qkv_copy(i + 4).start()
    r_v.take(0)
    r_up.across()
    loads["tokens"].wait()

    @pl.loop(0, rows // block)
    def _(i):
        at = pl.ds(pl.multiple_of(i * block, block), block)
        x = cot[at, :].astype(F32)
        inverse = lax.rsqrt(jnp.mean(x * x, axis=-1, keepdims=True) + norm_eps)
        normed = x * inverse
        grad_hidden = one[at, :]
        small[0:1, :] += jnp.sum(grad_hidden * normed, axis=0, keepdims=True)
        three[at, :] += rms_back(grad_hidden * gains[0:1, :], normed, inverse)

    put(three, grad_tokens)
    smalls = []

    def small_step():
        slot = len(smalls)
        device = ([sibling] + partners + line.others)[slot]
        copy = remote(
            small_land.at[2 * slot],
            small_land.at[2 * slot + 1],
            small_send.at[slot],
            small_recv.at[slot],
            device,
        )
        small_land[2 * slot] = small[...]
        copy.start()
        smalls.append(copy)

    def small_take():
        smalls[-1].wait_recv()
        small[...] += small_land[2 * len(smalls) - 1]

    small_count = 1 + bits + len(line.others)
    small_step()
    r_gate.outward()
    r_k.take(0)
    for i in range(1, bits):
        r_v.take(i)
    small_take()
    small_step()
    r_out.inward()
    r_q.take(0)
    for i in range(1, bits):
        r_k.take(i)
    small_take()
    small_step()
    for i in range(1, bits):
        r_q.take(i)
    r_out.across()
    r_up.outward()
    r_v.inward()
    small_take()
    small_step()
    r_out.outward()
    r_k.inward()
    r_v.across()
    while len(smalls) < small_count:
        small_take()
        small_step()
    r_q.inward()
    r_k.across()
    r_v.outward()
    small_take()
    r_q.across()
    r_k.outward()
    r_q.outward()

    for reduce in reduces:
        reduce.drain()
    for copy in smalls:
        copy.wait_send()
    for copy in swaps:
        if copy is not gate_swap and copy is not up_swap:
            copy.wait_send()
    for copy in writes:
        if copy is not output_put:
            copy.wait()


def backward_kernel(lay, lengths, tables, gains, sums, logs, weights, saved, tokens, cotangent):
    count = lay.fs
    half = count // 2
    rows, width = tokens.shape
    n, ff = weights[0].shape[1], weights[2].shape[1]
    shard, down = width // count, ff // count
    side, narrow = ff // 2, width // 2
    dma = pltpu.SemaphoreType.DMA
    vmem = pl.BlockSpec(memory_space=pltpu.VMEM)
    tall = pltpu.VMEM((rows, ff), BF16)
    flat = pltpu.VMEM((rows, width), BF16)
    full = pltpu.VMEM((rows, width), F32)
    small_steps = 1 + lay.bits + (lay.line.bit_length() - 1)
    operands = (lengths, *tables, gains, sums, logs, *weights, *saved, tokens, cotangent)
    return pl.pallas_call(
        functools.partial(backward_body, lay),
        in_specs=[pl.BlockSpec(memory_space=pltpu.SMEM)]
        + [vmem] * 5
        + [ANY] * (len(operands) - 6),
        out_specs=[ANY] * 8 + [vmem],
        out_shape=[
            struct((rows, width), BF16),
            struct((rows, width), F32),
            struct((rows, width), F32),
            struct((shard, n), BF16),
            struct((shard, width), BF16),
            struct((shard, ff), BF16),
            struct((shard, ff), BF16),
            struct((down, width), BF16),
            struct((8, width), F32),
        ],
        scratch_shapes=[
            tall,
            tall,
            tall,
            pltpu.VMEM((4, min(TILE, width), n), BF16),
            pltpu.VMEM((width, width), BF16),
            full,
            full,
            full,
            flat,
            pltpu.VMEM((2 * rows, width), BF16),
            pltpu.VMEM((2 * rows, width), BF16),
            flat,
            flat,
            pltpu.VMEM((rows, side), BF16),
            pltpu.VMEM((rows, side), BF16),
            pltpu.VMEM((rows, narrow), BF16),
            pltpu.VMEM((rows, narrow), BF16),
            pltpu.VMEM((rows, narrow), BF16),
            pltpu.VMEM((rows, narrow), BF16),
            pltpu.VMEM((half, down, narrow), BF16),
            pltpu.VMEM((count, shard, side), BF16),
            pltpu.VMEM((count, shard, side), BF16),
            pltpu.VMEM((4 * count, shard, narrow), BF16),
            pltpu.VMEM((half, down, narrow), BF16),
            pltpu.VMEM((half, shard, side), BF16),
            pltpu.VMEM((half, shard, side), BF16),
            pltpu.VMEM((4 * half, shard, narrow), BF16),
            pltpu.VMEM((half - 1, down, narrow), BF16),
            pltpu.VMEM((half - 1, shard, side), BF16),
            pltpu.VMEM((half - 1, shard, side), BF16),
            pltpu.VMEM((4 * (half - 1), shard, narrow), BF16),
            pltpu.VMEM((2 * small_steps, 8, width), F32),
            pltpu.VMEM((PAIR, rows), F32),
            dma((14 + half,)),
            dma((4,)),
            dma((6,)),
            dma((6,)),
            dma((3,)),
            dma((7 * count,)),
            dma((7 * count,)),
            dma((14,)),
            dma((14,)),
            pltpu.SemaphoreType.REGULAR((14,)),
            dma((7,)),
            dma((7,)),
            dma((7,)),
            dma((small_steps,)),
            dma((small_steps,)),
        ],
        compiler_params=pltpu.CompilerParams(
            collective_id=1, has_side_effects=True, vmem_limit_bytes=63 * 2**20
        ),
        cost_estimate=pl.CostEstimate(
            flops=4 * rows * width * (n + width + 3 * ff),
            bytes_accessed=80 * 2**20,
            transcendentals=0,
        ),
        name="backward",
    )(*operands)


def body(
    lay,
    tokens,
    first_values,
    lengths,
    gain_one,
    w_qkv,
    w_out,
    gain_two,
    w_gate,
    w_up,
    w_down,
    cotangent,
):
    rows, width = tokens.shape
    shard_rows = w_qkv.shape[0]
    tables = tuple(jnp.asarray(table) for table in rotary_tables(rows))
    gain_block = jnp.pad(jnp.stack([gain_one, gain_two]), ((0, GAIN_ROWS - 2), (0, 0)))
    results = forward_kernel(
        lay, lengths, tokens, first_values, tables, gain_block, cotangent, w_qkv, w_out, w_gate, w_up, w_down
    )
    weights, heads, logs, saved, gains, sums = (
        results[:5],
        results[5:8],
        results[8],
        results[9:17],
        results[17],
        results[18],
    )
    output, grad_tokens, grad_first, *totals, small = backward_kernel(
        lay, lengths, tables, gains, sums, logs, weights, (*heads, *saved), tokens, cotangent
    )
    shard_qkv, shard_out, shard_gate, shard_up, shard_down = (item.astype(F32) for item in totals)
    at = lax.axis_index("fsdp") * shard_rows
    entry_count = rows * width * lay.dp * lay.fs
    shard_gains = lax.dynamic_slice(small, (0, at), (2, shard_rows))
    norms = jnp.sum(small[2:4], axis=1) / entry_count
    return (
        output,
        grad_tokens,
        grad_first,
        shard_gains[0],
        shard_qkv,
        shard_out,
        shard_gains[1],
        shard_gate,
        shard_up,
        shard_down,
        norms[0],
        norms[1],
    )


def solution(mesh):
    both = P(AXES, None)
    rows = P("fsdp", None)
    in_specs = (both, both, P(AXES), P("fsdp"), rows, rows, P("fsdp"), rows, rows, rows, both)
    out_specs = (both, both, both, P("fsdp"), rows, rows, P("fsdp"), rows, rows, rows, P(), P())
    lay = Layout(mesh.shape["dp"], mesh.shape["fsdp"])
    return jax.shard_map(
        functools.partial(body, lay),
        mesh=mesh,
        in_specs=in_specs,
        out_specs=out_specs,
        check_vma=False,
    )
```

```python
import functools
import math

import jax
import jax.numpy as jnp
import numpy as np
from jax import lax
from jax.experimental import pallas as pl
from jax.experimental.pallas import tpu as pltpu
from jax.sharding import PartitionSpec as P

HEAD_DIM = 64
PAIR = 2 * HEAD_DIM
TILE = 256
GAIN_ROWS = 16
norm_eps = 1e-06
F32 = jnp.float32
BF16 = jnp.bfloat16
AXES = ("dp", "fsdp")
ANY = pl.BlockSpec(memory_space=pl.ANY)


def dot_nn(a, b):
    return lax.dot_general(a, b, (((1,), (0,)), ((), ())), preferred_element_type=F32)


def dot_nt(a, b):
    return lax.dot_general(a, b, (((1,), (1,)), ((), ())), preferred_element_type=F32)


def dot_tn(a, b):
    return lax.dot_general(a, b, (((0,), (0,)), ((), ())), preferred_element_type=F32)


def rotary_tables(count):
    half = HEAD_DIM // 2
    frequency = np.exp(
        -(np.arange(half, dtype=np.float32) * np.float32(2.0) / np.float32(HEAD_DIM))
        * np.float32(math.log(10000.0))
    ).astype(np.float32)
    angles = np.arange(count, dtype=np.float32)[:, None] * frequency[None, :]
    cosine = np.cos(angles.astype(np.float64)).astype(np.float32)
    sine = np.sin(angles.astype(np.float64)).astype(np.float32)
    cosine = np.concatenate([cosine] * 4, axis=1)
    sine = np.concatenate([-sine, sine, -sine, sine], axis=1)
    return cosine, sine


def swap_halves(x):
    half = HEAD_DIM // 2
    lane = lax.broadcasted_iota(jnp.int32, x.shape, 1)
    up = pltpu.roll(x, PAIR - half, 1)
    down = pltpu.roll(x, half, 1)
    return jnp.where((lane % HEAD_DIM) < half, up, down)


class Layout:
    def __init__(self, dp, fs):
        self.dp, self.fs = dp, fs
        self.bits = fs.bit_length() - 1
        self.line = dp // 2


def add_low(a, b):
    return (a.astype(F32) + b.astype(F32)).astype(BF16)


def start(copies):
    for copy in copies:
        copy.start()


def wait(copies):
    for copy in copies:
        copy.wait()


def struct(shape, dtype):
    return jax.ShapeDtypeStruct(shape, dtype)


class Place:
    def __init__(self, lay):
        self.bits, self.count = lay.bits, lay.fs
        self.d, self.f = lax.axis_index("dp"), lax.axis_index("fsdp")
        self.c = lax.rem(self.d, 2)
        self.flips = []
        for i in range(self.bits):
            ahead, back = 1 << i, 1 << (self.bits - 1 - i)
            one = ahead * (1 - 2 * lax.rem(self.f // ahead, 2))
            two = back * (1 - 2 * lax.rem(self.f // back, 2))
            self.flips.append(one + self.c * (two - one))

    def shard(self, m):
        return self.f + sum(self.flips[i] for i in range(self.bits) if (m >> i) & 1)

    def partner(self, i):
        return (self.d, self.f + self.flips[i])

    def sibling(self):
        return (self.d + 1 - 2 * self.c, self.f)

    def above(self):
        return (self.d + 2 - 4 * lax.rem(self.d // 2, 2), self.f)

    def group(self):
        others = []
        for m in range(1, self.count):
            others.append((self.d, self.shard(m)))
        return others


def remote(src, dst, send, recv, device):
    return pltpu.make_async_remote_copy(
        src_ref=src,
        dst_ref=dst,
        send_sem=send,
        recv_sem=recv,
        device_id=device,
        device_id_type=pl.DeviceIdType.MESH,
    )


class Gather:
    def __init__(self, place, own, full, first, total, lifted, sems, slot):
        self.place = place
        send, recv, up_send, up_recv, cross_send, cross_recv, more_send, more_recv = sems
        count = place.count
        rows, side = own.shape[0], total // 2
        column = pl.ds(pl.multiple_of(first + place.c * side, 128), side)
        size = rows // 2 if lifted else rows
        parity = lax.rem(place.d // 2, 2) if lifted else 0
        self.link, self.up, self.cross, self.more = [None], [None], [None], [None]

        def spot(piece, which):
            at = pl.multiple_of(place.shard(piece) * rows + which * size, size)
            return full.at[pl.ds(at, size), column]

        for m in range(1, count):
            step = m.bit_length() - 1
            before = m - (1 << step)
            source = spot(before, parity)
            if before == 0:
                source = own.at[pl.ds(pl.multiple_of(parity * size, size), size), column]
            at = slot * count + m
            self.link.append(
                remote(source, spot(before, parity), send.at[at], recv.at[at], place.partner(step))
            )
            here = spot(m, parity)
            self.cross.append(
                remote(here, here, cross_send.at[at], cross_recv.at[at], place.sibling())
            )
            if lifted:
                there = spot(m, 1 - parity)
                self.up.append(remote(here, here, up_send.at[at], up_recv.at[at], place.above()))
                self.more.append(
                    remote(there, there, more_send.at[at], more_recv.at[at], place.sibling())
                )

    def begin(self, m):
        self.link[m].start()

    def arrived(self, m):
        self.link[m].wait_recv()
        for i in range(m.bit_length(), self.place.bits):
            self.link[m + (1 << i)].start()
        self.cross[m].start()

    def lift(self, m):
        self.up[m].start()

    def landed(self, m):
        self.up[m].wait_recv()
        self.more[m].start()

    def complete(self):
        for copy in self.cross[1:] + self.more[1:]:
            copy.wait_recv()

    def drain(self):
        for copy in self.link[1:] + self.cross[1:] + self.up[1:] + self.more[1:]:
            copy.wait_send()


QK, V, OUT, GATE, UP, DOWN = range(6)
BEGIN, ARRIVE, LIFT, LAND = range(4)
NORMALISE, QUERIES, KEYS, VALUES, HEADS, PROJECT, GATES, UPS, SUM_DOWN = range(4, 13)
FORWARD_LIFTED = (QK, V, GATE, DOWN)
FORWARD_ORDER = (
    (BEGIN, QK, 1), (BEGIN, QK, 2), (BEGIN, V, 1), (BEGIN, V, 2), (BEGIN, GATE, 1),
    (NORMALISE, 0, 0), (ARRIVE, QK, 1), (ARRIVE, QK, 2), (LIFT, QK, 1), (LIFT, QK, 2),
    (ARRIVE, V, 1), (BEGIN, GATE, 2), (ARRIVE, V, 2), (ARRIVE, GATE, 1), (BEGIN, OUT, 1),
    (ARRIVE, QK, 3), (LIFT, QK, 3), (LAND, QK, 1), (LIFT, V, 1), (BEGIN, UP, 1), (ARRIVE, V, 3),
    (BEGIN, OUT, 2), (LIFT, V, 2), (LAND, QK, 2), (ARRIVE, OUT, 1), (BEGIN, DOWN, 1), (LIFT, V, 3),
    (LAND, QK, 3), (QUERIES, 0, 0), (ARRIVE, GATE, 2), (LAND, V, 1), (KEYS, 0, 0), (LIFT, GATE, 1),
    (LAND, V, 2), (LIFT, GATE, 2), (ARRIVE, OUT, 2), (LAND, V, 3), (VALUES, 0, 0), (BEGIN, UP, 2),
    (HEADS, 0, 0), (ARRIVE, UP, 1), (ARRIVE, GATE, 3), (HEADS, 0, 0), (LAND, GATE, 1),
    (LIFT, GATE, 3), (ARRIVE, OUT, 3), (BEGIN, DOWN, 2), (HEADS, 0, 0), (ARRIVE, DOWN, 1),
    (LAND, GATE, 2), (HEADS, 0, 0), (LIFT, DOWN, 1), (PROJECT, 0, 0), (LAND, GATE, 3),
    (ARRIVE, UP, 2), (GATES, 0, 0), (ARRIVE, UP, 3), (ARRIVE, DOWN, 2), (LIFT, DOWN, 2),
    (UPS, 0, 0), (ARRIVE, DOWN, 3), (LIFT, DOWN, 3), (LAND, DOWN, 1), (UPS, 0, 1), (LAND, DOWN, 2),
    (SUM_DOWN, 0, 0), (LAND, DOWN, 3),
)


def forward_body(
    lay,
    lengths,
    in_tokens,
    in_first,
    in_cosine,
    in_sine,
    gain_one_in,
    gain_two_in,
    cotangent,
    in_qkv,
    in_out,
    in_gate,
    in_up,
    in_down,
    full_qkv,
    full_out,
    full_gate,
    full_up,
    full_down,
    out_q,
    out_k,
    out_v,
    logs,
    hidden_one2,
    attended2,
    hidden_two2,
    out_after,
    out_gate,
    out_up,
    out_product,
    grad_down,
    gains,
    sums,
    w_qkv,
    w_out,
    w_gate,
    w_up,
    tokens,
    first,
    cosine,
    sine,
    gain_in,
    gain,
    hidden,
    queries,
    keys,
    values,
    attended,
    after,
    gate_pre,
    low_gate,
    low_up,
    product2,
    cot2,
    grad_low,
    turned,
    send,
    recv,
    up_send,
    up_recv,
    cross_send,
    cross_recv,
    more_send,
    more_recv,
    local,
    gain_send,
    gain_recv,
    swap_send,
    swap_recv,
    write,
):
    place = Place(lay)
    count, c = place.count, place.c
    rows, width = tokens.shape
    shard_rows = in_qkv.shape[0]
    ff = in_gate.shape[1]
    sibling = place.sibling()

    barrier = pltpu.get_barrier_semaphore()
    begins = []
    for i, (source, target) in enumerate(
        ((in_tokens, tokens), (in_cosine, cosine), (in_sine, sine), (in_first, first))
    ):
        begins.append(pltpu.make_async_copy(source, target, local.at[10 + i]))
    start(begins)
    known = [sibling, place.above()] + place.group()
    for device in known:
        pl.semaphore_signal(barrier, inc=1, device_id=device, device_id_type=pl.DeviceIdType.MESH)
    pl.semaphore_wait(barrier, len(known))

    sems = (send, recv, up_send, up_recv, cross_send, cross_recv, more_send, more_recv)

    def gather(who, own, full, first_column, total):
        return Gather(place, own, full, first_column, total, who in FORWARD_LIFTED, sems, who)

    gathers = {
        QK: gather(QK, in_qkv, w_qkv, 0, 2 * width),
        V: gather(V, in_qkv, w_qkv, 2 * width, width),
        OUT: gather(OUT, in_out, w_out, 0, width),
        GATE: gather(GATE, in_gate, w_gate, 0, ff),
        UP: gather(UP, in_up, w_up, 0, ff),
        DOWN: gather(DOWN, in_down, full_down, 0, width),
    }

    seen = {}

    def link(step):
        kind, who, turn = step
        one = gathers[who]
        if kind == BEGIN:
            firsts = [1 << i for i in range(place.bits)]
            for m in firsts[turn - 1 : turn] if count == 4 else firsts * (turn == 1):
                one.begin(m)
            return
        if count == 4:
            pieces = [turn]
        else:
            done = seen[who, kind] = seen.get((who, kind), 0) + 1
            pieces = range(1 + (done - 1) * (count - 1) // 3, 1 + done * (count - 1) // 3)
        for m in pieces:
            {ARRIVE: one.arrived, LIFT: one.lift, LAND: one.landed}[kind](m)

    gain_in[...] = jnp.zeros(gain_in.shape, BF16)
    gain_in[0:1, :] = gain_one_in[...].reshape(1, shard_rows)
    gain_in[1:2, :] = gain_two_in[...].reshape(1, shard_rows)
    gain_at = pl.multiple_of(place.f * shard_rows, shard_rows)
    gain_copies = []
    for m, device in enumerate(place.group()):
        gain_copies.append(
            remote(
                gain_in,
                gain.at[:, pl.ds(gain_at, shard_rows)],
                gain_send.at[m],
                gain_recv.at[m],
                device,
            )
        )
    gain_own = pltpu.make_async_copy(
        gain_in, gain.at[:, pl.ds(gain_at, shard_rows)], local.at[4]
    )
    start(gain_copies + [gain_own])
    order = list(FORWARD_ORDER)
    while order[0][0] == BEGIN:
        link(order.pop(0))
    own_rows = pl.ds(gain_at, shard_rows)
    locals_of = {}
    for slot, (name, source, full) in enumerate(
        ((QK, in_qkv, w_qkv), (OUT, in_out, w_out), (GATE, in_gate, w_gate), (UP, in_up, w_up))
    ):
        locals_of[name] = pltpu.make_async_copy(source, full.at[own_rows, :], local.at[slot])
        locals_of[name].start()
    half = width // 2
    down_rows = in_down.shape[0]
    down_at = pl.ds(pl.multiple_of(place.f * down_rows, down_rows), down_rows)
    down_in, down_out = [], []
    for i in range(2):
        stage = grad_low.at[pl.ds(i * down_rows, down_rows), :]
        side = pl.ds(i * half, half)
        down_in.append(pltpu.make_async_copy(in_down.at[:, side], stage, local.at[6 + i]))
        down_out.append(pltpu.make_async_copy(stage, full_down.at[down_at, side], local.at[8 + i]))
    start(down_in)

    writes = []

    def put(source, target):
        copy = pltpu.make_async_copy(source, target, write.at[len(writes)])
        copy.start()
        writes.append(copy)

    swaps = []

    def swap(source, target):
        slot = len(swaps)
        copy = remote(source, target, swap_send.at[slot], swap_recv.at[slot], sibling)
        copy.start()
        swaps.append(copy)
        return copy

    def share(source, target):
        put(source, target.at[pl.ds(0, rows), :])
        return swap(source, target.at[pl.ds(rows, rows), :])

    theirs = pl.multiple_of((1 - c) * half, 128)
    ours = pl.multiple_of(c * half, 128)
    cot_swap = swap(cotangent.at[:, pl.ds(theirs, half)], cot2.at[pl.ds(rows, rows), :])
    cot_own = pltpu.make_async_copy(
        cotangent.at[:, pl.ds(ours, half)], cot2.at[pl.ds(0, rows), :], local.at[5]
    )
    cot_own.start()

    block = min(TILE, rows)
    length = lengths[0]
    pairs = width // PAIR
    hidden_two = low_up.at[:, pl.ds(0, width)]
    two_swap, two_put, product_swaps = [], [], []

    def by_rows(step):
        @pl.loop(0, rows // block)
        def _(i):
            step(pl.ds(pl.multiple_of(i * block, block), block))

    def normalise():
        begins[0].wait()
        inputs = tokens[...].astype(F32)
        inverse = lax.rsqrt(jnp.mean(inputs * inputs, axis=-1, keepdims=True) + norm_eps)
        for copy in gain_copies:
            copy.wait_recv()
        gain_own.wait()
        gains[0:1, :] = gain[0:1, :].astype(F32)
        gains[1:2, :] = gain[1:2, :].astype(F32)
        gains[2:8, :] = jnp.zeros((6, width), F32)
        hidden[...] = (inputs * inverse * gains[0:1, :]).astype(BF16)
        share(hidden, hidden_one2)
        wait(down_in)
        start(down_out)
        sums[...] = jnp.zeros(sums.shape, F32)
        logs[...] = jnp.zeros(logs.shape, F32)

    def rotated(which, out, scale):
        def step(at):
            cos, sin = cosine[at, :], sine[at, :]
            raw = dot_nn(hidden[at, :], w_qkv[:, which * width : (which + 1) * width])
            for p in range(width // PAIR):
                x = raw[:, p * PAIR : (p + 1) * PAIR]
                low = (x * cos + swap_halves(x) * sin).astype(BF16)
                out[at, p * PAIR : (p + 1) * PAIR] = low * jnp.asarray(scale, BF16)

        by_rows(step)

    def mix(at):
        raw = dot_nn(hidden[at, :], w_qkv[:, 2 * width : 3 * width])
        kept = first[at, :].astype(F32)
        mixed = 0.5 * raw + 0.5 * kept
        values[at, :] = mixed.astype(BF16)
        sums[0:1, :] += jnp.sum(kept * kept, axis=0, keepdims=True)
        sums[1:2, :] += jnp.sum(mixed * mixed, axis=0, keepdims=True)

    turn = 2

    def attend(links):
        @pl.loop(0, pairs // turn)
        def _(i):
            for j in range(turn):
                attend_pair(i * turn + j, turned.at[j])
            for after_turn, steps in enumerate(links):
                if steps:

                    @pl.when(i == after_turn)
                    def _():
                        for step in steps:
                            link(step)

    def attend_pair(p, turned):
        at = pl.ds(pl.multiple_of(p * PAIR, PAIR), PAIR)
        q, k = queries[:, at], keys[:, at]
        v_t = values[:, at].T
        lane = lax.broadcasted_iota(jnp.int32, (rows, PAIR), 1)
        for head in range(2):
            inside = (lane // HEAD_DIM) == head
            k_head = jnp.where(inside, k, jnp.zeros_like(k))
            v_head = v_t[head * HEAD_DIM : (head + 1) * HEAD_DIM]
            for b in range(rows // block):
                upto = (b + 1) * block
                scores = dot_nt(k_head[:upto], q[b * block : upto])
                key = lax.broadcasted_iota(jnp.int32, scores.shape, 0)
                query = lax.broadcasted_iota(jnp.int32, (1, block), 1) + b * block
                allowed = key <= jnp.minimum(query, length - 1)
                scores = jnp.where(allowed, scores, -1e30)
                peak = jnp.max(scores, axis=0, keepdims=True)
                expo = jnp.exp(scores - peak)
                total = jnp.sum(expo, axis=0, keepdims=True)
                logs[p, head : head + 1, b * block : upto] = peak + jnp.log(total)
                out = dot_nn(v_head[:, :upto], expo.astype(BF16)) * (1.0 / total)
                turned[head * HEAD_DIM : (head + 1) * HEAD_DIM, b * block : upto] = out
        attended[:, at] = turned[...].T.astype(BF16)

    def project(at):
        x = tokens[at, :].astype(F32) + dot_nn(attended[at, :], w_out[...])
        after[at, :] = x
        scale = lax.rsqrt(jnp.mean(x * x, axis=-1, keepdims=True) + norm_eps)
        low_up[at, 0:width] = (x * scale * gains[1:2, :]).astype(BF16)

    def gate_rows(at):
        gate_pre[at, :] = dot_nn(low_up[at, 0:width], w_gate[...])
        low_gate[at, :] = gate_pre[at, :].astype(BF16)

    def up_rows(at):
        up_proj = dot_nn(low_up[at, 0:width], w_up[...])
        gate_of = gate_pre[at, :]
        product2[at, :] = (gate_of * jax.nn.sigmoid(gate_of) * up_proj).astype(BF16)
        low_up[at, :] = up_proj.astype(BF16)

    def compute(kind, part):
        if kind == NORMALISE:
            normalise()
        elif kind == QUERIES:
            wait(begins[1:])
            locals_of[QK].wait()
            gathers[QK].complete()
            rotated(0, queries, HEAD_DIM**-0.5)
            put(queries, out_q)
        elif kind == KEYS:
            rotated(1, keys, 1.0)
            put(keys, out_k)
        elif kind == VALUES:
            gathers[V].complete()
            put(w_qkv, full_qkv)
            by_rows(mix)
            put(values, out_v)
        elif kind == PROJECT:
            share(attended, attended2)
            locals_of[OUT].wait()
            gathers[OUT].complete()
            put(w_out, full_out)
            by_rows(project)
            put(after, out_after)
            two_swap.append(share(hidden_two, hidden_two2))
            two_put.append(writes[-1])
        elif kind == GATES:
            locals_of[GATE].wait()
            gathers[GATE].complete()
            put(w_gate, full_gate)
            by_rows(gate_rows)
            put(low_gate, out_gate)
        elif kind == UPS and part == 0:
            locals_of[UP].wait()
            gathers[UP].complete()
            put(w_up, full_up)
            two_swap[0].wait_send()
            two_put[0].wait()
            up_part(0)
        elif kind == UPS:
            up_part(1)
            put(low_up, out_up)
            put(product2.at[pl.ds(0, rows), :], out_product)
        else:
            wait(down_out)
            cot_own.wait()
            cot_swap.wait_recv()
            for copy in product_swaps:
                copy.wait_recv()

            @pl.loop(0, ff // TILE)
            def _(i):
                at = pl.ds(pl.multiple_of(i * TILE, TILE), TILE)
                grad_low[at, :] = dot_tn(product2[:, at], cot2[...]).astype(BF16)

            put(grad_low, grad_down)

    def up_part(i):
        size = rows // 2
        up_rows(pl.ds(i * size, size))
        copy = swap(product2.at[pl.ds(i * size, size), :], product2.at[pl.ds(rows + i * size, size), :])
        product_swaps.append(copy)

    while order:
        step = order.pop(0)
        if step[0] <= LAND:
            link(step)
        elif step[0] == HEADS:
            turns = pairs // turn
            links, at = [[] for _ in range(4)], 0
            while order and (order[0][0] <= LAND or order[0][0] == HEADS):
                if order[0][0] == HEADS:
                    order.pop(0)
                    at += 1
                else:
                    links[at].append(order.pop(0))
            spread = [[] for _ in range(turns)]
            for i, steps in enumerate(links):
                spread[(i + 1) * turns // 4 - 1] += steps
            attend(spread)
        else:
            compute(step[0], step[2])

    gathers[DOWN].complete()
    for one in gathers.values():
        one.drain()
    for copy in gain_copies:
        copy.wait_send()
    waited = [cot_swap, *product_swaps]
    for copy in swaps:
        if not any(copy is item for item in waited):
            copy.wait_recv()
        if copy is not two_swap[0]:
            copy.wait_send()
    for copy in writes:
        if copy is not two_put[0]:
            copy.wait()


def forward_kernel(lay, lengths, tokens, first, tables, gain_one, gain_two, cotangent, w_qkv, w_out, w_gate, w_up, w_down):
    count = lay.fs
    rows, width = tokens.shape
    n, ff = w_qkv.shape[1], w_gate.shape[1]
    half = width // 2
    pairs = width // PAIR
    big = struct((rows, width), BF16)
    wide = struct((rows, ff), BF16)
    two = struct((2 * rows, width), BF16)
    dma = pltpu.SemaphoreType.DMA
    vmem = pl.BlockSpec(memory_space=pltpu.VMEM)
    weights = [(width, n), (width, width), (width, ff), (width, ff), (ff, width)]
    out_shape = (
        [struct(shape, BF16) for shape in weights]
        + [big, big, big, struct((pairs, 8, rows), F32)]
        + [two, two, two, struct((rows, width), F32), wide, wide, wide]
        + [struct((ff, half), BF16), struct((8, width), F32), struct((8, width), F32)]
    )
    out_specs = [ANY] * 8 + [vmem] + [ANY] * 8 + [vmem, vmem]
    return pl.pallas_call(
        functools.partial(forward_body, lay),
        in_specs=[pl.BlockSpec(memory_space=pltpu.SMEM)] + [ANY] * 4 + [vmem] * 2 + [ANY] * 6,
        out_specs=out_specs,
        out_shape=out_shape,
        scratch_shapes=[
            pltpu.VMEM((width, n), BF16),
            pltpu.VMEM((width, width), BF16),
            pltpu.VMEM((width, ff), BF16),
            pltpu.VMEM((width, ff), BF16),
            pltpu.VMEM((rows, width), BF16),
            pltpu.VMEM((rows, width), BF16),
            pltpu.VMEM((rows, PAIR), F32),
            pltpu.VMEM((rows, PAIR), F32),
            pltpu.VMEM((GAIN_ROWS, width // count), BF16),
            pltpu.VMEM((GAIN_ROWS, width), BF16),
            pltpu.VMEM((rows, width), BF16),
            pltpu.VMEM((rows, width), BF16),
            pltpu.VMEM((rows, width), BF16),
            pltpu.VMEM((rows, width), BF16),
            pltpu.VMEM((rows, width), BF16),
            pltpu.VMEM((rows, width), F32),
            pltpu.VMEM((rows, ff), F32),
            pltpu.VMEM((rows, ff), BF16),
            pltpu.VMEM((rows, ff), BF16),
            pltpu.VMEM((2 * rows, ff), BF16),
            pltpu.VMEM((2 * rows, half), BF16),
            pltpu.VMEM((ff, half), BF16),
            pltpu.VMEM((2, PAIR, rows), F32),
            *[dma((6 * count,))] * 8,
            dma((14,)),
            dma((count - 1,)),
            dma((count - 1,)),
            dma((6,)),
            dma((6,)),
            dma((16,)),
        ],
        compiler_params=pltpu.CompilerParams(
            collective_id=0, has_side_effects=True, vmem_limit_bytes=62 * 2**20
        ),
        cost_estimate=pl.CostEstimate(
            flops=2 * rows * width * (n + width + 3 * ff),
            bytes_accessed=60 * 2**20,
            transcendentals=0,
        ),
        name="forward",
    )(lengths, tokens, first, *tables, gain_one, gain_two, cotangent, w_qkv, w_out, w_gate, w_up, w_down)


def rms_back(grad, normed, inverse):
    return inverse * (grad - normed * jnp.mean(grad * normed, axis=-1, keepdims=True))


class Line:
    def __init__(self, lay, place):
        size = lay.line
        r = place.d // 2
        self.half = size // 2
        upper = r // self.half
        toward = 1 - 2 * upper
        self.depth = r * toward + upper * (size - 1)
        self.next = (place.d + 2 * toward, place.f)
        self.prev = (place.d - 2 * toward, place.f)
        self.middle = self.depth == self.half - 1
        self.inner = self.depth > 0
        self.others = []
        reach = 1
        while reach < size:
            self.others.append((place.d + 2 * reach * (1 - 2 * lax.rem(r // reach, 2)), place.f))
            reach *= 2


def signal(sem, device):
    pl.semaphore_signal(sem, inc=1, device_id=device, device_id_type=pl.DeviceIdType.MESH)


class Reduce:
    def __init__(
        self, place, line, slot, window, held, sources, first, later, final, column, sems
    ):
        send, recv, z_send, z_recv, credit, f_local, f_send, f_recv = sems
        self.place, self.line, self.held, self.window = place, line, held, window
        self.bits, count = place.bits, place.count
        self.count = count
        base = slot * count
        half = count // 2
        self.steps, self.lands = [], []
        at = 0
        for i in range(self.bits):
            blocks = count >> (i + 1)
            copies, lands = [], []
            for q in range(blocks):
                source = sources[q] if i == 0 else held.at[blocks + q, window]
                land = first.at[q, window] if i == 0 else later.at[at + q, window]
                index = base + q if i == 0 else base + half + at + q
                lands.append(land)
                copies.append(remote(source, land, send.at[index], recv.at[index], place.partner(i)))
            if i > 0:
                at += blocks
            self.steps.append(copies)
            self.lands.append(lands)
        mine, inner, outer = held.at[0, window], first.at[0, window], first.at[1, window]
        two = 2 * slot
        self.hops = {
            "in": remote(mine, inner, z_send.at[two], z_recv.at[two], line.next),
            "middle": remote(mine, outer, z_send.at[two], z_recv.at[two + 1], line.next),
            "back": remote(inner, outer, z_send.at[two + 1], z_recv.at[two + 1], line.prev),
            "out": remote(outer, outer, z_send.at[two + 1], z_recv.at[two + 1], line.prev),
        }
        self.mine, self.inner, self.outer = mine, inner, outer
        spot = final.at[window, column]
        self.ends = []
        for source in (inner, outer):
            self.ends.append(
                (
                    pltpu.make_async_copy(source, spot, f_local.at[slot]),
                    remote(source, spot, f_send.at[slot], f_recv.at[slot], place.sibling()),
                )
            )
        self.from_next, self.from_prev = credit.at[two], credit.at[two + 1]

    def begin(self, q):
        self.steps[0][q].start()

    def block(self, i, q):
        blocks = self.count >> (i + 1)
        self.steps[i][q].wait_recv()
        here = self.held.at[q, self.window]
        here[...] = add_low(here[...], self.lands[i][q][...])
        if i + 1 < self.bits and q >= blocks // 2:
            self.steps[i + 1][q - blocks // 2].start()

    def leaving(self):
        half = self.count // 2
        for q in reversed(range(half // 2, half)):
            self.block(0, q)

    def staying(self):
        for q in reversed(range(self.count // 4)):
            self.block(0, q)
        line = self.line

        @pl.when(line.middle)
        def _():
            signal(self.from_next, line.next)

        @pl.when(jnp.logical_not(line.middle))
        def _():
            signal(self.from_prev, line.next)

        @pl.when(line.inner)
        def _():
            signal(self.from_next, line.prev)

    def rest(self):
        for i in range(1, self.bits):
            for q in reversed(range(self.count >> (i + 1))):
                self.block(i, q)

        @pl.when(jnp.logical_not(self.line.inner))
        def _():
            self.onward()

    def onward(self):
        line = self.line
        pl.semaphore_wait(self.from_next, 1)

        @pl.when(line.middle)
        def _():
            self.hops["middle"].start()

        @pl.when(jnp.logical_not(line.middle))
        def _():
            self.hops["in"].start()

    def inward(self):
        @pl.when(self.line.inner)
        def _():
            self.hops["in"].wait_recv()
            self.mine[...] = add_low(self.mine[...], self.inner[...])
            self.onward()

    def finish(self, which):
        local, cross = self.ends[which]
        local.start()
        cross.start()

    def across(self):
        line = self.line

        @pl.when(line.middle)
        def _():
            self.hops["middle"].wait_recv()
            self.inner[...] = add_low(self.mine[...], self.outer[...])

            @pl.when(line.inner)
            def _():
                pl.semaphore_wait(self.from_prev, 1)
                self.hops["back"].start()

            self.finish(0)

    def outward(self):
        line = self.line
        if line.half == 1:
            return

        @pl.when(jnp.logical_not(line.middle))
        def _():
            self.hops["out"].wait_recv()

            @pl.when(line.inner)
            def _():
                pl.semaphore_wait(self.from_prev, 1)
                self.hops["out"].start()

            self.finish(1)

    def drain(self):
        for copies in self.steps:
            for copy in copies:
                copy.wait_send()
        self.hops["in"].wait_send()

        @pl.when(self.line.inner)
        def _():
            self.hops["out"].wait_send()

        local, cross = self.ends[0]
        local.wait()
        cross.wait_send()
        cross.wait_recv()


W_DOWN, W_GATE, W_UP, W_OUT, W_V, W_K, W_Q = range(7)
BACKWARD_PARTS = (2, 2, 4, 2, 2, 2, 2)
LEAVING, STAYING, REST, INWARD, ACROSS, OUTWARD, SMALL = range(7)
BLOCKS, MLP_TILES, NORM_TWO, ATTEND_GRAD, HEAD_PAIRS, QKV_TILES, NORM_ONE = range(7, 14)
BACKWARD_ORDER = (
    (LEAVING, W_DOWN, 0), (STAYING, W_DOWN, 0), (BLOCKS, W_GATE, 3), (BLOCKS, W_GATE, 2),
    (LEAVING, W_DOWN, 1), (BLOCKS, W_GATE, 1), (REST, W_DOWN, 0), (BLOCKS, W_GATE, 0),
    (BLOCKS, W_UP, 3), (BLOCKS, W_UP, 2), (BLOCKS, W_UP, 1), (BLOCKS, W_UP, 0),
    (STAYING, W_DOWN, 1), (MLP_TILES, 0, 0), (REST, W_DOWN, 1), (INWARD, W_DOWN, 0),
    (LEAVING, W_GATE, 0), (MLP_TILES, 0, 1), (MLP_TILES, 0, 2), (MLP_TILES, 0, 3),
    (LEAVING, W_GATE, 1), (NORM_TWO, 0, 0), (INWARD, W_DOWN, 1), (ACROSS, W_DOWN, 0),
    (ATTEND_GRAD, 0, 0), (STAYING, W_GATE, 0), (REST, W_GATE, 0), (BLOCKS, W_OUT, 3),
    (BLOCKS, W_OUT, 2), (BLOCKS, W_OUT, 1), (BLOCKS, W_OUT, 0), (HEAD_PAIRS, 0, 0),
    (STAYING, W_GATE, 1), (REST, W_GATE, 1), (HEAD_PAIRS, 0, 1), (LEAVING, W_UP, 0),
    (LEAVING, W_UP, 1), (INWARD, W_GATE, 0), (ACROSS, W_DOWN, 1), (OUTWARD, W_DOWN, 0),
    (HEAD_PAIRS, 0, 2), (LEAVING, W_UP, 2), (HEAD_PAIRS, 0, 3), (LEAVING, W_UP, 3),
    (HEAD_PAIRS, 0, 4), (INWARD, W_GATE, 1), (HEAD_PAIRS, 0, 5), (ACROSS, W_GATE, 0),
    (STAYING, W_UP, 0), (REST, W_UP, 0), (OUTWARD, W_DOWN, 1), (HEAD_PAIRS, 0, 6),
    (STAYING, W_UP, 1), (REST, W_UP, 1), (HEAD_PAIRS, 0, 7), (INWARD, W_UP, 0), (ACROSS, W_GATE, 1),
    (STAYING, W_UP, 2), (LEAVING, W_OUT, 0), (REST, W_UP, 2), (STAYING, W_UP, 3), (REST, W_UP, 3),
    (LEAVING, W_OUT, 1), (OUTWARD, W_GATE, 0), (INWARD, W_UP, 1), (BLOCKS, W_V, 3),
    (BLOCKS, W_V, 2), (BLOCKS, W_V, 1), (STAYING, W_OUT, 0), (BLOCKS, W_V, 0), (REST, W_OUT, 0),
    (ACROSS, W_UP, 0), (BLOCKS, W_K, 3), (BLOCKS, W_K, 2), (INWARD, W_UP, 2), (STAYING, W_OUT, 1),
    (BLOCKS, W_K, 1), (REST, W_OUT, 1), (BLOCKS, W_K, 0), (LEAVING, W_V, 0), (ACROSS, W_UP, 1),
    (OUTWARD, W_GATE, 1), (BLOCKS, W_Q, 3), (LEAVING, W_V, 1), (INWARD, W_UP, 3), (BLOCKS, W_Q, 2),
    (BLOCKS, W_Q, 1), (BLOCKS, W_Q, 0), (QKV_TILES, 0, 0), (INWARD, W_OUT, 0), (ACROSS, W_UP, 2),
    (STAYING, W_V, 0), (REST, W_V, 0), (OUTWARD, W_UP, 0), (QKV_TILES, 0, 1), (INWARD, W_OUT, 1),
    (ACROSS, W_UP, 3), (LEAVING, W_K, 0), (STAYING, W_V, 1), (REST, W_V, 1), (OUTWARD, W_UP, 1),
    (QKV_TILES, 0, 2), (LEAVING, W_K, 1), (INWARD, W_V, 0), (ACROSS, W_OUT, 0), (QKV_TILES, 0, 3),
    (ACROSS, W_OUT, 1), (INWARD, W_V, 1), (STAYING, W_K, 0), (REST, W_K, 0), (OUTWARD, W_UP, 2),
    (NORM_ONE, 0, 0), (LEAVING, W_Q, 0), (ACROSS, W_V, 0), (LEAVING, W_Q, 1), (STAYING, W_K, 1),
    (REST, W_K, 1), (INWARD, W_K, 0), (ACROSS, W_V, 1), (OUTWARD, W_UP, 3), (OUTWARD, W_OUT, 0),
    (SMALL, 0, 1), (STAYING, W_Q, 0), (OUTWARD, W_OUT, 1), (REST, W_Q, 0), (SMALL, 0, 2),
    (STAYING, W_Q, 1), (INWARD, W_K, 1), (REST, W_Q, 1), (ACROSS, W_K, 0), (OUTWARD, W_V, 0),
    (SMALL, 0, 3), (INWARD, W_Q, 0), (OUTWARD, W_V, 1), (SMALL, 0, 4), (ACROSS, W_K, 1),
    (INWARD, W_Q, 1), (OUTWARD, W_K, 0), (SMALL, 0, 5), (ACROSS, W_Q, 0), (OUTWARD, W_K, 1),
    (ACROSS, W_Q, 1), (OUTWARD, W_Q, 0), (OUTWARD, W_Q, 1),
)


def backward_body(
    lay,
    lengths,
    in_cosine,
    in_sine,
    gains,
    sums,
    in_logs,
    full_qkv,
    full_out,
    full_gate,
    full_up,
    full_down,
    in_q,
    in_k,
    in_v,
    hidden_one2,
    attended2,
    hidden_two2,
    in_after,
    in_gate,
    in_up,
    in_product,
    in_grad_down,
    tokens,
    cotangent,
    output,
    grad_tokens,
    grad_first,
    sum_qkv,
    sum_out,
    sum_gate,
    sum_up,
    sum_down,
    small,
    cosine,
    sine,
    logs,
    gate,
    up,
    product,
    ring,
    w_out,
    one,
    two,
    three,
    cot,
    left,
    right,
    low,
    attend_grad,
    gate_sib,
    up_sib,
    low_sib,
    q_sib,
    k_sib,
    v_sib,
    held_down,
    held_gate,
    held_up,
    held_narrow,
    first_down,
    first_gate,
    first_up,
    first_narrow,
    later_down,
    later_gate,
    later_up,
    later_narrow,
    small_land,
    turned,
    load_sem,
    ring_sem,
    swap_send,
    swap_recv,
    write_sem,
    send,
    recv,
    z_send,
    z_recv,
    credit,
    f_local,
    f_send,
    f_recv,
    small_send,
    small_recv,
):
    place = Place(lay)
    line = Line(lay, place)
    count, c = place.count, place.c
    sibling = place.sibling()
    rows, width = cot.shape
    ff = gate.shape[1]
    side, narrow = ff // 2, width // 2
    block = min(TILE, rows)
    bits = place.bits

    barrier = pltpu.get_barrier_semaphore()
    partners = [place.partner(i) for i in range(bits)]
    known = [sibling] + partners + line.others + [line.next]
    for device in known:
        signal(barrier, device)

    @pl.when(line.inner)
    def _():
        signal(barrier, line.prev)
        pl.semaphore_wait(barrier, len(known) + 1)

    @pl.when(jnp.logical_not(line.inner))
    def _():
        pl.semaphore_wait(barrier, len(known))

    loads = {}

    def load(name, source, target):
        copy = pltpu.make_async_copy(source, target, load_sem.at[len(loads)])
        copy.start()
        loads[name] = copy

    writes = []

    def put(source, target):
        copy = pltpu.make_async_copy(source, target, write_sem.at[len(writes)])
        copy.start()
        writes.append(copy)
        return copy

    swaps = []

    def swap(source, target):
        slot = len(swaps)
        copy = remote(source, target, swap_send.at[slot], swap_recv.at[slot], sibling)
        copy.start()
        swaps.append(copy)
        return copy

    def shard_of(p):
        m = sum(((p >> i) & 1) << (bits - 1 - i) for i in range(bits))
        return place.shard(m)

    sems = (send, recv, z_send, z_recv, credit, f_local, f_send, f_recv)
    half = count // 2
    down_rows = in_grad_down.shape[0] // count
    shard_rows = sum_qkv.shape[0]

    def down_block(p, window=None):
        at = pl.multiple_of(shard_of(p) * down_rows, down_rows)
        if window is None:
            return in_grad_down.at[pl.ds(at, down_rows), :]
        return in_grad_down.at[pl.ds(at + window.start, window.size), :]

    reduces = {}

    def reduce_of(name, held, first, later, final, offset, size):
        parts = BACKWARD_PARTS[name]
        part_rows = held.shape[1] // parts
        for part in range(parts):
            window = pl.ds(part * part_rows, part_rows)
            if name == W_DOWN:
                sources = [down_block(half + q, window) for q in range(half)]
            else:
                sources = [held.at[half + q, window] for q in range(half)]
            column = pl.ds(pl.multiple_of(offset + c * size, 128), size)
            reduces[name, part] = Reduce(
                place, line, len(reduces), window, held, sources, first, later, final, column, sems
            )

    def narrow_of(index, name, final, offset):
        at = index * count
        reduce_of(
            name,
            held_narrow.at[pl.ds(at, count)],
            first_narrow.at[pl.ds(index * half, half)],
            later_narrow.at[pl.ds(index * (half - 1), half - 1)],
            final,
            offset,
            narrow,
        )

    reduce_of(W_DOWN, held_down, first_down, later_down, sum_down, 0, narrow)
    reduce_of(W_GATE, held_gate, first_gate, later_gate, sum_gate, 0, side)
    reduce_of(W_UP, held_up, first_up, later_up, sum_up, 0, side)
    narrow_of(0, W_OUT, sum_out, 0)
    narrow_of(1, W_V, sum_qkv, 2 * width)
    narrow_of(2, W_K, sum_qkv, width)
    narrow_of(3, W_Q, sum_qkv, 0)

    def parts_of(name):
        return [reduces[name, i] for i in range(BACKWARD_PARTS[name])]

    smalls = []

    def small_step():
        slot = len(smalls)
        device = ([sibling] + partners + line.others)[slot]
        copy = remote(
            small_land.at[2 * slot],
            small_land.at[2 * slot + 1],
            small_send.at[slot],
            small_recv.at[slot],
            device,
        )
        small_land[2 * slot] = small[...]
        copy.start()
        smalls.append(copy)

    def small_take():
        smalls[-1].wait_recv()
        small[...] += small_land[2 * len(smalls) - 1]

    small_count = 1 + bits + len(line.others)

    def link(step):
        kind, who, part = step
        if kind == SMALL:
            while True:
                small_take()
                if len(smalls) == small_count:
                    return
                small_step()
                if part < 5:
                    return
        reduce = reduces[who, part]
        {
            LEAVING: reduce.leaving,
            STAYING: reduce.staying,
            REST: reduce.rest,
            INWARD: reduce.inward,
            ACROSS: reduce.across,
            OUTWARD: reduce.outward,
        }[kind]()

    for reduce in parts_of(W_DOWN):
        for q in reversed(range(half)):
            reduce.begin(q)

    tile = min(TILE, side)
    whole_tiles, rest = side // tile, side % tile

    def ring_copy(row, slot, size):
        return pltpu.make_async_copy(
            full_down.at[pl.ds(row, size), :],
            ring.at[slot, pl.ds(0, size), pl.ds(0, width)],
            ring_sem.at[slot],
        )

    theirs = pl.multiple_of((1 - c) * side, 128)
    ours = pl.multiple_of(c * side, 128)
    ring_copy(theirs, 0, tile).start()
    load("gate", in_gate, gate)
    load("up", in_up, up)
    load("cot", cotangent, cot)
    load("product", in_product, product)
    load("after", in_after, one)
    load("left", hidden_two2, left)
    down_loads = []
    for q in range(half):
        copy = pltpu.make_async_copy(down_block(q), held_down.at[q], load_sem.at[17 + q])
        copy.start()
        down_loads.append(copy)
    load("out", full_out, w_out)
    load("right", attended2, right)
    load("cosine", in_cosine, cosine)
    load("sine", in_sine, sine)
    load("logs", in_logs, logs)
    for name in ("gate", "up", "cot", "product", "after"):
        loads[name].wait()
    two[...] = one[...]

    def down_tile(at, slot, size):
        rows_of = ring[slot, 0:size, 0:width]
        grad_product = dot_nt(cot[...], rows_of)
        gate_pre = gate[:, pl.ds(at, size)].astype(F32)
        up_proj = up[:, pl.ds(at, size)].astype(F32)
        sigma = jax.nn.sigmoid(gate_pre)
        gate[:, pl.ds(at, size)] = (
            grad_product * up_proj * sigma * (1.0 + gate_pre * (1.0 - sigma))
        ).astype(BF16)
        up[:, pl.ds(at, size)] = (grad_product * (gate_pre * sigma)).astype(BF16)
        two[...] += dot_nn(product[:, pl.ds(at, size)], rows_of)

    def half_down(base, following):
        @pl.loop(0, whole_tiles)
        def _(t):
            slot = lax.rem(t, 2)
            at = pl.multiple_of(base + t * tile, 128)
            ring_copy(at, slot, tile).wait()

            @pl.when(t + 1 < whole_tiles)
            def _():
                ring_copy(pl.multiple_of(at + tile, 128), 1 - slot, tile).start()

            if rest:

                @pl.when(t + 1 == whole_tiles)
                def _():
                    ring_copy(pl.multiple_of(at + tile, 128), 2, rest).start()

            down_tile(at, slot, tile)

        if following is not None:
            ring_copy(following, 0, tile).start()
        if rest:
            at = pl.multiple_of(base + whole_tiles * tile, 128)
            ring_copy(at, 2, rest).wait()
            down_tile(at, 2, rest)

    half_down(theirs, ours)
    gate_swap = swap(gate.at[:, pl.ds(theirs, side)], gate_sib)
    up_swap = swap(up.at[:, pl.ds(theirs, side)], up_sib)
    half_down(ours, None)
    low[...] = two[...].astype(BF16)
    output_put = put(low, output)
    load("q", in_q, product.at[:, pl.ds(0, width)])
    load("k", in_k, product.at[:, pl.ds(width, width)])

    def tile_copies(i):
        at = pl.ds(i * block_w, block_w)
        return (
            pltpu.make_async_copy(
                full_gate.at[at, :], ring.at[i % 2, :, pl.ds(0, ff)], ring_sem.at[i % 2]
            ),
            pltpu.make_async_copy(
                full_up.at[at, :], ring.at[2 + i % 2, :, pl.ds(0, ff)], ring_sem.at[2 + i % 2]
            ),
        )

    block_w = min(TILE, width)
    start(tile_copies(0))
    start(tile_copies(1))

    def grad_block(held, p, both, own, other):
        at = pl.ds(pl.multiple_of(shard_of(p) * shard_rows, 128), shard_rows)
        held[p] = (
            dot_tn(both[0:rows, at], own) + dot_tn(both[rows : 2 * rows, at], other)
        ).astype(BF16)

    def grad_of(who, quarter, both, own, other):
        parts = parts_of(who)
        for p in reversed(range(quarter * count // 4, (quarter + 1) * count // 4)):
            grad_block(parts[0].held, p, both, own(), other())
            if p >= half:
                for part in parts:
                    part.begin(p - half)

    def ours_of(ref, offset, size):
        at = pl.ds(pl.multiple_of(offset + c * size, 128), size)
        return lambda: ref[:, at]

    tiles = width // block_w

    def back_tile(i):
        wait(tile_copies(i))
        at = slice(i * block_w, (i + 1) * block_w)
        two[:, at] = dot_nt(gate[...], ring[i % 2, :, 0:ff]) + dot_nt(up[...], ring[2 + i % 2, :, 0:ff])
        if i + 2 < tiles:
            start(tile_copies(i + 2))

    def back_end():
        output_put.wait()
        small[...] = jnp.zeros(small.shape, F32)
        small[2:4, :] = sums[0:2, :]

        @pl.loop(0, rows // block)
        def _(i):
            at = pl.ds(pl.multiple_of(i * block, block), block)
            x = one[at, :]
            inverse = lax.rsqrt(jnp.mean(x * x, axis=-1, keepdims=True) + norm_eps)
            normed = x * inverse
            grad_hidden = two[at, :]
            small[1:2, :] += jnp.sum(grad_hidden * normed, axis=0, keepdims=True)
            result = cot[at, :].astype(F32) + rms_back(grad_hidden * gains[1:2, :], normed, inverse)
            three[at, :] = result
            low[at, :] = result.astype(BF16)

        low_swap.append(swap(low.at[:, pl.ds(theirs_narrow, narrow)], low_sib))
        gate_swap.wait_send()
        up_swap.wait_send()
        load("v", in_v, up.at[:, pl.ds(width, width)])
        load("tokens", tokens, cot)

    theirs_narrow = pl.multiple_of((1 - c) * narrow, 128)
    low_swap, head_swaps = [], {}

    def qkv_copy(i):
        return pltpu.make_async_copy(
            full_qkv.at[pl.ds(i * block_w, block_w), :], ring.at[i % 4], ring_sem.at[i % 4]
        )

    def attended_grad():
        loads["out"].wait()

        @pl.loop(0, rows // block)
        def _(i):
            at = pl.ds(pl.multiple_of(i * block, block), block)
            attend_grad[at, :] = dot_nt(low[at, :], w_out[...]).astype(BF16)

        for i in range(min(4, tiles)):
            qkv_copy(i).start()
        loads["right"].wait()
        low_swap[0].wait_recv()

    length = lengths[0]
    pairs = width // PAIR
    q_grad, k_grad = gate.at[:, pl.ds(0, width)], gate.at[:, pl.ds(width, width)]
    v_grad = up.at[:, pl.ds(0, width)]

    def attend_back(base, links):
        @pl.loop(0, pairs // 2)
        def _(i):
            p = base + i
            at = pl.ds(pl.multiple_of(p * PAIR, PAIR), PAIR)
            shift = pl.ds(pl.multiple_of(width + p * PAIR, PAIR), PAIR)
            q, k, v, g = product[:, at], product[:, shift], up[:, shift], attend_grad[:, at]
            lane = lax.broadcasted_iota(jnp.int32, (rows, PAIR), 1)
            k_t = k.T
            sums_k, sums_v = [], []
            for head in range(2):
                inside = (lane // HEAD_DIM) == head
                k_head = jnp.where(inside, k, jnp.zeros_like(k))
                v_head = jnp.where(inside, v, jnp.zeros_like(v))
                k_turned = k_t[head * HEAD_DIM : (head + 1) * HEAD_DIM]
                parts_k, parts_v = [], []
                for b in range(rows // block):
                    upto = (b + 1) * block
                    q_block, g_block = q[b * block : upto], g[b * block : upto]
                    scores = dot_nt(k_head[:upto], q_block)
                    key = lax.broadcasted_iota(jnp.int32, scores.shape, 0)
                    query = lax.broadcasted_iota(jnp.int32, (1, block), 1) + b * block
                    log_total = logs[p, head : head + 1, b * block : upto]
                    allowed = key <= jnp.minimum(query, length - 1)
                    soft = jnp.where(allowed, jnp.exp(scores - log_total), 0.0)
                    grad_soft = dot_nt(v_head[:upto], g_block)
                    inner = jnp.sum(soft * grad_soft, axis=0, keepdims=True)
                    grad_scores = (soft * (grad_soft - inner)).astype(BF16)
                    turned[head * HEAD_DIM : (head + 1) * HEAD_DIM, b * block : upto] = dot_nn(
                        k_turned[:, :upto], grad_scores
                    )
                    parts_k.append(dot_nn(grad_scores, q_block))
                    parts_v.append(dot_nn(soft.astype(BF16), g_block))
                for parts, gathered in ((parts_k, sums_k), (parts_v, sums_v)):
                    rows_of = []
                    for r in range(rows // block):
                        piece = parts[r][r * block : (r + 1) * block]
                        for later in parts[r + 1 :]:
                            piece = piece + later[r * block : (r + 1) * block]
                        rows_of.append(piece)
                    gathered.append(jnp.concatenate(rows_of, axis=0))
            first_head = lane < HEAD_DIM
            cos, sin = cosine[...], sine[...]

            def back(x):
                return (x * cos - swap_halves(x) * sin).astype(BF16)

            gate[:, at] = back(turned[...].T * HEAD_DIM**-0.5)
            gate[:, shift] = back(jnp.where(first_head, sums_k[0], sums_k[1]))
            half_v = 0.5 * jnp.where(first_head, sums_v[0], sums_v[1])
            up[:, at] = half_v.astype(BF16)
            for after, steps in enumerate(links):
                if steps:

                    @pl.when(i == after)
                    def _():
                        for step in steps:
                            link(step)

    def qkv_tile(i):
        qkv_copy(i).wait()
        slot = i % 4
        one[:, i * block_w : (i + 1) * block_w] = (
            dot_nt(gate[:, 0:width], ring[slot, :, 0:width])
            + dot_nt(gate[:, width : 2 * width], ring[slot, :, width : 2 * width])
            + dot_nt(up[:, 0:width], ring[slot, :, 2 * width : 3 * width])
        )
        if i + 4 < tiles:
            qkv_copy(i + 4).start()

    def qkv_end():
        loads["tokens"].wait()
        low_swap[0].wait_send()

        @pl.loop(0, rows // block)
        def _(i):
            at = pl.ds(pl.multiple_of(i * block, block), block)
            x = cot[at, :].astype(F32)
            inverse = lax.rsqrt(jnp.mean(x * x, axis=-1, keepdims=True) + norm_eps)
            normed = x * inverse
            grad_hidden = one[at, :]
            small[0:1, :] += jnp.sum(grad_hidden * normed, axis=0, keepdims=True)
            grads = three[at, :] + rms_back(grad_hidden * gains[0:1, :], normed, inverse)
            low[at, :] = grads.astype(BF16)

        put(low, grad_tokens)
        small_step()

    def first_of(who, quarter):
        if quarter != 3:
            return
        if who == W_GATE:
            loads["left"].wait()
            gate_swap.wait_recv()
        elif who == W_UP:
            up_swap.wait_recv()
        elif who in head_swaps:
            if who == W_V:
                loads["one"].wait()
            head_swaps[who].wait_recv()

    lefts = {
        W_GATE: (left, ours_of(gate, 0, side), lambda: gate_sib[...]),
        W_UP: (left, ours_of(up, 0, side), lambda: up_sib[...]),
        W_OUT: (right, ours_of(low, 0, narrow), lambda: low_sib[...]),
        W_V: (left, ours_of(up, 0, narrow), lambda: v_sib[...]),
        W_K: (left, ours_of(gate, width, narrow), lambda: k_sib[...]),
        W_Q: (left, ours_of(gate, 0, narrow), lambda: q_sib[...]),
    }

    def compute(kind, who, quarter):
        if kind == NORM_TWO:
            back_end()
        elif kind == ATTEND_GRAD:
            attended_grad()
        elif kind == NORM_ONE:
            qkv_end()
        elif kind == BLOCKS:
            first_of(who, quarter)
            grad_of(who, quarter, *lefts[who])
            if who == W_UP and quarter == 0:
                load("one", hidden_one2, left)
        else:
            for i in range(quarter * tiles // 4, (quarter + 1) * tiles // 4):
                (back_tile if kind == MLP_TILES else qkv_tile)(i)

    order = list(BACKWARD_ORDER)
    while order:
        step = order.pop(0)
        if step[0] <= SMALL:
            if step == (LEAVING, W_DOWN, 0):
                for copy in down_loads:
                    copy.wait()
            link(step)
        elif step[0] == HEAD_PAIRS:
            upper = step[2] == 4
            links, at = [[] for _ in range(4)], 0
            while order and (order[0][0] <= SMALL or (order[0][0] == HEAD_PAIRS and at < 3)):
                if order[0][0] == HEAD_PAIRS:
                    order.pop(0)
                    at += 1
                else:
                    links[at].append(order.pop(0))
            if not upper:
                for key in ("q", "k", "v", "cosine", "sine", "logs"):
                    loads[key].wait()
            spread = [[] for _ in range(pairs // 2)]
            for i, steps in enumerate(links):
                spread[(i + 1) * (pairs // 2) // 4 - 1] += steps
            attend_back((c if upper else 1 - c) * (pairs // 2), spread)
            if upper:
                put(v_grad, grad_first)
            else:
                for key, ref, land in ((W_V, v_grad, v_sib), (W_K, k_grad, k_sib), (W_Q, q_grad, q_sib)):
                    head_swaps[key] = swap(ref.at[:, pl.ds(theirs_narrow, narrow)], land)
        else:
            compute(*step)

    for reduce in reduces.values():
        reduce.drain()
    for copy in smalls:
        copy.wait_send()
    for copy in swaps:
        if not any(copy is item for item in (gate_swap, up_swap, low_swap[0])):
            copy.wait_send()
    for copy in writes:
        if copy is not output_put:
            copy.wait()


def backward_kernel(lay, lengths, tables, gains, sums, logs, weights, saved, tokens, cotangent):
    count = lay.fs
    half = count // 2
    rows, width = tokens.shape
    n, ff = weights[0].shape[1], weights[2].shape[1]
    shard, down = width // count, ff // count
    side, narrow = ff // 2, width // 2
    dma = pltpu.SemaphoreType.DMA
    vmem = pl.BlockSpec(memory_space=pltpu.VMEM)
    tall = pltpu.VMEM((rows, ff), BF16)
    flat = pltpu.VMEM((rows, width), BF16)
    full = pltpu.VMEM((rows, width), F32)
    small_steps = 1 + lay.bits + (lay.line.bit_length() - 1)
    parts = sum(BACKWARD_PARTS)
    operands = (lengths, *tables, gains, sums, logs, *weights, *saved, tokens, cotangent)
    return pl.pallas_call(
        functools.partial(backward_body, lay),
        in_specs=[pl.BlockSpec(memory_space=pltpu.SMEM)]
        + [ANY, ANY, vmem, vmem]
        + [ANY] * (len(operands) - 5),
        out_specs=[ANY] * 8 + [vmem],
        out_shape=[
            struct((rows, width), BF16),
            struct((rows, width), BF16),
            struct((rows, width), BF16),
            struct((shard, n), BF16),
            struct((shard, width), BF16),
            struct((shard, ff), BF16),
            struct((shard, ff), BF16),
            struct((down, width), BF16),
            struct((8, width), F32),
        ],
        scratch_shapes=[
            pltpu.VMEM((rows, PAIR), F32),
            pltpu.VMEM((rows, PAIR), F32),
            pltpu.VMEM(logs.shape, F32),
            tall,
            tall,
            tall,
            pltpu.VMEM((4, min(TILE, width), n), BF16),
            pltpu.VMEM((width, width), BF16),
            full,
            full,
            full,
            flat,
            pltpu.VMEM((2 * rows, width), BF16),
            pltpu.VMEM((2 * rows, width), BF16),
            flat,
            flat,
            pltpu.VMEM((rows, side), BF16),
            pltpu.VMEM((rows, side), BF16),
            pltpu.VMEM((rows, narrow), BF16),
            pltpu.VMEM((rows, narrow), BF16),
            pltpu.VMEM((rows, narrow), BF16),
            pltpu.VMEM((rows, narrow), BF16),
            pltpu.VMEM((half, down, narrow), BF16),
            pltpu.VMEM((count, shard, side), BF16),
            pltpu.VMEM((count, shard, side), BF16),
            pltpu.VMEM((4 * count, shard, narrow), BF16),
            pltpu.VMEM((half, down, narrow), BF16),
            pltpu.VMEM((half, shard, side), BF16),
            pltpu.VMEM((half, shard, side), BF16),
            pltpu.VMEM((4 * half, shard, narrow), BF16),
            pltpu.VMEM((half - 1, down, narrow), BF16),
            pltpu.VMEM((half - 1, shard, side), BF16),
            pltpu.VMEM((half - 1, shard, side), BF16),
            pltpu.VMEM((4 * (half - 1), shard, narrow), BF16),
            pltpu.VMEM((2 * small_steps, 8, width), F32),
            pltpu.VMEM((PAIR, rows), F32),
            dma((17 + half,)),
            dma((4,)),
            dma((6,)),
            dma((6,)),
            dma((3,)),
            dma((parts * count,)),
            dma((parts * count,)),
            dma((2 * parts,)),
            dma((2 * parts,)),
            pltpu.SemaphoreType.REGULAR((2 * parts,)),
            dma((parts,)),
            dma((parts,)),
            dma((parts,)),
            dma((small_steps,)),
            dma((small_steps,)),
        ],
        compiler_params=pltpu.CompilerParams(
            collective_id=1, has_side_effects=True, vmem_limit_bytes=63 * 2**20
        ),
        cost_estimate=pl.CostEstimate(
            flops=4 * rows * width * (n + width + 3 * ff),
            bytes_accessed=80 * 2**20,
            transcendentals=0,
        ),
        name="backward",
    )(*operands)


def finish_body(lay, entries, small, *refs):
    count = (len(refs) - 4) // 2
    sources, targets = refs[:count], refs[count : 2 * count]
    gain_one, gain_two, first_norm, value_norm = refs[2 * count :]
    for source, target in zip(sources, targets):
        target[...] = source[...].astype(target.dtype)

    @pl.when(pl.program_id(0) == 0)
    def _():
        rows = gain_one.shape[0]
        at = pl.ds(pl.multiple_of(lax.axis_index("fsdp") * rows, rows), rows)
        gain_one[...] = small[0, at]
        gain_two[...] = small[1, at]
        first_norm[0, 0] = jnp.sum(small[2:3, :]) / entries
        value_norm[0, 0] = jnp.sum(small[3:4, :]) / entries


def finish_kernel(lay, results):
    output, grad_tokens, grad_first, *totals, small = results
    rows, width = output.shape
    moved = [output, grad_tokens, grad_first, *totals]
    kinds = [BF16, F32, F32] + [F32] * len(totals)

    steps = 2

    def spec(item):
        return pl.BlockSpec((item.shape[0] // steps, item.shape[1]), lambda i: (i, 0))

    shard = width // lay.fs
    line = pl.BlockSpec((shard,), lambda i: (0,))
    scalar = pl.BlockSpec((1, 1), lambda i: (0, 0), memory_space=pltpu.SMEM)
    done = pl.pallas_call(
        functools.partial(finish_body, lay, rows * width * lay.dp * lay.fs),
        grid=(steps,),
        in_specs=[pl.BlockSpec(small.shape, lambda i: (0, 0))] + [spec(item) for item in moved],
        out_specs=[spec(item) for item in moved] + [line, line, scalar, scalar],
        out_shape=[struct(item.shape, kind) for item, kind in zip(moved, kinds)]
        + [struct((shard,), F32)] * 2
        + [struct((1, 1), F32)] * 2,
        compiler_params=pltpu.CompilerParams(vmem_limit_bytes=63 * 2**20),
        cost_estimate=pl.CostEstimate(
            flops=0, bytes_accessed=30 * 2**20, transcendentals=0
        ),
        name="finish",
    )(small, *moved)
    output, grad_tokens, grad_first, qkv, out, gate, up, down, gain_one, gain_two, first, value = done
    return (
        output,
        grad_tokens,
        grad_first,
        gain_one,
        qkv,
        out,
        gain_two,
        gate,
        up,
        down,
        first.reshape(()),
        value.reshape(()),
    )


def body(
    lay,
    tokens,
    first_values,
    lengths,
    gain_one,
    w_qkv,
    w_out,
    gain_two,
    w_gate,
    w_up,
    w_down,
    cotangent,
):
    rows, width = tokens.shape
    tables = tuple(jnp.asarray(table) for table in rotary_tables(rows))
    results = forward_kernel(
        lay, lengths, tokens, first_values, tables, gain_one, gain_two, cotangent, w_qkv, w_out, w_gate, w_up, w_down
    )
    weights, heads, logs, saved, gains, sums = (
        results[:5],
        results[5:8],
        results[8],
        results[9:17],
        results[17],
        results[18],
    )
    results = backward_kernel(
        lay, lengths, tables, gains, sums, logs, weights, (*heads, *saved), tokens, cotangent
    )
    return finish_kernel(lay, results)


def solution(mesh):
    both = P(AXES, None)
    rows = P("fsdp", None)
    in_specs = (both, both, P(AXES), P("fsdp"), rows, rows, P("fsdp"), rows, rows, rows, both)
    out_specs = (both, both, both, P("fsdp"), rows, rows, P("fsdp"), rows, rows, rows, P(), P())
    lay = Layout(mesh.shape["dp"], mesh.shape["fsdp"])
    return jax.shard_map(
        functools.partial(body, lay),
        mesh=mesh,
        in_specs=in_specs,
        out_specs=out_specs,
        check_vma=False,
    )
```

```python
import functools
import math

import jax
import jax.numpy as jnp
import numpy as np
from jax import lax
from jax.experimental import pallas as pl
from jax.experimental.pallas import tpu as pltpu
from jax.sharding import PartitionSpec as P

HEAD_DIM = 64
PAIR = 2 * HEAD_DIM
TILE = 256
GAIN_ROWS = 16
norm_eps = 1e-06
F32 = jnp.float32
BF16 = jnp.bfloat16
AXES = ("dp", "fsdp")
ANY = pl.BlockSpec(memory_space=pl.ANY)


def dot_nn(a, b):
    return lax.dot_general(a, b, (((1,), (0,)), ((), ())), preferred_element_type=F32)


def dot_nt(a, b):
    return lax.dot_general(a, b, (((1,), (1,)), ((), ())), preferred_element_type=F32)


def dot_tn(a, b):
    return lax.dot_general(a, b, (((0,), (0,)), ((), ())), preferred_element_type=F32)


def rotary_tables(count):
    half = HEAD_DIM // 2
    frequency = np.exp(
        -(np.arange(half, dtype=np.float32) * np.float32(2.0) / np.float32(HEAD_DIM))
        * np.float32(math.log(10000.0))
    ).astype(np.float32)
    angles = np.arange(count, dtype=np.float32)[:, None] * frequency[None, :]
    cosine = np.cos(angles.astype(np.float64)).astype(np.float32)
    sine = np.sin(angles.astype(np.float64)).astype(np.float32)
    cosine = np.concatenate([cosine] * 4, axis=1)
    sine = np.concatenate([-sine, sine, -sine, sine], axis=1)
    return cosine, sine


def swap_halves(x):
    half = HEAD_DIM // 2
    lane = lax.broadcasted_iota(jnp.int32, x.shape, 1)
    up = pltpu.roll(x, PAIR - half, 1)
    down = pltpu.roll(x, half, 1)
    return jnp.where((lane % HEAD_DIM) < half, up, down)


class Layout:
    def __init__(self, dp, fs):
        self.dp, self.fs = dp, fs
        self.bits = fs.bit_length() - 1
        self.line = dp // 2


def add_low(a, b):
    return (a.astype(F32) + b.astype(F32)).astype(BF16)


def start(copies):
    for copy in copies:
        copy.start()


def wait(copies):
    for copy in copies:
        copy.wait()


def struct(shape, dtype):
    return jax.ShapeDtypeStruct(shape, dtype)


class Place:
    def __init__(self, lay):
        self.bits, self.count = lay.bits, lay.fs
        self.d, self.f = lax.axis_index("dp"), lax.axis_index("fsdp")
        self.c = lax.rem(self.d, 2)
        self.flips = []
        for i in range(self.bits):
            ahead, back = 1 << i, 1 << (self.bits - 1 - i)
            one = ahead * (1 - 2 * lax.rem(self.f // ahead, 2))
            two = back * (1 - 2 * lax.rem(self.f // back, 2))
            self.flips.append(one + self.c * (two - one))

    def shard(self, m):
        return self.f + sum(self.flips[i] for i in range(self.bits) if (m >> i) & 1)

    def partner(self, i):
        return (self.d, self.f + self.flips[i])

    def sibling(self):
        return (self.d + 1 - 2 * self.c, self.f)

    def above(self):
        return (self.d + 2 - 4 * lax.rem(self.d // 2, 2), self.f)

    def group(self):
        others = []
        for m in range(1, self.count):
            others.append((self.d, self.shard(m)))
        return others


def remote(src, dst, send, recv, device):
    return pltpu.make_async_remote_copy(
        src_ref=src,
        dst_ref=dst,
        send_sem=send,
        recv_sem=recv,
        device_id=device,
        device_id_type=pl.DeviceIdType.MESH,
    )


class Gather:
    def __init__(self, place, own, full, first, total, lifted, sems, slot):
        self.place = place
        send, recv, up_send, up_recv, cross_send, cross_recv, more_send, more_recv = sems
        count = place.count
        rows, side = own.shape[0], total // 2
        column = pl.ds(pl.multiple_of(first + place.c * side, 128), side)
        size = rows // 2 if lifted else rows
        parity = lax.rem(place.d // 2, 2) if lifted else 0
        self.link, self.up, self.cross, self.more = [None], [None], [None], [None]

        def spot(piece, which):
            at = pl.multiple_of(place.shard(piece) * rows + which * size, size)
            return full.at[pl.ds(at, size), column]

        for m in range(1, count):
            step = m.bit_length() - 1
            before = m - (1 << step)
            source = spot(before, parity)
            if before == 0:
                source = own.at[pl.ds(pl.multiple_of(parity * size, size), size), column]
            at = slot * count + m
            self.link.append(
                remote(source, spot(before, parity), send.at[at], recv.at[at], place.partner(step))
            )
            here = spot(m, parity)
            self.cross.append(
                remote(here, here, cross_send.at[at], cross_recv.at[at], place.sibling())
            )
            if lifted:
                there = spot(m, 1 - parity)
                self.up.append(remote(here, here, up_send.at[at], up_recv.at[at], place.above()))
                self.more.append(
                    remote(there, there, more_send.at[at], more_recv.at[at], place.sibling())
                )

    def begin(self, m):
        self.link[m].start()

    def arrived(self, m):
        self.link[m].wait_recv()
        for i in range(m.bit_length(), self.place.bits):
            self.link[m + (1 << i)].start()
        self.cross[m].start()

    def lift(self, m):
        self.up[m].start()

    def landed(self, m):
        self.up[m].wait_recv()
        self.more[m].start()

    def complete(self):
        for copy in self.cross[1:] + self.more[1:]:
            copy.wait_recv()

    def drain(self):
        for copy in self.link[1:] + self.cross[1:] + self.up[1:] + self.more[1:]:
            copy.wait_send()


QK, V, OUT, GATE, UP, DOWN = range(6)
BEGIN, ARRIVE, LIFT, LAND = range(4)
NORMALISE, QUERIES, KEYS, VALUES, HEADS, PROJECT, GATES, UPS, SUM_DOWN = range(4, 13)
FORWARD_LIFTED = (QK, V, GATE, DOWN)
FORWARD_ORDER = (
    (BEGIN, QK, 1), (BEGIN, QK, 2), (BEGIN, V, 1), (BEGIN, V, 2), (BEGIN, GATE, 1),
    (NORMALISE, 0, 0), (ARRIVE, QK, 1), (ARRIVE, QK, 2), (LIFT, QK, 1), (LIFT, QK, 2),
    (ARRIVE, V, 1), (BEGIN, GATE, 2), (ARRIVE, V, 2), (ARRIVE, GATE, 1), (BEGIN, OUT, 1),
    (ARRIVE, QK, 3), (LIFT, QK, 3), (LAND, QK, 1), (LIFT, V, 1), (BEGIN, UP, 1), (ARRIVE, V, 3),
    (BEGIN, OUT, 2), (LIFT, V, 2), (LAND, QK, 2), (ARRIVE, OUT, 1), (BEGIN, DOWN, 1), (LIFT, V, 3),
    (LAND, QK, 3), (QUERIES, 0, 0), (ARRIVE, GATE, 2), (LAND, V, 1), (KEYS, 0, 0), (LIFT, GATE, 1),
    (LAND, V, 2), (LIFT, GATE, 2), (ARRIVE, OUT, 2), (LAND, V, 3), (VALUES, 0, 0), (BEGIN, UP, 2),
    (HEADS, 0, 0), (ARRIVE, UP, 1), (ARRIVE, GATE, 3), (HEADS, 0, 0), (LAND, GATE, 1),
    (LIFT, GATE, 3), (ARRIVE, OUT, 3), (BEGIN, DOWN, 2), (HEADS, 0, 0), (ARRIVE, DOWN, 1),
    (LAND, GATE, 2), (HEADS, 0, 0), (LIFT, DOWN, 1), (PROJECT, 0, 0), (LAND, GATE, 3),
    (ARRIVE, UP, 2), (GATES, 0, 0), (ARRIVE, UP, 3), (ARRIVE, DOWN, 2), (LIFT, DOWN, 2),
    (UPS, 0, 0), (ARRIVE, DOWN, 3), (LIFT, DOWN, 3), (LAND, DOWN, 1), (UPS, 0, 1), (LAND, DOWN, 2),
    (SUM_DOWN, 0, 0), (LAND, DOWN, 3),
)


def forward_body(
    lay,
    lengths,
    in_tokens,
    in_first,
    in_cosine,
    in_sine,
    gain_one_in,
    gain_two_in,
    cotangent,
    in_qkv,
    in_out,
    in_gate,
    in_up,
    in_down,
    full_qkv,
    full_out,
    full_gate,
    full_up,
    full_down,
    out_q,
    out_k,
    out_v,
    logs,
    hidden_one2,
    attended2,
    hidden_two2,
    out_after,
    out_gate,
    out_up,
    out_product,
    grad_down,
    gains,
    sums,
    w_qkv,
    w_out,
    w_gate,
    w_up,
    tokens,
    first,
    cosine,
    sine,
    gain_in,
    gain,
    hidden,
    queries,
    keys,
    values,
    attended,
    after,
    gate_pre,
    low_gate,
    low_up,
    product2,
    cot2,
    grad_low,
    turned,
    send,
    recv,
    up_send,
    up_recv,
    cross_send,
    cross_recv,
    more_send,
    more_recv,
    local,
    gain_send,
    gain_recv,
    swap_send,
    swap_recv,
    write,
):
    place = Place(lay)
    count, c = place.count, place.c
    rows, width = tokens.shape
    shard_rows = in_qkv.shape[0]
    ff = in_gate.shape[1]
    sibling = place.sibling()

    barrier = pltpu.get_barrier_semaphore()
    begins = []
    for i, (source, target) in enumerate(
        ((in_tokens, tokens), (in_cosine, cosine), (in_sine, sine), (in_first, first))
    ):
        begins.append(pltpu.make_async_copy(source, target, local.at[10 + i]))
    start(begins)
    known = [sibling, place.above()] + place.group()
    for device in known:
        pl.semaphore_signal(barrier, inc=1, device_id=device, device_id_type=pl.DeviceIdType.MESH)
    pl.semaphore_wait(barrier, len(known))

    sems = (send, recv, up_send, up_recv, cross_send, cross_recv, more_send, more_recv)

    def gather(who, own, full, first_column, total):
        return Gather(place, own, full, first_column, total, who in FORWARD_LIFTED, sems, who)

    gathers = {
        QK: gather(QK, in_qkv, w_qkv, 0, 2 * width),
        V: gather(V, in_qkv, w_qkv, 2 * width, width),
        OUT: gather(OUT, in_out, w_out, 0, width),
        GATE: gather(GATE, in_gate, w_gate, 0, ff),
        UP: gather(UP, in_up, w_up, 0, ff),
        DOWN: gather(DOWN, in_down, full_down, 0, width),
    }

    seen = {}

    def link(step):
        kind, who, turn = step
        one = gathers[who]
        if kind == BEGIN:
            firsts = [1 << i for i in range(place.bits)]
            for m in firsts[turn - 1 : turn] if count == 4 else firsts * (turn == 1):
                one.begin(m)
            return
        if count == 4:
            pieces = [turn]
        else:
            done = seen[who, kind] = seen.get((who, kind), 0) + 1
            pieces = range(1 + (done - 1) * (count - 1) // 3, 1 + done * (count - 1) // 3)
        for m in pieces:
            {ARRIVE: one.arrived, LIFT: one.lift, LAND: one.landed}[kind](m)

    gain_in[...] = jnp.zeros(gain_in.shape, BF16)
    gain_in[0:1, :] = gain_one_in[...].reshape(1, shard_rows)
    gain_in[1:2, :] = gain_two_in[...].reshape(1, shard_rows)
    gain_at = pl.multiple_of(place.f * shard_rows, shard_rows)
    gain_copies = []
    for m, device in enumerate(place.group()):
        gain_copies.append(
            remote(
                gain_in,
                gain.at[:, pl.ds(gain_at, shard_rows)],
                gain_send.at[m],
                gain_recv.at[m],
                device,
            )
        )
    gain_own = pltpu.make_async_copy(
        gain_in, gain.at[:, pl.ds(gain_at, shard_rows)], local.at[4]
    )
    start(gain_copies + [gain_own])
    order = list(FORWARD_ORDER)
    while order[0][0] == BEGIN:
        link(order.pop(0))
    own_rows = pl.ds(gain_at, shard_rows)
    locals_of = {}
    for slot, (name, source, full) in enumerate(
        ((QK, in_qkv, w_qkv), (OUT, in_out, w_out), (GATE, in_gate, w_gate), (UP, in_up, w_up))
    ):
        locals_of[name] = pltpu.make_async_copy(source, full.at[own_rows, :], local.at[slot])
        locals_of[name].start()
    half = width // 2
    down_rows = in_down.shape[0]
    down_at = pl.ds(pl.multiple_of(place.f * down_rows, down_rows), down_rows)
    down_in, down_out = [], []
    for i in range(2):
        stage = grad_low.at[pl.ds(i * down_rows, down_rows), :]
        side = pl.ds(i * half, half)
        down_in.append(pltpu.make_async_copy(in_down.at[:, side], stage, local.at[6 + i]))
        down_out.append(pltpu.make_async_copy(stage, full_down.at[down_at, side], local.at[8 + i]))
    start(down_in)

    writes = []

    def put(source, target):
        copy = pltpu.make_async_copy(source, target, write.at[len(writes)])
        copy.start()
        writes.append(copy)

    swaps = []

    def swap(source, target):
        slot = len(swaps)
        copy = remote(source, target, swap_send.at[slot], swap_recv.at[slot], sibling)
        copy.start()
        swaps.append(copy)
        return copy

    def share(source, target):
        put(source, target.at[pl.ds(0, rows), :])
        return swap(source, target.at[pl.ds(rows, rows), :])

    theirs = pl.multiple_of((1 - c) * half, 128)
    ours = pl.multiple_of(c * half, 128)
    cot_swap = swap(cotangent.at[:, pl.ds(theirs, half)], cot2.at[pl.ds(rows, rows), :])
    cot_own = pltpu.make_async_copy(
        cotangent.at[:, pl.ds(ours, half)], cot2.at[pl.ds(0, rows), :], local.at[5]
    )
    cot_own.start()

    block = min(TILE, rows)
    length = lengths[0]
    pairs = width // PAIR
    hidden_two = low_up.at[:, pl.ds(0, width)]
    two_swap, two_put, product_swaps = [], [], []

    def by_rows(step):
        @pl.loop(0, rows // block)
        def _(i):
            step(pl.ds(pl.multiple_of(i * block, block), block))

    def normalise():
        begins[0].wait()
        inputs = tokens[...].astype(F32)
        inverse = lax.rsqrt(jnp.mean(inputs * inputs, axis=-1, keepdims=True) + norm_eps)
        for copy in gain_copies:
            copy.wait_recv()
        gain_own.wait()
        gains[0:1, :] = gain[0:1, :].astype(F32)
        gains[1:2, :] = gain[1:2, :].astype(F32)
        gains[2:8, :] = jnp.zeros((6, width), F32)
        hidden[...] = (inputs * inverse * gains[0:1, :]).astype(BF16)
        share(hidden, hidden_one2)
        wait(down_in)
        start(down_out)
        sums[...] = jnp.zeros(sums.shape, F32)
        logs[...] = jnp.zeros(logs.shape, F32)

    def rotated(which, out, scale):
        def step(at):
            cos, sin = cosine[at, :], sine[at, :]
            raw = dot_nn(hidden[at, :], w_qkv[:, which * width : (which + 1) * width])
            for p in range(width // PAIR):
                x = raw[:, p * PAIR : (p + 1) * PAIR]
                low = (x * cos + swap_halves(x) * sin).astype(BF16)
                out[at, p * PAIR : (p + 1) * PAIR] = low * jnp.asarray(scale, BF16)

        by_rows(step)

    def mix(at):
        raw = dot_nn(hidden[at, :], w_qkv[:, 2 * width : 3 * width])
        kept = first[at, :].astype(F32)
        mixed = 0.5 * raw + 0.5 * kept
        values[at, :] = mixed.astype(BF16)
        sums[0:1, :] += jnp.sum(kept * kept, axis=0, keepdims=True)
        sums[1:2, :] += jnp.sum(mixed * mixed, axis=0, keepdims=True)

    turn = 2

    def attend(links):
        @pl.loop(0, pairs // turn)
        def _(i):
            for j in range(turn):
                attend_pair(i * turn + j, turned.at[j])
            for after_turn, steps in enumerate(links):
                if steps:

                    @pl.when(i == after_turn)
                    def _():
                        for step in steps:
                            link(step)

    def attend_pair(p, turned):
        at = pl.ds(pl.multiple_of(p * PAIR, PAIR), PAIR)
        q, k = queries[:, at], keys[:, at]
        v_t = values[:, at].T
        lane = lax.broadcasted_iota(jnp.int32, (rows, PAIR), 1)
        for head in range(2):
            inside = (lane // HEAD_DIM) == head
            k_head = jnp.where(inside, k, jnp.zeros_like(k))
            v_head = v_t[head * HEAD_DIM : (head + 1) * HEAD_DIM]
            for b in range(rows // block):
                upto = (b + 1) * block
                scores = dot_nt(k_head[:upto], q[b * block : upto])
                key = lax.broadcasted_iota(jnp.int32, scores.shape, 0)
                query = lax.broadcasted_iota(jnp.int32, (1, block), 1) + b * block
                allowed = key <= jnp.minimum(query, length - 1)
                scores = jnp.where(allowed, scores, -1e30)
                peak = jnp.max(scores, axis=0, keepdims=True)
                expo = jnp.exp(scores - peak)
                total = jnp.sum(expo, axis=0, keepdims=True)
                logs[p, head : head + 1, b * block : upto] = peak + jnp.log(total)
                out = dot_nn(v_head[:, :upto], expo.astype(BF16)) * (1.0 / total)
                turned[head * HEAD_DIM : (head + 1) * HEAD_DIM, b * block : upto] = out
        attended[:, at] = turned[...].T.astype(BF16)

    def project(at):
        x = tokens[at, :].astype(F32) + dot_nn(attended[at, :], w_out[...])
        after[at, :] = x
        scale = lax.rsqrt(jnp.mean(x * x, axis=-1, keepdims=True) + norm_eps)
        low_up[at, 0:width] = (x * scale * gains[1:2, :]).astype(BF16)

    def gate_rows(at):
        gate_pre[at, :] = dot_nn(low_up[at, 0:width], w_gate[...])
        low_gate[at, :] = gate_pre[at, :].astype(BF16)

    def up_rows(at):
        up_proj = dot_nn(low_up[at, 0:width], w_up[...])
        gate_of = gate_pre[at, :]
        product2[at, :] = (gate_of * jax.nn.sigmoid(gate_of) * up_proj).astype(BF16)
        low_up[at, :] = up_proj.astype(BF16)

    def compute(kind, part):
        if kind == NORMALISE:
            normalise()
        elif kind == QUERIES:
            wait(begins[1:])
            locals_of[QK].wait()
            gathers[QK].complete()
            rotated(0, queries, HEAD_DIM**-0.5)
            put(queries, out_q)
        elif kind == KEYS:
            rotated(1, keys, 1.0)
            put(keys, out_k)
        elif kind == VALUES:
            gathers[V].complete()
            put(w_qkv, full_qkv)
            by_rows(mix)
            put(values, out_v)
        elif kind == PROJECT:
            share(attended, attended2)
            locals_of[OUT].wait()
            gathers[OUT].complete()
            put(w_out, full_out)
            by_rows(project)
            put(after, out_after)
            two_swap.append(share(hidden_two, hidden_two2))
            two_put.append(writes[-1])
        elif kind == GATES:
            locals_of[GATE].wait()
            gathers[GATE].complete()
            put(w_gate, full_gate)
            by_rows(gate_rows)
            put(low_gate, out_gate)
        elif kind == UPS and part == 0:
            locals_of[UP].wait()
            gathers[UP].complete()
            put(w_up, full_up)
            two_swap[0].wait_send()
            two_put[0].wait()
            steps = []
            while order[0][0] <= LAND:
                steps.append(order.pop(0))
            up_parts(steps)
        elif kind == UPS:
            put(low_up, out_up)
            put(product2.at[pl.ds(0, rows), :], out_product)
        else:
            wait(down_out)
            cot_own.wait()
            cot_swap.wait_recv()
            for copy in product_swaps:
                copy.wait_recv()

            @pl.loop(0, ff // TILE)
            def _(i):
                at = pl.ds(pl.multiple_of(i * TILE, TILE), TILE)
                grad_low[at, :] = dot_tn(product2[:, at], cot2[...]).astype(BF16)

            put(grad_low, grad_down)

    def up_parts(steps):
        size = rows // 2
        for i in range(2):
            part = pl.ds(i * size, size)
            there = pl.ds(rows + i * size, size)
            slot = len(swaps)
            copy = remote(
                product2.at[part, :], product2.at[there, :], swap_send.at[slot], swap_recv.at[slot], sibling
            )
            swaps.append(copy)
            product_swaps.append(copy)

        @pl.loop(0, 2)
        def _(i):
            up_rows(pl.ds(pl.multiple_of(i * size, size), size))

            @pl.when(i == 0)
            def _():
                product_swaps[0].start()
                for step in steps:
                    link(step)

            @pl.when(i == 1)
            def _():
                product_swaps[1].start()

    while order:
        step = order.pop(0)
        if step[0] <= LAND:
            link(step)
        elif step[0] == HEADS:
            turns = pairs // turn
            links, at = [[] for _ in range(4)], 0
            while order and (order[0][0] <= LAND or order[0][0] == HEADS):
                if order[0][0] == HEADS:
                    order.pop(0)
                    at += 1
                else:
                    links[at].append(order.pop(0))
            spread = [[] for _ in range(turns)]
            for i, steps in enumerate(links):
                spread[(i + 1) * turns // 4 - 1] += steps
            attend(spread)
        else:
            compute(step[0], step[2])

    gathers[DOWN].complete()
    for one in gathers.values():
        one.drain()
    for copy in gain_copies:
        copy.wait_send()
    waited = [cot_swap, *product_swaps]
    for copy in swaps:
        if not any(copy is item for item in waited):
            copy.wait_recv()
        if copy is not two_swap[0]:
            copy.wait_send()
    for copy in writes:
        if copy is not two_put[0]:
            copy.wait()


def forward_kernel(lay, lengths, tokens, first, tables, gain_one, gain_two, cotangent, w_qkv, w_out, w_gate, w_up, w_down):
    count = lay.fs
    rows, width = tokens.shape
    n, ff = w_qkv.shape[1], w_gate.shape[1]
    half = width // 2
    pairs = width // PAIR
    big = struct((rows, width), BF16)
    wide = struct((rows, ff), BF16)
    two = struct((2 * rows, width), BF16)
    dma = pltpu.SemaphoreType.DMA
    vmem = pl.BlockSpec(memory_space=pltpu.VMEM)
    weights = [(width, n), (width, width), (width, ff), (width, ff), (ff, width)]
    out_shape = (
        [struct(shape, BF16) for shape in weights]
        + [big, big, big, struct((pairs, 8, rows), F32)]
        + [two, two, two, struct((rows, width), F32), wide, wide, wide]
        + [struct((ff, half), BF16), struct((8, width), F32), struct((8, width), F32)]
    )
    out_specs = [ANY] * 8 + [vmem] + [ANY] * 8 + [vmem, vmem]
    return pl.pallas_call(
        functools.partial(forward_body, lay),
        in_specs=[pl.BlockSpec(memory_space=pltpu.SMEM)] + [ANY] * 4 + [vmem] * 2 + [ANY] * 6,
        out_specs=out_specs,
        out_shape=out_shape,
        scratch_shapes=[
            pltpu.VMEM((width, n), BF16),
            pltpu.VMEM((width, width), BF16),
            pltpu.VMEM((width, ff), BF16),
            pltpu.VMEM((width, ff), BF16),
            pltpu.VMEM((rows, width), BF16),
            pltpu.VMEM((rows, width), BF16),
            pltpu.VMEM((rows, PAIR), F32),
            pltpu.VMEM((rows, PAIR), F32),
            pltpu.VMEM((GAIN_ROWS, width // count), BF16),
            pltpu.VMEM((GAIN_ROWS, width), BF16),
            pltpu.VMEM((rows, width), BF16),
            pltpu.VMEM((rows, width), BF16),
            pltpu.VMEM((rows, width), BF16),
            pltpu.VMEM((rows, width), BF16),
            pltpu.VMEM((rows, width), BF16),
            pltpu.VMEM((rows, width), F32),
            pltpu.VMEM((rows, ff), F32),
            pltpu.VMEM((rows, ff), BF16),
            pltpu.VMEM((rows, ff), BF16),
            pltpu.VMEM((2 * rows, ff), BF16),
            pltpu.VMEM((2 * rows, half), BF16),
            pltpu.VMEM((ff, half), BF16),
            pltpu.VMEM((2, PAIR, rows), F32),
            *[dma((6 * count,))] * 8,
            dma((14,)),
            dma((count - 1,)),
            dma((count - 1,)),
            dma((6,)),
            dma((6,)),
            dma((16,)),
        ],
        compiler_params=pltpu.CompilerParams(
            collective_id=0, has_side_effects=True, vmem_limit_bytes=62 * 2**20
        ),
        cost_estimate=pl.CostEstimate(
            flops=2 * rows * width * (n + width + 3 * ff),
            bytes_accessed=60 * 2**20,
            transcendentals=0,
        ),
        name="forward",
    )(lengths, tokens, first, *tables, gain_one, gain_two, cotangent, w_qkv, w_out, w_gate, w_up, w_down)


def rms_back(grad, normed, inverse):
    return inverse * (grad - normed * jnp.mean(grad * normed, axis=-1, keepdims=True))


class Line:
    def __init__(self, lay, place):
        size = lay.line
        r = place.d // 2
        self.half = size // 2
        upper = r // self.half
        toward = 1 - 2 * upper
        self.depth = r * toward + upper * (size - 1)
        self.next = (place.d + 2 * toward, place.f)
        self.prev = (place.d - 2 * toward, place.f)
        self.middle = self.depth == self.half - 1
        self.inner = self.depth > 0
        self.others = []
        reach = 1
        while reach < size:
            self.others.append((place.d + 2 * reach * (1 - 2 * lax.rem(r // reach, 2)), place.f))
            reach *= 2


def signal(sem, device):
    pl.semaphore_signal(sem, inc=1, device_id=device, device_id_type=pl.DeviceIdType.MESH)


class Reduce:
    def __init__(
        self, place, line, slot, window, held, sources, first, later, final, column, sems
    ):
        send, recv, z_send, z_recv, credit, f_local, f_send, f_recv = sems
        self.place, self.line, self.held, self.window = place, line, held, window
        self.bits, count = place.bits, place.count
        self.count = count
        base = slot * count
        half = count // 2
        self.steps, self.lands = [], []
        at = 0
        for i in range(self.bits):
            blocks = count >> (i + 1)
            copies, lands = [], []
            for q in range(blocks):
                source = sources[q] if i == 0 else held.at[blocks + q, window]
                land = first.at[q, window] if i == 0 else later.at[at + q, window]
                index = base + q if i == 0 else base + half + at + q
                lands.append(land)
                copies.append(remote(source, land, send.at[index], recv.at[index], place.partner(i)))
            if i > 0:
                at += blocks
            self.steps.append(copies)
            self.lands.append(lands)
        mine, inner, outer = held.at[0, window], first.at[0, window], first.at[1, window]
        two = 2 * slot
        self.hops = {
            "in": remote(mine, inner, z_send.at[two], z_recv.at[two], line.next),
            "middle": remote(mine, outer, z_send.at[two], z_recv.at[two + 1], line.next),
            "back": remote(inner, outer, z_send.at[two + 1], z_recv.at[two + 1], line.prev),
            "out": remote(outer, outer, z_send.at[two + 1], z_recv.at[two + 1], line.prev),
        }
        self.mine, self.inner, self.outer = mine, inner, outer
        spot = final.at[window, column]
        self.ends = []
        for source in (inner, outer):
            self.ends.append(
                (
                    pltpu.make_async_copy(source, spot, f_local.at[slot]),
                    remote(source, spot, f_send.at[slot], f_recv.at[slot], place.sibling()),
                )
            )
        self.from_next, self.from_prev = credit.at[two], credit.at[two + 1]

    def begin(self, q):
        self.steps[0][q].start()

    def block(self, i, q):
        blocks = self.count >> (i + 1)
        self.steps[i][q].wait_recv()
        here = self.held.at[q, self.window]
        here[...] = add_low(here[...], self.lands[i][q][...])
        if i + 1 < self.bits and q >= blocks // 2:
            self.steps[i + 1][q - blocks // 2].start()

    def leaving(self):
        half = self.count // 2
        for q in reversed(range(half // 2, half)):
            self.block(0, q)

    def staying(self):
        for q in reversed(range(self.count // 4)):
            self.block(0, q)
        line = self.line

        @pl.when(line.middle)
        def _():
            signal(self.from_next, line.next)

        @pl.when(jnp.logical_not(line.middle))
        def _():
            signal(self.from_prev, line.next)

        @pl.when(line.inner)
        def _():
            signal(self.from_next, line.prev)

    def rest(self):
        for i in range(1, self.bits):
            for q in reversed(range(self.count >> (i + 1))):
                self.block(i, q)

        @pl.when(jnp.logical_not(self.line.inner))
        def _():
            self.onward()

    def onward(self):
        line = self.line
        pl.semaphore_wait(self.from_next, 1)

        @pl.when(line.middle)
        def _():
            self.hops["middle"].start()

        @pl.when(jnp.logical_not(line.middle))
        def _():
            self.hops["in"].start()

    def inward(self):
        @pl.when(self.line.inner)
        def _():
            self.hops["in"].wait_recv()
            self.mine[...] = add_low(self.mine[...], self.inner[...])
            self.onward()

    def finish(self, which):
        local, cross = self.ends[which]
        local.start()
        cross.start()

    def across(self):
        line = self.line

        @pl.when(line.middle)
        def _():
            self.hops["middle"].wait_recv()
            self.inner[...] = add_low(self.mine[...], self.outer[...])

            @pl.when(line.inner)
            def _():
                pl.semaphore_wait(self.from_prev, 1)
                self.hops["back"].start()

            self.finish(0)

    def outward(self):
        line = self.line
        if line.half == 1:
            return

        @pl.when(jnp.logical_not(line.middle))
        def _():
            self.hops["out"].wait_recv()

            @pl.when(line.inner)
            def _():
                pl.semaphore_wait(self.from_prev, 1)
                self.hops["out"].start()

            self.finish(1)

    def drain(self):
        for copies in self.steps:
            for copy in copies:
                copy.wait_send()
        self.hops["in"].wait_send()

        @pl.when(self.line.inner)
        def _():
            self.hops["out"].wait_send()

        local, cross = self.ends[0]
        local.wait()
        cross.wait_send()
        cross.wait_recv()


W_DOWN, W_GATE, W_UP, W_OUT, W_V, W_K, W_Q = range(7)
BACKWARD_PARTS = (2, 2, 4, 2, 2, 2, 2)
LEAVING, STAYING, REST, INWARD, ACROSS, OUTWARD, SMALL = range(7)
BLOCKS, MLP_TILES, NORM_TWO, ATTEND_GRAD, HEAD_PAIRS, QKV_TILES, NORM_ONE = range(7, 14)
BACKWARD_ORDER = (
    (LEAVING, W_DOWN, 0), (STAYING, W_DOWN, 0), (BLOCKS, W_GATE, 3), (BLOCKS, W_GATE, 2),
    (LEAVING, W_DOWN, 1), (BLOCKS, W_GATE, 1), (REST, W_DOWN, 0), (BLOCKS, W_GATE, 0),
    (BLOCKS, W_UP, 3), (BLOCKS, W_UP, 2), (BLOCKS, W_UP, 1), (BLOCKS, W_UP, 0),
    (STAYING, W_DOWN, 1), (MLP_TILES, 0, 0), (REST, W_DOWN, 1), (INWARD, W_DOWN, 0),
    (LEAVING, W_GATE, 0), (MLP_TILES, 0, 1), (MLP_TILES, 0, 2), (MLP_TILES, 0, 3),
    (LEAVING, W_GATE, 1), (NORM_TWO, 0, 0), (INWARD, W_DOWN, 1), (ACROSS, W_DOWN, 0),
    (ATTEND_GRAD, 0, 0), (STAYING, W_GATE, 0), (REST, W_GATE, 0), (BLOCKS, W_OUT, 3),
    (BLOCKS, W_OUT, 2), (BLOCKS, W_OUT, 1), (BLOCKS, W_OUT, 0), (HEAD_PAIRS, 0, 0),
    (STAYING, W_GATE, 1), (REST, W_GATE, 1), (HEAD_PAIRS, 0, 1), (LEAVING, W_UP, 0),
    (LEAVING, W_UP, 1), (INWARD, W_GATE, 0), (ACROSS, W_DOWN, 1), (OUTWARD, W_DOWN, 0),
    (HEAD_PAIRS, 0, 2), (LEAVING, W_UP, 2), (HEAD_PAIRS, 0, 3), (LEAVING, W_UP, 3),
    (HEAD_PAIRS, 0, 4), (INWARD, W_GATE, 1), (HEAD_PAIRS, 0, 5), (ACROSS, W_GATE, 0),
    (STAYING, W_UP, 0), (REST, W_UP, 0), (OUTWARD, W_DOWN, 1), (HEAD_PAIRS, 0, 6),
    (STAYING, W_UP, 1), (REST, W_UP, 1), (HEAD_PAIRS, 0, 7), (INWARD, W_UP, 0), (ACROSS, W_GATE, 1),
    (STAYING, W_UP, 2), (LEAVING, W_OUT, 0), (REST, W_UP, 2), (STAYING, W_UP, 3), (REST, W_UP, 3),
    (LEAVING, W_OUT, 1), (OUTWARD, W_GATE, 0), (INWARD, W_UP, 1), (BLOCKS, W_V, 3),
    (BLOCKS, W_V, 2), (BLOCKS, W_V, 1), (STAYING, W_OUT, 0), (BLOCKS, W_V, 0), (REST, W_OUT, 0),
    (ACROSS, W_UP, 0), (BLOCKS, W_K, 3), (BLOCKS, W_K, 2), (INWARD, W_UP, 2), (STAYING, W_OUT, 1),
    (BLOCKS, W_K, 1), (REST, W_OUT, 1), (BLOCKS, W_K, 0), (LEAVING, W_V, 0), (ACROSS, W_UP, 1),
    (OUTWARD, W_GATE, 1), (BLOCKS, W_Q, 3), (LEAVING, W_V, 1), (INWARD, W_UP, 3), (BLOCKS, W_Q, 2),
    (BLOCKS, W_Q, 1), (BLOCKS, W_Q, 0), (QKV_TILES, 0, 0), (INWARD, W_OUT, 0), (ACROSS, W_UP, 2),
    (STAYING, W_V, 0), (REST, W_V, 0), (OUTWARD, W_UP, 0), (QKV_TILES, 0, 1), (INWARD, W_OUT, 1),
    (ACROSS, W_UP, 3), (LEAVING, W_K, 0), (STAYING, W_V, 1), (REST, W_V, 1), (OUTWARD, W_UP, 1),
    (QKV_TILES, 0, 2), (LEAVING, W_K, 1), (INWARD, W_V, 0), (ACROSS, W_OUT, 0), (QKV_TILES, 0, 3),
    (ACROSS, W_OUT, 1), (INWARD, W_V, 1), (STAYING, W_K, 0), (REST, W_K, 0), (OUTWARD, W_UP, 2),
    (NORM_ONE, 0, 0), (LEAVING, W_Q, 0), (ACROSS, W_V, 0), (LEAVING, W_Q, 1), (STAYING, W_K, 1),
    (REST, W_K, 1), (INWARD, W_K, 0), (ACROSS, W_V, 1), (OUTWARD, W_UP, 3), (OUTWARD, W_OUT, 0),
    (SMALL, 0, 1), (STAYING, W_Q, 0), (OUTWARD, W_OUT, 1), (REST, W_Q, 0), (SMALL, 0, 2),
    (STAYING, W_Q, 1), (INWARD, W_K, 1), (REST, W_Q, 1), (ACROSS, W_K, 0), (OUTWARD, W_V, 0),
    (SMALL, 0, 3), (INWARD, W_Q, 0), (OUTWARD, W_V, 1), (SMALL, 0, 4), (ACROSS, W_K, 1),
    (INWARD, W_Q, 1), (OUTWARD, W_K, 0), (SMALL, 0, 5), (ACROSS, W_Q, 0), (OUTWARD, W_K, 1),
    (ACROSS, W_Q, 1), (OUTWARD, W_Q, 0), (OUTWARD, W_Q, 1),
)


def backward_body(
    lay,
    lengths,
    in_cosine,
    in_sine,
    gains,
    sums,
    in_logs,
    full_qkv,
    full_out,
    full_gate,
    full_up,
    full_down,
    in_q,
    in_k,
    in_v,
    hidden_one2,
    attended2,
    hidden_two2,
    in_after,
    in_gate,
    in_up,
    in_product,
    in_grad_down,
    tokens,
    cotangent,
    output,
    grad_tokens,
    grad_first,
    sum_qkv,
    sum_out,
    sum_gate,
    sum_up,
    sum_down,
    small,
    cosine,
    sine,
    logs,
    gate,
    up,
    product,
    ring,
    w_out,
    one,
    two,
    three,
    cot,
    left,
    right,
    low,
    attend_grad,
    gate_sib,
    up_sib,
    low_sib,
    q_sib,
    k_sib,
    v_sib,
    held_down,
    held_gate,
    held_up,
    held_narrow,
    first_down,
    first_gate,
    first_up,
    first_narrow,
    later_down,
    later_gate,
    later_up,
    later_narrow,
    small_land,
    turned,
    load_sem,
    ring_sem,
    swap_send,
    swap_recv,
    write_sem,
    send,
    recv,
    z_send,
    z_recv,
    credit,
    f_local,
    f_send,
    f_recv,
    small_send,
    small_recv,
):
    place = Place(lay)
    line = Line(lay, place)
    count, c = place.count, place.c
    sibling = place.sibling()
    rows, width = cot.shape
    ff = gate.shape[1]
    side, narrow = ff // 2, width // 2
    block = min(TILE, rows)
    bits = place.bits

    barrier = pltpu.get_barrier_semaphore()
    partners = [place.partner(i) for i in range(bits)]
    known = [sibling] + partners + line.others + [line.next]
    for device in known:
        signal(barrier, device)

    @pl.when(line.inner)
    def _():
        signal(barrier, line.prev)
        pl.semaphore_wait(barrier, len(known) + 1)

    @pl.when(jnp.logical_not(line.inner))
    def _():
        pl.semaphore_wait(barrier, len(known))

    loads = {}

    def load(name, source, target):
        copy = pltpu.make_async_copy(source, target, load_sem.at[len(loads)])
        copy.start()
        loads[name] = copy

    writes = []

    def put(source, target):
        copy = pltpu.make_async_copy(source, target, write_sem.at[len(writes)])
        copy.start()
        writes.append(copy)
        return copy

    swaps = []

    def swap(source, target, begin=True):
        slot = len(swaps)
        copy = remote(source, target, swap_send.at[slot], swap_recv.at[slot], sibling)
        if begin:
            copy.start()
        swaps.append(copy)
        return copy

    def shard_of(p):
        m = sum(((p >> i) & 1) << (bits - 1 - i) for i in range(bits))
        return place.shard(m)

    sems = (send, recv, z_send, z_recv, credit, f_local, f_send, f_recv)
    half = count // 2
    down_rows = in_grad_down.shape[0] // count
    shard_rows = sum_qkv.shape[0]

    def down_block(p, window=None):
        at = pl.multiple_of(shard_of(p) * down_rows, down_rows)
        if window is None:
            return in_grad_down.at[pl.ds(at, down_rows), :]
        return in_grad_down.at[pl.ds(at + window.start, window.size), :]

    reduces = {}

    def reduce_of(name, held, first, later, final, offset, size):
        parts = BACKWARD_PARTS[name]
        part_rows = held.shape[1] // parts
        for part in range(parts):
            window = pl.ds(part * part_rows, part_rows)
            if name == W_DOWN:
                sources = [down_block(half + q, window) for q in range(half)]
            else:
                sources = [held.at[half + q, window] for q in range(half)]
            column = pl.ds(pl.multiple_of(offset + c * size, 128), size)
            reduces[name, part] = Reduce(
                place, line, len(reduces), window, held, sources, first, later, final, column, sems
            )

    def narrow_of(index, name, final, offset):
        at = index * count
        reduce_of(
            name,
            held_narrow.at[pl.ds(at, count)],
            first_narrow.at[pl.ds(index * half, half)],
            later_narrow.at[pl.ds(index * (half - 1), half - 1)],
            final,
            offset,
            narrow,
        )

    reduce_of(W_DOWN, held_down, first_down, later_down, sum_down, 0, narrow)
    reduce_of(W_GATE, held_gate, first_gate, later_gate, sum_gate, 0, side)
    reduce_of(W_UP, held_up, first_up, later_up, sum_up, 0, side)
    narrow_of(0, W_OUT, sum_out, 0)
    narrow_of(1, W_V, sum_qkv, 2 * width)
    narrow_of(2, W_K, sum_qkv, width)
    narrow_of(3, W_Q, sum_qkv, 0)

    def parts_of(name):
        return [reduces[name, i] for i in range(BACKWARD_PARTS[name])]

    smalls = []

    def small_step():
        slot = len(smalls)
        device = ([sibling] + partners + line.others)[slot]
        copy = remote(
            small_land.at[2 * slot],
            small_land.at[2 * slot + 1],
            small_send.at[slot],
            small_recv.at[slot],
            device,
        )
        small_land[2 * slot] = small[...]
        copy.start()
        smalls.append(copy)

    def small_take():
        smalls[-1].wait_recv()
        small[...] += small_land[2 * len(smalls) - 1]

    small_count = 1 + bits + len(line.others)

    def link(step):
        kind, who, part = step
        if kind == SMALL:
            while True:
                small_take()
                if len(smalls) == small_count:
                    return
                small_step()
                if part < 5:
                    return
        reduce = reduces[who, part]
        {
            LEAVING: reduce.leaving,
            STAYING: reduce.staying,
            REST: reduce.rest,
            INWARD: reduce.inward,
            ACROSS: reduce.across,
            OUTWARD: reduce.outward,
        }[kind]()

    for reduce in parts_of(W_DOWN):
        for q in reversed(range(half)):
            reduce.begin(q)

    tile = min(TILE, side)
    whole_tiles, rest = side // tile, side % tile

    def ring_copy(row, slot, size):
        return pltpu.make_async_copy(
            full_down.at[pl.ds(row, size), :],
            ring.at[slot, pl.ds(0, size), pl.ds(0, width)],
            ring_sem.at[slot],
        )

    theirs = pl.multiple_of((1 - c) * side, 128)
    ours = pl.multiple_of(c * side, 128)
    ring_copy(theirs, 0, tile).start()
    load("gate", in_gate, gate)
    load("up", in_up, up)
    load("cot", cotangent, cot)
    load("product", in_product, product)
    load("after", in_after, one)
    load("left", hidden_two2, left)
    down_loads = []
    for q in range(half):
        copy = pltpu.make_async_copy(down_block(q), held_down.at[q], load_sem.at[17 + q])
        copy.start()
        down_loads.append(copy)
    load("out", full_out, w_out)
    load("right", attended2, right)
    load("cosine", in_cosine, cosine)
    load("sine", in_sine, sine)
    load("logs", in_logs, logs)
    for name in ("gate", "up", "cot", "product", "after"):
        loads[name].wait()
    two[...] = one[...]

    def down_tile(at, slot, size):
        rows_of = ring[slot, 0:size, 0:width]
        grad_product = dot_nt(cot[...], rows_of)
        gate_pre = gate[:, pl.ds(at, size)].astype(F32)
        up_proj = up[:, pl.ds(at, size)].astype(F32)
        sigma = jax.nn.sigmoid(gate_pre)
        gate[:, pl.ds(at, size)] = (
            grad_product * up_proj * sigma * (1.0 + gate_pre * (1.0 - sigma))
        ).astype(BF16)
        up[:, pl.ds(at, size)] = (grad_product * (gate_pre * sigma)).astype(BF16)
        two[...] += dot_nn(product[:, pl.ds(at, size)], rows_of)

    gate_swap = swap(gate.at[:, pl.ds(theirs, side)], gate_sib, begin=False)
    up_swap = swap(up.at[:, pl.ds(theirs, side)], up_sib, begin=False)

    @pl.loop(0, 2)
    def _(turn):
        base = pl.multiple_of(lax.rem(1 - c + turn, 2) * side, 128)

        @pl.loop(0, whole_tiles)
        def _(t):
            slot = lax.rem(t, 2)
            at = pl.multiple_of(base + t * tile, 128)
            ring_copy(at, slot, tile).wait()

            @pl.when(t + 1 < whole_tiles)
            def _():
                ring_copy(pl.multiple_of(at + tile, 128), 1 - slot, tile).start()

            if rest:

                @pl.when(t + 1 == whole_tiles)
                def _():
                    ring_copy(pl.multiple_of(at + tile, 128), 2, rest).start()

            down_tile(at, slot, tile)

        @pl.when(turn == 0)
        def _():
            ring_copy(ours, 0, tile).start()

        if rest:
            at = pl.multiple_of(base + whole_tiles * tile, 128)
            ring_copy(at, 2, rest).wait()
            down_tile(at, 2, rest)

        @pl.when(turn == 0)
        def _():
            gate_swap.start()
            up_swap.start()

    low[...] = two[...].astype(BF16)
    output_put = put(low, output)
    load("q", in_q, product.at[:, pl.ds(0, width)])
    load("k", in_k, product.at[:, pl.ds(width, width)])

    def tile_copies(i):
        at = pl.ds(pl.multiple_of(i * block_w, block_w), block_w)
        slot = lax.rem(i, 2)
        return (
            pltpu.make_async_copy(
                full_gate.at[at, :], ring.at[slot, :, pl.ds(0, ff)], ring_sem.at[slot]
            ),
            pltpu.make_async_copy(
                full_up.at[at, :], ring.at[2 + slot, :, pl.ds(0, ff)], ring_sem.at[2 + slot]
            ),
        )

    block_w = min(TILE, width)
    start(tile_copies(0))
    start(tile_copies(1))

    def shard_at(p):
        flips = [place.flips[bits - 1 - i] * lax.rem(p // (1 << i), 2) for i in range(bits)]
        return place.f + sum(flips)

    def grad_blocks(who, both, own, other, links):
        parts = parts_of(who)
        held = parts[0].held

        @pl.loop(0, count)
        def _(i):
            p = count - 1 - i
            at = pl.ds(pl.multiple_of(shard_at(p) * shard_rows, 128), shard_rows)
            held[p] = (
                dot_tn(both[0:rows, at], own()) + dot_tn(both[rows : 2 * rows, at], other())
            ).astype(BF16)
            for q in range(half):

                @pl.when(p == half + q)
                def _():
                    for part in parts:
                        part.begin(q)

            between(i, links)

    def ours_of(ref, offset, size):
        at = pl.ds(pl.multiple_of(offset + c * size, 128), size)
        return lambda: ref[:, at]

    tiles = width // block_w

    def between(turn, links):
        for after, steps in enumerate(links):
            if steps:

                @pl.when(turn == after)
                def _():
                    for step in steps:
                        link(step)

    def back_tiles(links):
        @pl.loop(0, tiles)
        def _(i):
            wait(tile_copies(i))
            slot = lax.rem(i, 2)
            at = pl.ds(pl.multiple_of(i * block_w, block_w), block_w)
            two[:, at] = dot_nt(gate[...], ring[slot, :, 0:ff]) + dot_nt(
                up[...], ring[2 + slot, :, 0:ff]
            )

            @pl.when(i + 2 < tiles)
            def _():
                start(tile_copies(i + 2))

            between(i, links)

    def back_end():
        output_put.wait()
        small[...] = jnp.zeros(small.shape, F32)
        small[2:4, :] = sums[0:2, :]

        @pl.loop(0, rows // block)
        def _(i):
            at = pl.ds(pl.multiple_of(i * block, block), block)
            x = one[at, :]
            inverse = lax.rsqrt(jnp.mean(x * x, axis=-1, keepdims=True) + norm_eps)
            normed = x * inverse
            grad_hidden = two[at, :]
            small[1:2, :] += jnp.sum(grad_hidden * normed, axis=0, keepdims=True)
            result = cot[at, :].astype(F32) + rms_back(grad_hidden * gains[1:2, :], normed, inverse)
            three[at, :] = result
            low[at, :] = result.astype(BF16)

        low_swap.append(swap(low.at[:, pl.ds(theirs_narrow, narrow)], low_sib))
        gate_swap.wait_send()
        up_swap.wait_send()
        load("v", in_v, up.at[:, pl.ds(width, width)])
        load("tokens", tokens, cot)

    theirs_narrow = pl.multiple_of((1 - c) * narrow, 128)
    low_swap, head_swaps = [], {}

    def qkv_copy(i):
        at = pl.ds(pl.multiple_of(i * block_w, block_w), block_w)
        slot = lax.rem(i, 4)
        return pltpu.make_async_copy(full_qkv.at[at, :], ring.at[slot], ring_sem.at[slot])

    def attended_grad():
        loads["out"].wait()

        @pl.loop(0, rows // block)
        def _(i):
            at = pl.ds(pl.multiple_of(i * block, block), block)
            attend_grad[at, :] = dot_nt(low[at, :], w_out[...]).astype(BF16)

        for i in range(min(4, tiles)):
            qkv_copy(i).start()
        loads["right"].wait()
        low_swap[0].wait_recv()

    length = lengths[0]
    pairs = width // PAIR
    q_grad, k_grad = gate.at[:, pl.ds(0, width)], gate.at[:, pl.ds(width, width)]
    v_grad = up.at[:, pl.ds(0, width)]

    def attend_back(links):
        @pl.loop(0, pairs)
        def _(i):
            p = lax.rem((1 - c) * (pairs // 2) + i, pairs)
            at = pl.ds(pl.multiple_of(p * PAIR, PAIR), PAIR)
            shift = pl.ds(pl.multiple_of(width + p * PAIR, PAIR), PAIR)
            q, k, v, g = product[:, at], product[:, shift], up[:, shift], attend_grad[:, at]
            lane = lax.broadcasted_iota(jnp.int32, (rows, PAIR), 1)
            k_t = k.T
            sums_k, sums_v = [], []
            for head in range(2):
                inside = (lane // HEAD_DIM) == head
                k_head = jnp.where(inside, k, jnp.zeros_like(k))
                v_head = jnp.where(inside, v, jnp.zeros_like(v))
                k_turned = k_t[head * HEAD_DIM : (head + 1) * HEAD_DIM]
                parts_k, parts_v = [], []
                for b in range(rows // block):
                    upto = (b + 1) * block
                    q_block, g_block = q[b * block : upto], g[b * block : upto]
                    scores = dot_nt(k_head[:upto], q_block)
                    key = lax.broadcasted_iota(jnp.int32, scores.shape, 0)
                    query = lax.broadcasted_iota(jnp.int32, (1, block), 1) + b * block
                    log_total = logs[p, head : head + 1, b * block : upto]
                    allowed = key <= jnp.minimum(query, length - 1)
                    soft = jnp.where(allowed, jnp.exp(scores - log_total), 0.0)
                    grad_soft = dot_nt(v_head[:upto], g_block)
                    inner = jnp.sum(soft * grad_soft, axis=0, keepdims=True)
                    grad_scores = (soft * (grad_soft - inner)).astype(BF16)
                    turned[head * HEAD_DIM : (head + 1) * HEAD_DIM, b * block : upto] = dot_nn(
                        k_turned[:, :upto], grad_scores
                    )
                    parts_k.append(dot_nn(grad_scores, q_block))
                    parts_v.append(dot_nn(soft.astype(BF16), g_block))
                for parts, gathered in ((parts_k, sums_k), (parts_v, sums_v)):
                    rows_of = []
                    for r in range(rows // block):
                        piece = parts[r][r * block : (r + 1) * block]
                        for later in parts[r + 1 :]:
                            piece = piece + later[r * block : (r + 1) * block]
                        rows_of.append(piece)
                    gathered.append(jnp.concatenate(rows_of, axis=0))
            first_head = lane < HEAD_DIM
            cos, sin = cosine[...], sine[...]

            def back(x):
                return (x * cos - swap_halves(x) * sin).astype(BF16)

            gate[:, at] = back(turned[...].T * HEAD_DIM**-0.5)
            gate[:, shift] = back(jnp.where(first_head, sums_k[0], sums_k[1]))
            half_v = 0.5 * jnp.where(first_head, sums_v[0], sums_v[1])
            up[:, at] = half_v.astype(BF16)
            between(i, links)

            @pl.when(i == pairs // 2 - 1)
            def _():
                for copy in head_swaps.values():
                    copy.start()

    def qkv_tiles(links):
        @pl.loop(0, tiles)
        def _(i):
            qkv_copy(i).wait()
            slot = lax.rem(i, 4)
            at = pl.ds(pl.multiple_of(i * block_w, block_w), block_w)
            one[:, at] = (
                dot_nt(gate[:, 0:width], ring[slot, :, 0:width])
                + dot_nt(gate[:, width : 2 * width], ring[slot, :, width : 2 * width])
                + dot_nt(up[:, 0:width], ring[slot, :, 2 * width : 3 * width])
            )

            @pl.when(i + 4 < tiles)
            def _():
                qkv_copy(i + 4).start()

            between(i, links)

    def qkv_end():
        loads["tokens"].wait()
        low_swap[0].wait_send()

        @pl.loop(0, rows // block)
        def _(i):
            at = pl.ds(pl.multiple_of(i * block, block), block)
            x = cot[at, :].astype(F32)
            inverse = lax.rsqrt(jnp.mean(x * x, axis=-1, keepdims=True) + norm_eps)
            normed = x * inverse
            grad_hidden = one[at, :]
            small[0:1, :] += jnp.sum(grad_hidden * normed, axis=0, keepdims=True)
            grads = three[at, :] + rms_back(grad_hidden * gains[0:1, :], normed, inverse)
            low[at, :] = grads.astype(BF16)

        put(low, grad_tokens)
        small_step()

    def first_of(who):
        if who == W_GATE:
            loads["left"].wait()
            gate_swap.wait_recv()
        elif who == W_UP:
            up_swap.wait_recv()
        elif who in head_swaps:
            if who == W_V:
                loads["one"].wait()
            head_swaps[who].wait_recv()

    lefts = {
        W_GATE: (left, ours_of(gate, 0, side), lambda: gate_sib[...]),
        W_UP: (left, ours_of(up, 0, side), lambda: up_sib[...]),
        W_OUT: (right, ours_of(low, 0, narrow), lambda: low_sib[...]),
        W_V: (left, ours_of(up, 0, narrow), lambda: v_sib[...]),
        W_K: (left, ours_of(gate, width, narrow), lambda: k_sib[...]),
        W_Q: (left, ours_of(gate, 0, narrow), lambda: q_sib[...]),
    }

    def compute(kind):
        if kind == NORM_TWO:
            back_end()
        elif kind == ATTEND_GRAD:
            attended_grad()
        elif kind == NORM_ONE:
            qkv_end()

    def turns_of(kind, who, turns, every):
        links, at = [[] for _ in range(every)], 0
        while order and (order[0][0] <= SMALL or (order[0][0], order[0][1]) == (kind, who)):
            if order[0][0] == kind:
                order.pop(0)
                at += 1
            else:
                links[at].append(order.pop(0))
        spread = [[] for _ in range(turns)]
        for i, steps in enumerate(links):
            spread[(i + 1) * turns // every - 1] += steps
        return spread

    order = list(BACKWARD_ORDER)
    while order:
        step = order.pop(0)
        if step[0] <= SMALL:
            if step == (LEAVING, W_DOWN, 0):
                for copy in down_loads:
                    copy.wait()
            link(step)
        elif step[0] == HEAD_PAIRS:
            for key in ("q", "k", "v", "cosine", "sine", "logs"):
                loads[key].wait()
            for key, ref, land in ((W_V, v_grad, v_sib), (W_K, k_grad, k_sib), (W_Q, q_grad, q_sib)):
                head_swaps[key] = swap(ref.at[:, pl.ds(theirs_narrow, narrow)], land, begin=False)
            attend_back(turns_of(HEAD_PAIRS, 0, pairs, 8))
            put(v_grad, grad_first)
        elif step[0] == BLOCKS:
            who = step[1]
            first_of(who)
            grad_blocks(who, *lefts[who], turns_of(BLOCKS, who, count, 4))
            if who == W_UP:
                load("one", hidden_one2, left)
        elif step[0] == MLP_TILES:
            back_tiles(turns_of(MLP_TILES, 0, tiles, 4))
        elif step[0] == QKV_TILES:
            qkv_tiles(turns_of(QKV_TILES, 0, tiles, 4))
        else:
            compute(step[0])

    for reduce in reduces.values():
        reduce.drain()
    for copy in smalls:
        copy.wait_send()
    for copy in swaps:
        if not any(copy is item for item in (gate_swap, up_swap, low_swap[0])):
            copy.wait_send()
    for copy in writes:
        if copy is not output_put:
            copy.wait()


def backward_kernel(lay, lengths, tables, gains, sums, logs, weights, saved, tokens, cotangent):
    count = lay.fs
    half = count // 2
    rows, width = tokens.shape
    n, ff = weights[0].shape[1], weights[2].shape[1]
    shard, down = width // count, ff // count
    side, narrow = ff // 2, width // 2
    dma = pltpu.SemaphoreType.DMA
    vmem = pl.BlockSpec(memory_space=pltpu.VMEM)
    tall = pltpu.VMEM((rows, ff), BF16)
    flat = pltpu.VMEM((rows, width), BF16)
    full = pltpu.VMEM((rows, width), F32)
    small_steps = 1 + lay.bits + (lay.line.bit_length() - 1)
    parts = sum(BACKWARD_PARTS)
    operands = (lengths, *tables, gains, sums, logs, *weights, *saved, tokens, cotangent)
    return pl.pallas_call(
        functools.partial(backward_body, lay),
        in_specs=[pl.BlockSpec(memory_space=pltpu.SMEM)]
        + [ANY, ANY, vmem, vmem]
        + [ANY] * (len(operands) - 5),
        out_specs=[ANY] * 8 + [vmem],
        out_shape=[
            struct((rows, width), BF16),
            struct((rows, width), BF16),
            struct((rows, width), BF16),
            struct((shard, n), BF16),
            struct((shard, width), BF16),
            struct((shard, ff), BF16),
            struct((shard, ff), BF16),
            struct((down, width), BF16),
            struct((8, width), F32),
        ],
        scratch_shapes=[
            pltpu.VMEM((rows, PAIR), F32),
            pltpu.VMEM((rows, PAIR), F32),
            pltpu.VMEM(logs.shape, F32),
            tall,
            tall,
            tall,
            pltpu.VMEM((4, min(TILE, width), n), BF16),
            pltpu.VMEM((width, width), BF16),
            full,
            full,
            full,
            flat,
            pltpu.VMEM((2 * rows, width), BF16),
            pltpu.VMEM((2 * rows, width), BF16),
            flat,
            flat,
            pltpu.VMEM((rows, side), BF16),
            pltpu.VMEM((rows, side), BF16),
            pltpu.VMEM((rows, narrow), BF16),
            pltpu.VMEM((rows, narrow), BF16),
            pltpu.VMEM((rows, narrow), BF16),
            pltpu.VMEM((rows, narrow), BF16),
            pltpu.VMEM((half, down, narrow), BF16),
            pltpu.VMEM((count, shard, side), BF16),
            pltpu.VMEM((count, shard, side), BF16),
            pltpu.VMEM((4 * count, shard, narrow), BF16),
            pltpu.VMEM((half, down, narrow), BF16),
            pltpu.VMEM((half, shard, side), BF16),
            pltpu.VMEM((half, shard, side), BF16),
            pltpu.VMEM((4 * half, shard, narrow), BF16),
            pltpu.VMEM((half - 1, down, narrow), BF16),
            pltpu.VMEM((half - 1, shard, side), BF16),
            pltpu.VMEM((half - 1, shard, side), BF16),
            pltpu.VMEM((4 * (half - 1), shard, narrow), BF16),
            pltpu.VMEM((2 * small_steps, 8, width), F32),
            pltpu.VMEM((PAIR, rows), F32),
            dma((17 + half,)),
            dma((4,)),
            dma((6,)),
            dma((6,)),
            dma((3,)),
            dma((parts * count,)),
            dma((parts * count,)),
            dma((2 * parts,)),
            dma((2 * parts,)),
            pltpu.SemaphoreType.REGULAR((2 * parts,)),
            dma((parts,)),
            dma((parts,)),
            dma((parts,)),
            dma((small_steps,)),
            dma((small_steps,)),
        ],
        compiler_params=pltpu.CompilerParams(
            collective_id=1, has_side_effects=True, vmem_limit_bytes=63 * 2**20
        ),
        cost_estimate=pl.CostEstimate(
            flops=4 * rows * width * (n + width + 3 * ff),
            bytes_accessed=80 * 2**20,
            transcendentals=0,
        ),
        name="backward",
    )(*operands)


def finish_body(lay, entries, small, *refs):
    count = (len(refs) - 4) // 2
    sources, targets = refs[:count], refs[count : 2 * count]
    gain_one, gain_two, first_norm, value_norm = refs[2 * count :]
    for source, target in zip(sources, targets):
        target[...] = source[...].astype(target.dtype)

    @pl.when(pl.program_id(0) == 0)
    def _():
        rows = gain_one.shape[0]
        at = pl.ds(pl.multiple_of(lax.axis_index("fsdp") * rows, rows), rows)
        gain_one[...] = small[0, at]
        gain_two[...] = small[1, at]
        first_norm[0, 0] = jnp.sum(small[2:3, :]) / entries
        value_norm[0, 0] = jnp.sum(small[3:4, :]) / entries


def finish_kernel(lay, results):
    output, grad_tokens, grad_first, *totals, small = results
    rows, width = output.shape
    moved = [output, grad_tokens, grad_first, *totals]
    kinds = [BF16, F32, F32] + [F32] * len(totals)

    steps = 2

    def spec(item):
        return pl.BlockSpec((item.shape[0] // steps, item.shape[1]), lambda i: (i, 0))

    shard = width // lay.fs
    line = pl.BlockSpec((shard,), lambda i: (0,))
    scalar = pl.BlockSpec((1, 1), lambda i: (0, 0), memory_space=pltpu.SMEM)
    done = pl.pallas_call(
        functools.partial(finish_body, lay, rows * width * lay.dp * lay.fs),
        grid=(steps,),
        in_specs=[pl.BlockSpec(small.shape, lambda i: (0, 0))] + [spec(item) for item in moved],
        out_specs=[spec(item) for item in moved] + [line, line, scalar, scalar],
        out_shape=[struct(item.shape, kind) for item, kind in zip(moved, kinds)]
        + [struct((shard,), F32)] * 2
        + [struct((1, 1), F32)] * 2,
        compiler_params=pltpu.CompilerParams(vmem_limit_bytes=63 * 2**20),
        cost_estimate=pl.CostEstimate(
            flops=0, bytes_accessed=30 * 2**20, transcendentals=0
        ),
        name="finish",
    )(small, *moved)
    output, grad_tokens, grad_first, qkv, out, gate, up, down, gain_one, gain_two, first, value = done
    return (
        output,
        grad_tokens,
        grad_first,
        gain_one,
        qkv,
        out,
        gain_two,
        gate,
        up,
        down,
        first.reshape(()),
        value.reshape(()),
    )


def body(
    lay,
    tokens,
    first_values,
    lengths,
    gain_one,
    w_qkv,
    w_out,
    gain_two,
    w_gate,
    w_up,
    w_down,
    cotangent,
):
    rows, width = tokens.shape
    tables = tuple(jnp.asarray(table) for table in rotary_tables(rows))
    results = forward_kernel(
        lay, lengths, tokens, first_values, tables, gain_one, gain_two, cotangent, w_qkv, w_out, w_gate, w_up, w_down
    )
    weights, heads, logs, saved, gains, sums = (
        results[:5],
        results[5:8],
        results[8],
        results[9:17],
        results[17],
        results[18],
    )
    results = backward_kernel(
        lay, lengths, tables, gains, sums, logs, weights, (*heads, *saved), tokens, cotangent
    )
    return finish_kernel(lay, results)


def solution(mesh):
    both = P(AXES, None)
    rows = P("fsdp", None)
    in_specs = (both, both, P(AXES), P("fsdp"), rows, rows, P("fsdp"), rows, rows, rows, both)
    out_specs = (both, both, both, P("fsdp"), rows, rows, P("fsdp"), rows, rows, rows, P(), P())
    lay = Layout(mesh.shape["dp"], mesh.shape["fsdp"])
    return jax.shard_map(
        functools.partial(body, lay),
        mesh=mesh,
        in_specs=in_specs,
        out_specs=out_specs,
        check_vma=False,
    )
```

```python
import functools
import math

import jax
import jax.numpy as jnp
import numpy as np
from jax import lax
from jax.experimental import pallas as pl
from jax.experimental.pallas import tpu as pltpu
from jax.sharding import PartitionSpec as P

HEAD_DIM = 64
PAIR = 2 * HEAD_DIM
TILE = 256
GAIN_ROWS = 16
norm_eps = 1e-06
F32 = jnp.float32
BF16 = jnp.bfloat16
AXES = ("dp", "fsdp")
ANY = pl.BlockSpec(memory_space=pl.ANY)


def dot_nn(a, b):
    return lax.dot_general(a, b, (((1,), (0,)), ((), ())), preferred_element_type=F32)


def dot_nt(a, b):
    return lax.dot_general(a, b, (((1,), (1,)), ((), ())), preferred_element_type=F32)


def dot_tn(a, b):
    return lax.dot_general(a, b, (((0,), (0,)), ((), ())), preferred_element_type=F32)


def rotary_tables(count):
    half = HEAD_DIM // 2
    frequency = np.exp(
        -(np.arange(half, dtype=np.float32) * np.float32(2.0) / np.float32(HEAD_DIM))
        * np.float32(math.log(10000.0))
    ).astype(np.float32)
    angles = np.arange(count, dtype=np.float32)[:, None] * frequency[None, :]
    cosine = np.cos(angles.astype(np.float64)).astype(np.float32)
    sine = np.sin(angles.astype(np.float64)).astype(np.float32)
    cosine = np.concatenate([cosine] * 4, axis=1)
    sine = np.concatenate([-sine, sine, -sine, sine], axis=1)
    return cosine, sine


def swap_halves(x):
    half = HEAD_DIM // 2
    lane = lax.broadcasted_iota(jnp.int32, x.shape, 1)
    up = pltpu.roll(x, PAIR - half, 1)
    down = pltpu.roll(x, half, 1)
    return jnp.where((lane % HEAD_DIM) < half, up, down)


class Layout:
    def __init__(self, dp, fs):
        self.dp, self.fs = dp, fs
        self.bits = fs.bit_length() - 1
        self.line = dp // 2


def add_low(a, b):
    return (a.astype(F32) + b.astype(F32)).astype(BF16)


def start(copies):
    for copy in copies:
        copy.start()


def wait(copies):
    for copy in copies:
        copy.wait()


def struct(shape, dtype):
    return jax.ShapeDtypeStruct(shape, dtype)


class Place:
    def __init__(self, lay):
        self.bits, self.count = lay.bits, lay.fs
        self.d, self.f = lax.axis_index("dp"), lax.axis_index("fsdp")
        self.c = lax.rem(self.d, 2)
        self.flips = []
        for i in range(self.bits):
            ahead, back = 1 << i, 1 << (self.bits - 1 - i)
            one = ahead * (1 - 2 * lax.rem(self.f // ahead, 2))
            two = back * (1 - 2 * lax.rem(self.f // back, 2))
            self.flips.append(one + self.c * (two - one))

    def shard(self, m):
        return self.f + sum(self.flips[i] for i in range(self.bits) if (m >> i) & 1)

    def partner(self, i):
        return (self.d, self.f + self.flips[i])

    def sibling(self):
        return (self.d + 1 - 2 * self.c, self.f)

    def above(self):
        return (self.d + 2 - 4 * lax.rem(self.d // 2, 2), self.f)

    def group(self):
        others = []
        for m in range(1, self.count):
            others.append((self.d, self.shard(m)))
        return others


def remote(src, dst, send, recv, device):
    return pltpu.make_async_remote_copy(
        src_ref=src,
        dst_ref=dst,
        send_sem=send,
        recv_sem=recv,
        device_id=device,
        device_id_type=pl.DeviceIdType.MESH,
    )


class Gather:
    def __init__(self, place, own, full, first, total, lifted, sems, slot):
        self.place = place
        send, recv, up_send, up_recv, cross_send, cross_recv, more_send, more_recv = sems
        count = place.count
        rows, side = own.shape[0], total // 2
        column = pl.ds(pl.multiple_of(first + place.c * side, 128), side)
        size = rows // 2 if lifted else rows
        parity = lax.rem(place.d // 2, 2) if lifted else 0
        self.link, self.up, self.cross, self.more = [None], [None], [None], [None]

        def spot(piece, which):
            at = pl.multiple_of(place.shard(piece) * rows + which * size, size)
            return full.at[pl.ds(at, size), column]

        for m in range(1, count):
            step = m.bit_length() - 1
            before = m - (1 << step)
            source = spot(before, parity)
            if before == 0:
                source = own.at[pl.ds(pl.multiple_of(parity * size, size), size), column]
            at = slot * count + m
            self.link.append(
                remote(source, spot(before, parity), send.at[at], recv.at[at], place.partner(step))
            )
            here = spot(m, parity)
            self.cross.append(
                remote(here, here, cross_send.at[at], cross_recv.at[at], place.sibling())
            )
            if lifted:
                there = spot(m, 1 - parity)
                self.up.append(remote(here, here, up_send.at[at], up_recv.at[at], place.above()))
                self.more.append(
                    remote(there, there, more_send.at[at], more_recv.at[at], place.sibling())
                )

    def begin(self, m):
        self.link[m].start()

    def arrived(self, m):
        self.link[m].wait_recv()
        for i in range(m.bit_length(), self.place.bits):
            self.link[m + (1 << i)].start()
        self.cross[m].start()

    def lift(self, m):
        self.up[m].start()

    def landed(self, m):
        self.up[m].wait_recv()
        self.more[m].start()

    def complete(self):
        for copy in self.cross[1:] + self.more[1:]:
            copy.wait_recv()

    def drain(self):
        for copy in self.link[1:] + self.cross[1:] + self.up[1:] + self.more[1:]:
            copy.wait_send()


QK, V, OUT, GATE, UP, DOWN = range(6)
BEGIN, ARRIVE, LIFT, LAND = range(4)
NORMALISE, QUERIES, KEYS, VALUES, HEADS, PROJECT, GATES, UPS, SUM_DOWN = range(4, 13)
FORWARD_LIFTED = (QK, V, GATE, DOWN)
FORWARD_ORDER = (
    (BEGIN, QK, 1), (BEGIN, QK, 2), (NORMALISE, 0, 0), (BEGIN, GATE, 1), (ARRIVE, QK, 1),
    (ARRIVE, QK, 2), (LIFT, QK, 2), (BEGIN, V, 1), (LIFT, QK, 1), (BEGIN, OUT, 1), (BEGIN, V, 2),
    (ARRIVE, V, 1), (BEGIN, GATE, 2), (ARRIVE, V, 2), (ARRIVE, GATE, 1), (ARRIVE, QK, 3),
    (LIFT, QK, 3), (LAND, QK, 2), (ARRIVE, V, 3), (ARRIVE, OUT, 1), (BEGIN, OUT, 2), (LIFT, V, 2),
    (ARRIVE, GATE, 2), (LAND, QK, 1), (BEGIN, UP, 1), (LIFT, V, 1), (LAND, QK, 3), (LIFT, V, 3),
    (QUERIES, 0, 0), (LAND, V, 2), (LIFT, GATE, 1), (ARRIVE, GATE, 3), (BEGIN, DOWN, 1),
    (BEGIN, UP, 2), (LIFT, GATE, 2), (BEGIN, DOWN, 2), (KEYS, 0, 0), (LAND, V, 1), (LAND, V, 3),
    (VALUES, 0, 0), (ARRIVE, OUT, 3), (LIFT, GATE, 3), (HEADS, 0, 0), (HEADS, 0, 0),
    (LAND, GATE, 1), (ARRIVE, OUT, 2), (HEADS, 0, 0), (ARRIVE, UP, 1), (HEADS, 0, 0),
    (ARRIVE, DOWN, 1), (ARRIVE, UP, 2), (LAND, GATE, 2), (LIFT, DOWN, 1), (PROJECT, 0, 0),
    (ARRIVE, DOWN, 2), (LIFT, DOWN, 2), (LAND, GATE, 3), (GATES, 0, 0), (ARRIVE, UP, 3),
    (LAND, DOWN, 1), (UPS, 0, 0), (ARRIVE, DOWN, 3), (LIFT, DOWN, 3), (UPS, 0, 1), (LAND, DOWN, 2),
    (SUM_DOWN, 0, 0), (LAND, DOWN, 3),
)


def forward_body(
    lay,
    lengths,
    in_tokens,
    in_first,
    in_cosine,
    in_sine,
    gain_one_in,
    gain_two_in,
    cotangent,
    in_qkv,
    in_out,
    in_gate,
    in_up,
    in_down,
    full_qkv,
    full_out,
    full_gate,
    full_up,
    full_down,
    out_q,
    out_k,
    out_v,
    logs,
    hidden_one2,
    attended2,
    hidden_two2,
    out_after,
    out_gate,
    out_up,
    out_product,
    grad_down,
    gains,
    sums,
    w_qkv,
    w_out,
    w_gate,
    w_up,
    tokens,
    first,
    cosine,
    sine,
    gain_in,
    gain,
    hidden,
    queries,
    keys,
    values,
    attended,
    after,
    gate_pre,
    low_gate,
    low_up,
    product2,
    cot2,
    grad_low,
    turned,
    send,
    recv,
    up_send,
    up_recv,
    cross_send,
    cross_recv,
    more_send,
    more_recv,
    local,
    gain_send,
    gain_recv,
    swap_send,
    swap_recv,
    write,
):
    place = Place(lay)
    count, c = place.count, place.c
    rows, width = tokens.shape
    shard_rows = in_qkv.shape[0]
    ff = in_gate.shape[1]
    sibling = place.sibling()

    barrier = pltpu.get_barrier_semaphore()
    begins = []
    for i, (source, target) in enumerate(
        ((in_tokens, tokens), (in_cosine, cosine), (in_sine, sine), (in_first, first))
    ):
        begins.append(pltpu.make_async_copy(source, target, local.at[10 + i]))
    start(begins)
    known = [sibling, place.above()] + place.group()
    for device in known:
        pl.semaphore_signal(barrier, inc=1, device_id=device, device_id_type=pl.DeviceIdType.MESH)
    pl.semaphore_wait(barrier, len(known))

    sems = (send, recv, up_send, up_recv, cross_send, cross_recv, more_send, more_recv)

    def gather(who, own, full, first_column, total):
        return Gather(place, own, full, first_column, total, who in FORWARD_LIFTED, sems, who)

    gathers = {
        QK: gather(QK, in_qkv, w_qkv, 0, 2 * width),
        V: gather(V, in_qkv, w_qkv, 2 * width, width),
        OUT: gather(OUT, in_out, w_out, 0, width),
        GATE: gather(GATE, in_gate, w_gate, 0, ff),
        UP: gather(UP, in_up, w_up, 0, ff),
        DOWN: gather(DOWN, in_down, full_down, 0, width),
    }

    seen = {}

    def link(step):
        kind, who, turn = step
        one = gathers[who]
        if kind == BEGIN:
            firsts = [1 << i for i in range(place.bits)]
            for m in firsts[turn - 1 : turn] if count == 4 else firsts * (turn == 1):
                one.begin(m)
            return
        if count == 4:
            pieces = [turn]
        else:
            done = seen[who, kind] = seen.get((who, kind), 0) + 1
            pieces = range(1 + (done - 1) * (count - 1) // 3, 1 + done * (count - 1) // 3)
        for m in pieces:
            {ARRIVE: one.arrived, LIFT: one.lift, LAND: one.landed}[kind](m)

    gain_in[...] = jnp.zeros(gain_in.shape, BF16)
    gain_in[0:1, :] = gain_one_in[...].reshape(1, shard_rows)
    gain_in[1:2, :] = gain_two_in[...].reshape(1, shard_rows)
    gain_at = pl.multiple_of(place.f * shard_rows, shard_rows)
    gain_copies = []
    for m, device in enumerate(place.group()):
        gain_copies.append(
            remote(
                gain_in,
                gain.at[:, pl.ds(gain_at, shard_rows)],
                gain_send.at[m],
                gain_recv.at[m],
                device,
            )
        )
    gain_own = pltpu.make_async_copy(
        gain_in, gain.at[:, pl.ds(gain_at, shard_rows)], local.at[4]
    )
    start(gain_copies + [gain_own])
    order = list(FORWARD_ORDER)
    while order[0][0] == BEGIN:
        link(order.pop(0))
    own_rows = pl.ds(gain_at, shard_rows)
    locals_of = {}
    for slot, (name, source, full) in enumerate(
        ((QK, in_qkv, w_qkv), (OUT, in_out, w_out), (GATE, in_gate, w_gate), (UP, in_up, w_up))
    ):
        locals_of[name] = pltpu.make_async_copy(source, full.at[own_rows, :], local.at[slot])
        locals_of[name].start()
    half = width // 2
    down_rows = in_down.shape[0]
    down_at = pl.ds(pl.multiple_of(place.f * down_rows, down_rows), down_rows)
    down_in, down_out = [], []
    for i in range(2):
        stage = grad_low.at[pl.ds(i * down_rows, down_rows), :]
        side = pl.ds(i * half, half)
        down_in.append(pltpu.make_async_copy(in_down.at[:, side], stage, local.at[6 + i]))
        down_out.append(pltpu.make_async_copy(stage, full_down.at[down_at, side], local.at[8 + i]))
    start(down_in)

    writes = []

    def put(source, target):
        copy = pltpu.make_async_copy(source, target, write.at[len(writes)])
        copy.start()
        writes.append(copy)

    swaps = []

    def swap(source, target):
        slot = len(swaps)
        copy = remote(source, target, swap_send.at[slot], swap_recv.at[slot], sibling)
        copy.start()
        swaps.append(copy)
        return copy

    def share(source, target):
        put(source, target.at[pl.ds(0, rows), :])
        return swap(source, target.at[pl.ds(rows, rows), :])

    theirs = pl.multiple_of((1 - c) * half, 128)
    ours = pl.multiple_of(c * half, 128)
    cot_swap = swap(cotangent.at[:, pl.ds(theirs, half)], cot2.at[pl.ds(rows, rows), :])
    cot_own = pltpu.make_async_copy(
        cotangent.at[:, pl.ds(ours, half)], cot2.at[pl.ds(0, rows), :], local.at[5]
    )
    cot_own.start()

    block = min(TILE, rows)
    length = lengths[0]
    pairs = width // PAIR
    hidden_two = low_up.at[:, pl.ds(0, width)]
    two_swap, two_put, product_swaps = [], [], []

    def by_rows(step):
        @pl.loop(0, rows // block)
        def _(i):
            step(pl.ds(pl.multiple_of(i * block, block), block))

    def normalise():
        begins[0].wait()
        inputs = tokens[...].astype(F32)
        inverse = lax.rsqrt(jnp.mean(inputs * inputs, axis=-1, keepdims=True) + norm_eps)
        for copy in gain_copies:
            copy.wait_recv()
        gain_own.wait()
        gains[0:1, :] = gain[0:1, :].astype(F32)
        gains[1:2, :] = gain[1:2, :].astype(F32)
        gains[2:8, :] = jnp.zeros((6, width), F32)
        hidden[...] = (inputs * inverse * gains[0:1, :]).astype(BF16)
        share(hidden, hidden_one2)
        wait(down_in)
        start(down_out)
        sums[...] = jnp.zeros(sums.shape, F32)
        logs[...] = jnp.zeros(logs.shape, F32)

    def rotated(which, out, scale):
        def step(at):
            cos, sin = cosine[at, :], sine[at, :]
            raw = dot_nn(hidden[at, :], w_qkv[:, which * width : (which + 1) * width])
            for p in range(width // PAIR):
                x = raw[:, p * PAIR : (p + 1) * PAIR]
                low = (x * cos + swap_halves(x) * sin).astype(BF16)
                out[at, p * PAIR : (p + 1) * PAIR] = low * jnp.asarray(scale, BF16)

        by_rows(step)

    def mix(at):
        raw = dot_nn(hidden[at, :], w_qkv[:, 2 * width : 3 * width])
        kept = first[at, :].astype(F32)
        mixed = 0.5 * raw + 0.5 * kept
        values[at, :] = mixed.astype(BF16)
        sums[0:1, :] += jnp.sum(kept * kept, axis=0, keepdims=True)
        sums[1:2, :] += jnp.sum(mixed * mixed, axis=0, keepdims=True)

    turn = 2

    def attend(links):
        @pl.loop(0, pairs // turn)
        def _(i):
            for j in range(turn):
                attend_pair(i * turn + j, turned.at[j])
            for after_turn, steps in enumerate(links):
                if steps:

                    @pl.when(i == after_turn)
                    def _():
                        for step in steps:
                            link(step)

    def attend_pair(p, turned):
        at = pl.ds(pl.multiple_of(p * PAIR, PAIR), PAIR)
        q, k = queries[:, at], keys[:, at]
        v_t = values[:, at].T
        lane = lax.broadcasted_iota(jnp.int32, (rows, PAIR), 1)
        for head in range(2):
            inside = (lane // HEAD_DIM) == head
            k_head = jnp.where(inside, k, jnp.zeros_like(k))
            v_head = v_t[head * HEAD_DIM : (head + 1) * HEAD_DIM]
            for b in range(rows // block):
                upto = (b + 1) * block
                scores = dot_nt(k_head[:upto], q[b * block : upto])
                key = lax.broadcasted_iota(jnp.int32, scores.shape, 0)
                query = lax.broadcasted_iota(jnp.int32, (1, block), 1) + b * block
                allowed = key <= jnp.minimum(query, length - 1)
                scores = jnp.where(allowed, scores, -1e30)
                peak = jnp.max(scores, axis=0, keepdims=True)
                expo = jnp.exp(scores - peak)
                total = jnp.sum(expo, axis=0, keepdims=True)
                logs[p, head : head + 1, b * block : upto] = peak + jnp.log(total)
                out = dot_nn(v_head[:, :upto], expo.astype(BF16)) * (1.0 / total)
                turned[head * HEAD_DIM : (head + 1) * HEAD_DIM, b * block : upto] = out
        attended[:, at] = turned[...].T.astype(BF16)

    def project(at):
        x = tokens[at, :].astype(F32) + dot_nn(attended[at, :], w_out[...])
        after[at, :] = x
        scale = lax.rsqrt(jnp.mean(x * x, axis=-1, keepdims=True) + norm_eps)
        low_up[at, 0:width] = (x * scale * gains[1:2, :]).astype(BF16)

    def gate_rows(at):
        gate_pre[at, :] = dot_nn(low_up[at, 0:width], w_gate[...])
        low_gate[at, :] = gate_pre[at, :].astype(BF16)

    def up_rows(at):
        up_proj = dot_nn(low_up[at, 0:width], w_up[...])
        gate_of = gate_pre[at, :]
        product2[at, :] = (gate_of * jax.nn.sigmoid(gate_of) * up_proj).astype(BF16)
        low_up[at, :] = up_proj.astype(BF16)

    def compute(kind, part):
        if kind == NORMALISE:
            normalise()
        elif kind == QUERIES:
            wait(begins[1:])
            locals_of[QK].wait()
            gathers[QK].complete()
            rotated(0, queries, HEAD_DIM**-0.5)
            put(queries, out_q)
        elif kind == KEYS:
            rotated(1, keys, 1.0)
            put(keys, out_k)
        elif kind == VALUES:
            gathers[V].complete()
            put(w_qkv, full_qkv)
            by_rows(mix)
            put(values, out_v)
        elif kind == PROJECT:
            share(attended, attended2)
            locals_of[OUT].wait()
            gathers[OUT].complete()
            put(w_out, full_out)
            by_rows(project)
            put(after, out_after)
            two_swap.append(share(hidden_two, hidden_two2))
            two_put.append(writes[-1])
        elif kind == GATES:
            locals_of[GATE].wait()
            gathers[GATE].complete()
            put(w_gate, full_gate)
            by_rows(gate_rows)
            put(low_gate, out_gate)
        elif kind == UPS and part == 0:
            locals_of[UP].wait()
            gathers[UP].complete()
            put(w_up, full_up)
            two_swap[0].wait_send()
            two_put[0].wait()
            steps = []
            while order[0][0] <= LAND:
                steps.append(order.pop(0))
            up_parts(steps)
        elif kind == UPS:
            put(low_up, out_up)
            put(product2.at[pl.ds(0, rows), :], out_product)
        else:
            wait(down_out)
            cot_own.wait()
            cot_swap.wait_recv()
            for copy in product_swaps:
                copy.wait_recv()

            @pl.loop(0, ff // TILE)
            def _(i):
                at = pl.ds(pl.multiple_of(i * TILE, TILE), TILE)
                grad_low[at, :] = dot_tn(product2[:, at], cot2[...]).astype(BF16)

            put(grad_low, grad_down)

    def up_parts(steps):
        size = rows // 2
        for i in range(2):
            part = pl.ds(i * size, size)
            there = pl.ds(rows + i * size, size)
            slot = len(swaps)
            copy = remote(
                product2.at[part, :], product2.at[there, :], swap_send.at[slot], swap_recv.at[slot], sibling
            )
            swaps.append(copy)
            product_swaps.append(copy)

        @pl.loop(0, 2)
        def _(i):
            up_rows(pl.ds(pl.multiple_of(i * size, size), size))

            @pl.when(i == 0)
            def _():
                product_swaps[0].start()
                for step in steps:
                    link(step)

            @pl.when(i == 1)
            def _():
                product_swaps[1].start()

    while order:
        step = order.pop(0)
        if step[0] <= LAND:
            link(step)
        elif step[0] == HEADS:
            turns = pairs // turn
            links, at = [[] for _ in range(4)], 0
            while order and (order[0][0] <= LAND or order[0][0] == HEADS):
                if order[0][0] == HEADS:
                    order.pop(0)
                    at += 1
                else:
                    links[at].append(order.pop(0))
            spread = [[] for _ in range(turns)]
            for i, steps in enumerate(links):
                spread[(i + 1) * turns // 4 - 1] += steps
            attend(spread)
        else:
            compute(step[0], step[2])

    gathers[DOWN].complete()
    for one in gathers.values():
        one.drain()
    for copy in gain_copies:
        copy.wait_send()
    waited = [cot_swap, *product_swaps]
    for copy in swaps:
        if not any(copy is item for item in waited):
            copy.wait_recv()
        if copy is not two_swap[0]:
            copy.wait_send()
    for copy in writes:
        if copy is not two_put[0]:
            copy.wait()


def forward_kernel(lay, lengths, tokens, first, tables, gain_one, gain_two, cotangent, w_qkv, w_out, w_gate, w_up, w_down):
    count = lay.fs
    rows, width = tokens.shape
    n, ff = w_qkv.shape[1], w_gate.shape[1]
    half = width // 2
    pairs = width // PAIR
    big = struct((rows, width), BF16)
    wide = struct((rows, ff), BF16)
    two = struct((2 * rows, width), BF16)
    dma = pltpu.SemaphoreType.DMA
    vmem = pl.BlockSpec(memory_space=pltpu.VMEM)
    weights = [(width, n), (width, width), (width, ff), (width, ff), (ff, width)]
    out_shape = (
        [struct(shape, BF16) for shape in weights]
        + [big, big, big, struct((pairs, 8, rows), F32)]
        + [two, two, two, struct((rows, width), F32), wide, wide, wide]
        + [struct((ff, half), BF16), struct((8, width), F32), struct((8, width), F32)]
    )
    out_specs = [ANY] * 8 + [vmem] + [ANY] * 8 + [vmem, vmem]
    return pl.pallas_call(
        functools.partial(forward_body, lay),
        in_specs=[pl.BlockSpec(memory_space=pltpu.SMEM)] + [ANY] * 4 + [vmem] * 2 + [ANY] * 6,
        out_specs=out_specs,
        out_shape=out_shape,
        scratch_shapes=[
            pltpu.VMEM((width, n), BF16),
            pltpu.VMEM((width, width), BF16),
            pltpu.VMEM((width, ff), BF16),
            pltpu.VMEM((width, ff), BF16),
            pltpu.VMEM((rows, width), BF16),
            pltpu.VMEM((rows, width), BF16),
            pltpu.VMEM((rows, PAIR), F32),
            pltpu.VMEM((rows, PAIR), F32),
            pltpu.VMEM((GAIN_ROWS, width // count), BF16),
            pltpu.VMEM((GAIN_ROWS, width), BF16),
            pltpu.VMEM((rows, width), BF16),
            pltpu.VMEM((rows, width), BF16),
            pltpu.VMEM((rows, width), BF16),
            pltpu.VMEM((rows, width), BF16),
            pltpu.VMEM((rows, width), BF16),
            pltpu.VMEM((rows, width), F32),
            pltpu.VMEM((rows, ff), F32),
            pltpu.VMEM((rows, ff), BF16),
            pltpu.VMEM((rows, ff), BF16),
            pltpu.VMEM((2 * rows, ff), BF16),
            pltpu.VMEM((2 * rows, half), BF16),
            pltpu.VMEM((ff, half), BF16),
            pltpu.VMEM((2, PAIR, rows), F32),
            *[dma((6 * count,))] * 8,
            dma((14,)),
            dma((count - 1,)),
            dma((count - 1,)),
            dma((6,)),
            dma((6,)),
            dma((16,)),
        ],
        compiler_params=pltpu.CompilerParams(
            collective_id=0, has_side_effects=True, vmem_limit_bytes=62 * 2**20
        ),
        cost_estimate=pl.CostEstimate(
            flops=2 * rows * width * (n + width + 3 * ff),
            bytes_accessed=60 * 2**20,
            transcendentals=0,
        ),
        name="forward",
    )(lengths, tokens, first, *tables, gain_one, gain_two, cotangent, w_qkv, w_out, w_gate, w_up, w_down)


def rms_back(grad, normed, inverse):
    return inverse * (grad - normed * jnp.mean(grad * normed, axis=-1, keepdims=True))


class Line:
    def __init__(self, lay, place):
        size = lay.line
        r = place.d // 2
        self.half = size // 2
        upper = r // self.half
        toward = 1 - 2 * upper
        self.depth = r * toward + upper * (size - 1)
        self.next = (place.d + 2 * toward, place.f)
        self.prev = (place.d - 2 * toward, place.f)
        self.middle = self.depth == self.half - 1
        self.inner = self.depth > 0
        self.others = []
        reach = 1
        while reach < size:
            self.others.append((place.d + 2 * reach * (1 - 2 * lax.rem(r // reach, 2)), place.f))
            reach *= 2


def signal(sem, device):
    pl.semaphore_signal(sem, inc=1, device_id=device, device_id_type=pl.DeviceIdType.MESH)


class Reduce:
    def __init__(
        self, place, line, slot, window, held, sources, first, later, final, column, sems
    ):
        send, recv, z_send, z_recv, credit, f_local, f_send, f_recv = sems
        self.place, self.line, self.held, self.window = place, line, held, window
        self.bits, count = place.bits, place.count
        self.count = count
        base = slot * count
        half = count // 2
        self.steps, self.lands = [], []
        at = 0
        for i in range(self.bits):
            blocks = count >> (i + 1)
            copies, lands = [], []
            for q in range(blocks):
                source = sources[q] if i == 0 else held.at[blocks + q, window]
                land = first.at[q, window] if i == 0 else later.at[at + q, window]
                index = base + q if i == 0 else base + half + at + q
                lands.append(land)
                copies.append(remote(source, land, send.at[index], recv.at[index], place.partner(i)))
            if i > 0:
                at += blocks
            self.steps.append(copies)
            self.lands.append(lands)
        mine, inner, outer = held.at[0, window], first.at[0, window], first.at[1, window]
        two = 2 * slot
        self.hops = {
            "in": remote(mine, inner, z_send.at[two], z_recv.at[two], line.next),
            "middle": remote(mine, outer, z_send.at[two], z_recv.at[two + 1], line.next),
            "back": remote(inner, outer, z_send.at[two + 1], z_recv.at[two + 1], line.prev),
            "out": remote(outer, outer, z_send.at[two + 1], z_recv.at[two + 1], line.prev),
        }
        self.mine, self.inner, self.outer = mine, inner, outer
        spot = final.at[window, column]
        self.ends = []
        for source in (inner, outer):
            self.ends.append(
                (
                    pltpu.make_async_copy(source, spot, f_local.at[slot]),
                    remote(source, spot, f_send.at[slot], f_recv.at[slot], place.sibling()),
                )
            )
        self.from_next, self.from_prev = credit.at[two], credit.at[two + 1]

    def begin(self, q):
        self.steps[0][q].start()

    def block(self, i, q):
        blocks = self.count >> (i + 1)
        self.steps[i][q].wait_recv()
        here = self.held.at[q, self.window]
        here[...] = add_low(here[...], self.lands[i][q][...])
        if i + 1 < self.bits and q >= blocks // 2:
            self.steps[i + 1][q - blocks // 2].start()

    def leaving(self):
        half = self.count // 2
        for q in reversed(range(half // 2, half)):
            self.block(0, q)

    def staying(self):
        for q in reversed(range(self.count // 4)):
            self.block(0, q)
        line = self.line

        @pl.when(line.middle)
        def _():
            signal(self.from_next, line.next)

        @pl.when(jnp.logical_not(line.middle))
        def _():
            signal(self.from_prev, line.next)

        @pl.when(line.inner)
        def _():
            signal(self.from_next, line.prev)

    def rest(self):
        for i in range(1, self.bits):
            for q in reversed(range(self.count >> (i + 1))):
                self.block(i, q)

        @pl.when(jnp.logical_not(self.line.inner))
        def _():
            self.onward()

    def onward(self):
        line = self.line
        pl.semaphore_wait(self.from_next, 1)

        @pl.when(line.middle)
        def _():
            self.hops["middle"].start()

        @pl.when(jnp.logical_not(line.middle))
        def _():
            self.hops["in"].start()

    def inward(self):
        @pl.when(self.line.inner)
        def _():
            self.hops["in"].wait_recv()
            self.mine[...] = add_low(self.mine[...], self.inner[...])
            self.onward()

    def finish(self, which):
        local, cross = self.ends[which]
        local.start()
        cross.start()

    def across(self):
        line = self.line

        @pl.when(line.middle)
        def _():
            self.hops["middle"].wait_recv()
            self.inner[...] = add_low(self.mine[...], self.outer[...])

            @pl.when(line.inner)
            def _():
                pl.semaphore_wait(self.from_prev, 1)
                self.hops["back"].start()

            self.finish(0)

    def outward(self):
        line = self.line
        if line.half == 1:
            return

        @pl.when(jnp.logical_not(line.middle))
        def _():
            self.hops["out"].wait_recv()

            @pl.when(line.inner)
            def _():
                pl.semaphore_wait(self.from_prev, 1)
                self.hops["out"].start()

            self.finish(1)

    def drain(self):
        for copies in self.steps:
            for copy in copies:
                copy.wait_send()
        self.hops["in"].wait_send()

        @pl.when(self.line.inner)
        def _():
            self.hops["out"].wait_send()

        local, cross = self.ends[0]
        local.wait()
        cross.wait_send()
        cross.wait_recv()


W_DOWN, W_GATE, W_UP, W_OUT, W_V, W_K, W_Q = range(7)
BACKWARD_PARTS = (2, 2, 4, 2, 2, 4, 4)
LEAVING, STAYING, REST, INWARD, ACROSS, OUTWARD, SMALL = range(7)
BLOCKS, MLP_TILES, NORM_TWO, ATTEND_GRAD, HEAD_PAIRS, QKV_TILES, NORM_ONE = range(7, 14)
BACKWARD_ORDER = (
    (LEAVING, W_DOWN, 0), (STAYING, W_DOWN, 0), (BLOCKS, W_GATE, 3), (BLOCKS, W_GATE, 2),
    (LEAVING, W_DOWN, 1), (BLOCKS, W_GATE, 1), (REST, W_DOWN, 0), (BLOCKS, W_GATE, 0),
    (BLOCKS, W_UP, 3), (BLOCKS, W_UP, 2), (BLOCKS, W_UP, 1), (BLOCKS, W_UP, 0),
    (STAYING, W_DOWN, 1), (MLP_TILES, 0, 0), (REST, W_DOWN, 1), (INWARD, W_DOWN, 0),
    (LEAVING, W_GATE, 0), (MLP_TILES, 0, 1), (MLP_TILES, 0, 2), (MLP_TILES, 0, 3),
    (LEAVING, W_GATE, 1), (NORM_TWO, 0, 0), (INWARD, W_DOWN, 1), (ACROSS, W_DOWN, 0),
    (ATTEND_GRAD, 0, 0), (STAYING, W_GATE, 0), (REST, W_GATE, 0), (BLOCKS, W_OUT, 3),
    (BLOCKS, W_OUT, 2), (BLOCKS, W_OUT, 1), (BLOCKS, W_OUT, 0), (HEAD_PAIRS, 0, 0),
    (STAYING, W_GATE, 1), (REST, W_GATE, 1), (HEAD_PAIRS, 0, 1), (LEAVING, W_UP, 0),
    (LEAVING, W_UP, 1), (INWARD, W_GATE, 0), (ACROSS, W_DOWN, 1), (OUTWARD, W_DOWN, 0),
    (HEAD_PAIRS, 0, 2), (LEAVING, W_UP, 2), (HEAD_PAIRS, 0, 3), (LEAVING, W_UP, 3),
    (HEAD_PAIRS, 0, 4), (INWARD, W_GATE, 1), (HEAD_PAIRS, 0, 5), (ACROSS, W_GATE, 0),
    (STAYING, W_UP, 0), (REST, W_UP, 0), (OUTWARD, W_DOWN, 1), (HEAD_PAIRS, 0, 6),
    (STAYING, W_UP, 1), (REST, W_UP, 1), (HEAD_PAIRS, 0, 7), (INWARD, W_UP, 0), (ACROSS, W_GATE, 1),
    (STAYING, W_UP, 2), (LEAVING, W_OUT, 0), (REST, W_UP, 2), (STAYING, W_UP, 3), (REST, W_UP, 3),
    (LEAVING, W_OUT, 1), (OUTWARD, W_GATE, 0), (INWARD, W_UP, 1), (BLOCKS, W_V, 3),
    (BLOCKS, W_V, 2), (BLOCKS, W_V, 1), (STAYING, W_OUT, 0), (BLOCKS, W_V, 0), (REST, W_OUT, 0),
    (ACROSS, W_UP, 0), (BLOCKS, W_K, 3), (BLOCKS, W_K, 2), (INWARD, W_UP, 2), (STAYING, W_OUT, 1),
    (BLOCKS, W_K, 1), (REST, W_OUT, 1), (BLOCKS, W_K, 0), (LEAVING, W_V, 0), (ACROSS, W_UP, 1),
    (OUTWARD, W_GATE, 1), (BLOCKS, W_Q, 3), (LEAVING, W_V, 1), (INWARD, W_UP, 3), (BLOCKS, W_Q, 2),
    (BLOCKS, W_Q, 1), (BLOCKS, W_Q, 0), (QKV_TILES, 0, 0), (INWARD, W_OUT, 0), (ACROSS, W_UP, 2),
    (STAYING, W_V, 0), (REST, W_V, 0), (OUTWARD, W_UP, 0), (QKV_TILES, 0, 1), (LEAVING, W_K, 0),
    (INWARD, W_OUT, 1), (LEAVING, W_K, 1), (ACROSS, W_UP, 3), (LEAVING, W_K, 2), (STAYING, W_V, 1),
    (REST, W_V, 1), (LEAVING, W_K, 3), (INWARD, W_V, 0), (ACROSS, W_OUT, 0), (OUTWARD, W_UP, 1),
    (QKV_TILES, 0, 2), (STAYING, W_K, 0), (REST, W_K, 0), (ACROSS, W_OUT, 1), (STAYING, W_K, 1),
    (REST, W_K, 1), (OUTWARD, W_UP, 2), (QKV_TILES, 0, 3), (INWARD, W_V, 1), (INWARD, W_K, 0),
    (LEAVING, W_Q, 0), (ACROSS, W_V, 0), (LEAVING, W_Q, 1), (STAYING, W_K, 2), (REST, W_K, 2),
    (LEAVING, W_Q, 2), (INWARD, W_K, 1), (STAYING, W_K, 3), (REST, W_K, 3), (LEAVING, W_Q, 3),
    (OUTWARD, W_UP, 3), (OUTWARD, W_OUT, 0), (NORM_ONE, 0, 0), (INWARD, W_K, 2), (INWARD, W_K, 3),
    (ACROSS, W_V, 1), (ACROSS, W_K, 0), (ACROSS, W_K, 1), (STAYING, W_Q, 0), (REST, W_Q, 0),
    (STAYING, W_Q, 1), (REST, W_Q, 1), (SMALL, 0, 1), (STAYING, W_Q, 2), (REST, W_Q, 2),
    (ACROSS, W_K, 2), (STAYING, W_Q, 3), (REST, W_Q, 3), (OUTWARD, W_OUT, 1), (OUTWARD, W_V, 0),
    (ACROSS, W_K, 3), (INWARD, W_Q, 0), (OUTWARD, W_V, 1), (SMALL, 0, 2), (INWARD, W_Q, 1),
    (OUTWARD, W_K, 0), (INWARD, W_Q, 2), (SMALL, 0, 3), (ACROSS, W_Q, 0), (OUTWARD, W_K, 1),
    (INWARD, W_Q, 3), (OUTWARD, W_K, 2), (ACROSS, W_Q, 1), (SMALL, 0, 4), (OUTWARD, W_K, 3),
    (ACROSS, W_Q, 2), (OUTWARD, W_Q, 0), (ACROSS, W_Q, 3), (SMALL, 0, 5), (OUTWARD, W_Q, 1),
    (OUTWARD, W_Q, 2), (OUTWARD, W_Q, 3),
)


def backward_body(
    lay,
    lengths,
    in_cosine,
    in_sine,
    gains,
    sums,
    in_logs,
    full_qkv,
    full_out,
    full_gate,
    full_up,
    full_down,
    in_q,
    in_k,
    in_v,
    hidden_one2,
    attended2,
    hidden_two2,
    in_after,
    in_gate,
    in_up,
    in_product,
    in_grad_down,
    tokens,
    cotangent,
    output,
    grad_tokens,
    grad_first,
    sum_qkv,
    sum_out,
    sum_gate,
    sum_up,
    sum_down,
    small,
    cosine,
    sine,
    logs,
    gate,
    up,
    product,
    ring,
    w_out,
    one,
    two,
    three,
    cot,
    left,
    right,
    low,
    attend_grad,
    gate_sib,
    up_sib,
    low_sib,
    q_sib,
    k_sib,
    v_sib,
    held_down,
    held_gate,
    held_up,
    held_narrow,
    first_down,
    first_gate,
    first_up,
    first_narrow,
    later_down,
    later_gate,
    later_up,
    later_narrow,
    small_land,
    turned,
    load_sem,
    ring_sem,
    swap_send,
    swap_recv,
    write_sem,
    send,
    recv,
    z_send,
    z_recv,
    credit,
    f_local,
    f_send,
    f_recv,
    small_send,
    small_recv,
):
    place = Place(lay)
    line = Line(lay, place)
    count, c = place.count, place.c
    sibling = place.sibling()
    rows, width = cot.shape
    ff = gate.shape[1]
    side, narrow = ff // 2, width // 2
    block = min(TILE, rows)
    bits = place.bits

    barrier = pltpu.get_barrier_semaphore()
    partners = [place.partner(i) for i in range(bits)]
    known = [sibling] + partners + line.others + [line.next]
    for device in known:
        signal(barrier, device)

    @pl.when(line.inner)
    def _():
        signal(barrier, line.prev)
        pl.semaphore_wait(barrier, len(known) + 1)

    @pl.when(jnp.logical_not(line.inner))
    def _():
        pl.semaphore_wait(barrier, len(known))

    loads = {}

    def load(name, source, target):
        copy = pltpu.make_async_copy(source, target, load_sem.at[len(loads)])
        copy.start()
        loads[name] = copy

    writes = []

    def put(source, target):
        copy = pltpu.make_async_copy(source, target, write_sem.at[len(writes)])
        copy.start()
        writes.append(copy)
        return copy

    swaps = []

    def swap(source, target, begin=True):
        slot = len(swaps)
        copy = remote(source, target, swap_send.at[slot], swap_recv.at[slot], sibling)
        if begin:
            copy.start()
        swaps.append(copy)
        return copy

    def shard_of(p):
        m = sum(((p >> i) & 1) << (bits - 1 - i) for i in range(bits))
        return place.shard(m)

    sems = (send, recv, z_send, z_recv, credit, f_local, f_send, f_recv)
    half = count // 2
    down_rows = in_grad_down.shape[0] // count
    shard_rows = sum_qkv.shape[0]

    def down_block(p, window=None):
        at = pl.multiple_of(shard_of(p) * down_rows, down_rows)
        if window is None:
            return in_grad_down.at[pl.ds(at, down_rows), :]
        return in_grad_down.at[pl.ds(at + window.start, window.size), :]

    reduces = {}

    def reduce_of(name, held, first, later, final, offset, size):
        parts = BACKWARD_PARTS[name]
        part_rows = held.shape[1] // parts
        for part in range(parts):
            window = pl.ds(part * part_rows, part_rows)
            if name == W_DOWN:
                sources = [down_block(half + q, window) for q in range(half)]
            else:
                sources = [held.at[half + q, window] for q in range(half)]
            column = pl.ds(pl.multiple_of(offset + c * size, 128), size)
            reduces[name, part] = Reduce(
                place, line, len(reduces), window, held, sources, first, later, final, column, sems
            )

    def narrow_of(index, name, final, offset):
        at = index * count
        reduce_of(
            name,
            held_narrow.at[pl.ds(at, count)],
            first_narrow.at[pl.ds(index * half, half)],
            later_narrow.at[pl.ds(index * (half - 1), half - 1)],
            final,
            offset,
            narrow,
        )

    reduce_of(W_DOWN, held_down, first_down, later_down, sum_down, 0, narrow)
    reduce_of(W_GATE, held_gate, first_gate, later_gate, sum_gate, 0, side)
    reduce_of(W_UP, held_up, first_up, later_up, sum_up, 0, side)
    narrow_of(0, W_OUT, sum_out, 0)
    narrow_of(1, W_V, sum_qkv, 2 * width)
    narrow_of(2, W_K, sum_qkv, width)
    narrow_of(3, W_Q, sum_qkv, 0)

    def parts_of(name):
        return [reduces[name, i] for i in range(BACKWARD_PARTS[name])]

    smalls = []

    def small_step():
        slot = len(smalls)
        device = ([sibling] + partners + line.others)[slot]
        copy = remote(
            small_land.at[2 * slot],
            small_land.at[2 * slot + 1],
            small_send.at[slot],
            small_recv.at[slot],
            device,
        )
        small_land[2 * slot] = small[...]
        copy.start()
        smalls.append(copy)

    def small_take():
        smalls[-1].wait_recv()
        small[...] += small_land[2 * len(smalls) - 1]

    small_count = 1 + bits + len(line.others)

    def link(step):
        kind, who, part = step
        if kind == SMALL:
            while True:
                small_take()
                if len(smalls) == small_count:
                    return
                small_step()
                if part < 5:
                    return
        reduce = reduces[who, part]
        {
            LEAVING: reduce.leaving,
            STAYING: reduce.staying,
            REST: reduce.rest,
            INWARD: reduce.inward,
            ACROSS: reduce.across,
            OUTWARD: reduce.outward,
        }[kind]()

    for reduce in parts_of(W_DOWN):
        for q in reversed(range(half)):
            reduce.begin(q)

    tile = min(TILE, side)
    whole_tiles, rest = side // tile, side % tile

    def ring_copy(row, slot, size):
        return pltpu.make_async_copy(
            full_down.at[pl.ds(row, size), :],
            ring.at[slot, pl.ds(0, size), pl.ds(0, width)],
            ring_sem.at[slot],
        )

    theirs = pl.multiple_of((1 - c) * side, 128)
    ours = pl.multiple_of(c * side, 128)
    ring_copy(theirs, 0, tile).start()
    load("gate", in_gate, gate)
    load("up", in_up, up)
    load("cot", cotangent, cot)
    load("product", in_product, product)
    load("after", in_after, one)
    load("left", hidden_two2, left)
    down_loads = []
    for q in range(half):
        copy = pltpu.make_async_copy(down_block(q), held_down.at[q], load_sem.at[17 + q])
        copy.start()
        down_loads.append(copy)
    load("out", full_out, w_out)
    load("right", attended2, right)
    load("cosine", in_cosine, cosine)
    load("sine", in_sine, sine)
    load("logs", in_logs, logs)
    for name in ("gate", "up", "cot", "product", "after"):
        loads[name].wait()
    two[...] = one[...]

    def down_tile(at, slot, size):
        rows_of = ring[slot, 0:size, 0:width]
        grad_product = dot_nt(cot[...], rows_of)
        gate_pre = gate[:, pl.ds(at, size)].astype(F32)
        up_proj = up[:, pl.ds(at, size)].astype(F32)
        sigma = jax.nn.sigmoid(gate_pre)
        gate[:, pl.ds(at, size)] = (
            grad_product * up_proj * sigma * (1.0 + gate_pre * (1.0 - sigma))
        ).astype(BF16)
        up[:, pl.ds(at, size)] = (grad_product * (gate_pre * sigma)).astype(BF16)
        two[...] += dot_nn(product[:, pl.ds(at, size)], rows_of)

    gate_swap = swap(gate.at[:, pl.ds(theirs, side)], gate_sib, begin=False)
    up_swap = swap(up.at[:, pl.ds(theirs, side)], up_sib, begin=False)

    @pl.loop(0, 2)
    def _(turn):
        base = pl.multiple_of(lax.rem(1 - c + turn, 2) * side, 128)

        @pl.loop(0, whole_tiles)
        def _(t):
            slot = lax.rem(t, 2)
            at = pl.multiple_of(base + t * tile, 128)
            ring_copy(at, slot, tile).wait()

            @pl.when(t + 1 < whole_tiles)
            def _():
                ring_copy(pl.multiple_of(at + tile, 128), 1 - slot, tile).start()

            if rest:

                @pl.when(t + 1 == whole_tiles)
                def _():
                    ring_copy(pl.multiple_of(at + tile, 128), 2, rest).start()

            down_tile(at, slot, tile)

        @pl.when(turn == 0)
        def _():
            ring_copy(ours, 0, tile).start()

        if rest:
            at = pl.multiple_of(base + whole_tiles * tile, 128)
            ring_copy(at, 2, rest).wait()
            down_tile(at, 2, rest)

        @pl.when(turn == 0)
        def _():
            gate_swap.start()
            up_swap.start()

    low[...] = two[...].astype(BF16)
    output_put = put(low, output)
    load("q", in_q, product.at[:, pl.ds(0, width)])
    load("k", in_k, product.at[:, pl.ds(width, width)])

    def tile_copies(i):
        at = pl.ds(pl.multiple_of(i * block_w, block_w), block_w)
        slot = lax.rem(i, 2)
        return (
            pltpu.make_async_copy(
                full_gate.at[at, :], ring.at[slot, :, pl.ds(0, ff)], ring_sem.at[slot]
            ),
            pltpu.make_async_copy(
                full_up.at[at, :], ring.at[2 + slot, :, pl.ds(0, ff)], ring_sem.at[2 + slot]
            ),
        )

    block_w = min(TILE, width)
    start(tile_copies(0))
    start(tile_copies(1))

    def shard_at(p):
        flips = [place.flips[bits - 1 - i] * lax.rem(p // (1 << i), 2) for i in range(bits)]
        return place.f + sum(flips)

    def grad_blocks(who, both, own, other, links):
        parts = parts_of(who)
        held = parts[0].held

        @pl.loop(0, count)
        def _(i):
            p = count - 1 - i
            at = pl.ds(pl.multiple_of(shard_at(p) * shard_rows, 128), shard_rows)
            held[p] = (
                dot_tn(both[0:rows, at], own()) + dot_tn(both[rows : 2 * rows, at], other())
            ).astype(BF16)
            for q in range(half):

                @pl.when(p == half + q)
                def _():
                    for part in parts:
                        part.begin(q)

            between(i, links)

    def ours_of(ref, offset, size):
        at = pl.ds(pl.multiple_of(offset + c * size, 128), size)
        return lambda: ref[:, at]

    tiles = width // block_w

    def between(turn, links):
        for after, steps in enumerate(links):
            if steps:

                @pl.when(turn == after)
                def _():
                    for step in steps:
                        link(step)

    def back_tiles(links):
        @pl.loop(0, tiles)
        def _(i):
            wait(tile_copies(i))
            slot = lax.rem(i, 2)
            at = pl.ds(pl.multiple_of(i * block_w, block_w), block_w)
            two[:, at] = dot_nt(gate[...], ring[slot, :, 0:ff]) + dot_nt(
                up[...], ring[2 + slot, :, 0:ff]
            )

            @pl.when(i + 2 < tiles)
            def _():
                start(tile_copies(i + 2))

            between(i, links)

    def back_end():
        output_put.wait()
        small[...] = jnp.zeros(small.shape, F32)
        small[2:4, :] = sums[0:2, :]

        @pl.loop(0, rows // block)
        def _(i):
            at = pl.ds(pl.multiple_of(i * block, block), block)
            x = one[at, :]
            inverse = lax.rsqrt(jnp.mean(x * x, axis=-1, keepdims=True) + norm_eps)
            normed = x * inverse
            grad_hidden = two[at, :]
            small[1:2, :] += jnp.sum(grad_hidden * normed, axis=0, keepdims=True)
            result = cot[at, :].astype(F32) + rms_back(grad_hidden * gains[1:2, :], normed, inverse)
            three[at, :] = result
            low[at, :] = result.astype(BF16)

        low_swap.append(swap(low.at[:, pl.ds(theirs_narrow, narrow)], low_sib))
        gate_swap.wait_send()
        up_swap.wait_send()
        load("v", in_v, up.at[:, pl.ds(width, width)])
        load("tokens", tokens, cot)

    theirs_narrow = pl.multiple_of((1 - c) * narrow, 128)
    low_swap, head_swaps = [], {}

    def qkv_copy(i):
        at = pl.ds(pl.multiple_of(i * block_w, block_w), block_w)
        slot = lax.rem(i, 4)
        return pltpu.make_async_copy(full_qkv.at[at, :], ring.at[slot], ring_sem.at[slot])

    def attended_grad():
        loads["out"].wait()

        @pl.loop(0, rows // block)
        def _(i):
            at = pl.ds(pl.multiple_of(i * block, block), block)
            attend_grad[at, :] = dot_nt(low[at, :], w_out[...]).astype(BF16)

        for i in range(min(4, tiles)):
            qkv_copy(i).start()
        loads["right"].wait()
        low_swap[0].wait_recv()

    length = lengths[0]
    pairs = width // PAIR
    q_grad, k_grad = gate.at[:, pl.ds(0, width)], gate.at[:, pl.ds(width, width)]
    v_grad = up.at[:, pl.ds(0, width)]

    def attend_back(links):
        @pl.loop(0, pairs)
        def _(i):
            p = lax.rem((1 - c) * (pairs // 2) + i, pairs)
            at = pl.ds(pl.multiple_of(p * PAIR, PAIR), PAIR)
            shift = pl.ds(pl.multiple_of(width + p * PAIR, PAIR), PAIR)
            q, k, v, g = product[:, at], product[:, shift], up[:, shift], attend_grad[:, at]
            lane = lax.broadcasted_iota(jnp.int32, (rows, PAIR), 1)
            k_t = k.T
            sums_k, sums_v = [], []
            for head in range(2):
                inside = (lane // HEAD_DIM) == head
                k_head = jnp.where(inside, k, jnp.zeros_like(k))
                v_head = jnp.where(inside, v, jnp.zeros_like(v))
                k_turned = k_t[head * HEAD_DIM : (head + 1) * HEAD_DIM]
                parts_k, parts_v = [], []
                for b in range(rows // block):
                    upto = (b + 1) * block
                    q_block, g_block = q[b * block : upto], g[b * block : upto]
                    scores = dot_nt(k_head[:upto], q_block)
                    key = lax.broadcasted_iota(jnp.int32, scores.shape, 0)
                    query = lax.broadcasted_iota(jnp.int32, (1, block), 1) + b * block
                    log_total = logs[p, head : head + 1, b * block : upto]
                    allowed = key <= jnp.minimum(query, length - 1)
                    soft = jnp.where(allowed, jnp.exp(scores - log_total), 0.0)
                    grad_soft = dot_nt(v_head[:upto], g_block)
                    inner = jnp.sum(soft * grad_soft, axis=0, keepdims=True)
                    grad_scores = (soft * (grad_soft - inner)).astype(BF16)
                    turned[head * HEAD_DIM : (head + 1) * HEAD_DIM, b * block : upto] = dot_nn(
                        k_turned[:, :upto], grad_scores
                    )
                    parts_k.append(dot_nn(grad_scores, q_block))
                    parts_v.append(dot_nn(soft.astype(BF16), g_block))
                for parts, gathered in ((parts_k, sums_k), (parts_v, sums_v)):
                    rows_of = []
                    for r in range(rows // block):
                        piece = parts[r][r * block : (r + 1) * block]
                        for later in parts[r + 1 :]:
                            piece = piece + later[r * block : (r + 1) * block]
                        rows_of.append(piece)
                    gathered.append(jnp.concatenate(rows_of, axis=0))
            first_head = lane < HEAD_DIM
            cos, sin = cosine[...], sine[...]

            def back(x):
                return (x * cos - swap_halves(x) * sin).astype(BF16)

            gate[:, at] = back(turned[...].T * HEAD_DIM**-0.5)
            gate[:, shift] = back(jnp.where(first_head, sums_k[0], sums_k[1]))
            half_v = 0.5 * jnp.where(first_head, sums_v[0], sums_v[1])
            up[:, at] = half_v.astype(BF16)
            between(i, links)

            @pl.when(i == pairs // 2 - 1)
            def _():
                for copy in head_swaps.values():
                    copy.start()

    def qkv_tiles(links):
        @pl.loop(0, tiles)
        def _(i):
            qkv_copy(i).wait()
            slot = lax.rem(i, 4)
            at = pl.ds(pl.multiple_of(i * block_w, block_w), block_w)
            one[:, at] = (
                dot_nt(gate[:, 0:width], ring[slot, :, 0:width])
                + dot_nt(gate[:, width : 2 * width], ring[slot, :, width : 2 * width])
                + dot_nt(up[:, 0:width], ring[slot, :, 2 * width : 3 * width])
            )

            @pl.when(i + 4 < tiles)
            def _():
                qkv_copy(i + 4).start()

            between(i, links)

    def qkv_end():
        loads["tokens"].wait()
        low_swap[0].wait_send()

        @pl.loop(0, rows // block)
        def _(i):
            at = pl.ds(pl.multiple_of(i * block, block), block)
            x = cot[at, :].astype(F32)
            inverse = lax.rsqrt(jnp.mean(x * x, axis=-1, keepdims=True) + norm_eps)
            normed = x * inverse
            grad_hidden = one[at, :]
            small[0:1, :] += jnp.sum(grad_hidden * normed, axis=0, keepdims=True)
            grads = three[at, :] + rms_back(grad_hidden * gains[0:1, :], normed, inverse)
            low[at, :] = grads.astype(BF16)

        put(low, grad_tokens)
        small_step()

    def first_of(who):
        if who == W_GATE:
            loads["left"].wait()
            gate_swap.wait_recv()
        elif who == W_UP:
            up_swap.wait_recv()
        elif who in head_swaps:
            if who == W_V:
                loads["one"].wait()
            head_swaps[who].wait_recv()

    lefts = {
        W_GATE: (left, ours_of(gate, 0, side), lambda: gate_sib[...]),
        W_UP: (left, ours_of(up, 0, side), lambda: up_sib[...]),
        W_OUT: (right, ours_of(low, 0, narrow), lambda: low_sib[...]),
        W_V: (left, ours_of(up, 0, narrow), lambda: v_sib[...]),
        W_K: (left, ours_of(gate, width, narrow), lambda: k_sib[...]),
        W_Q: (left, ours_of(gate, 0, narrow), lambda: q_sib[...]),
    }

    def compute(kind):
        if kind == NORM_TWO:
            back_end()
        elif kind == ATTEND_GRAD:
            attended_grad()
        elif kind == NORM_ONE:
            qkv_end()

    def turns_of(kind, who, turns, every):
        links, at = [[] for _ in range(every)], 0
        while order and (order[0][0] <= SMALL or (order[0][0], order[0][1]) == (kind, who)):
            if order[0][0] == kind:
                order.pop(0)
                at += 1
            else:
                links[at].append(order.pop(0))
        spread = [[] for _ in range(turns)]
        for i, steps in enumerate(links):
            spread[(i + 1) * turns // every - 1] += steps
        return spread

    order = list(BACKWARD_ORDER)
    while order:
        step = order.pop(0)
        if step[0] <= SMALL:
            if step == (LEAVING, W_DOWN, 0):
                for copy in down_loads:
                    copy.wait()
            link(step)
        elif step[0] == HEAD_PAIRS:
            for key in ("q", "k", "v", "cosine", "sine", "logs"):
                loads[key].wait()
            for key, ref, land in ((W_V, v_grad, v_sib), (W_K, k_grad, k_sib), (W_Q, q_grad, q_sib)):
                head_swaps[key] = swap(ref.at[:, pl.ds(theirs_narrow, narrow)], land, begin=False)
            attend_back(turns_of(HEAD_PAIRS, 0, pairs, 8))
            put(v_grad, grad_first)
        elif step[0] == BLOCKS:
            who = step[1]
            first_of(who)
            grad_blocks(who, *lefts[who], turns_of(BLOCKS, who, count, 4))
            if who == W_UP:
                load("one", hidden_one2, left)
        elif step[0] == MLP_TILES:
            back_tiles(turns_of(MLP_TILES, 0, tiles, 4))
        elif step[0] == QKV_TILES:
            qkv_tiles(turns_of(QKV_TILES, 0, tiles, 4))
        else:
            compute(step[0])

    for reduce in reduces.values():
        reduce.drain()
    for copy in smalls:
        copy.wait_send()
    for copy in swaps:
        if not any(copy is item for item in (gate_swap, up_swap, low_swap[0])):
            copy.wait_send()
    for copy in writes:
        if copy is not output_put:
            copy.wait()


def backward_kernel(lay, lengths, tables, gains, sums, logs, weights, saved, tokens, cotangent):
    count = lay.fs
    half = count // 2
    rows, width = tokens.shape
    n, ff = weights[0].shape[1], weights[2].shape[1]
    shard, down = width // count, ff // count
    side, narrow = ff // 2, width // 2
    dma = pltpu.SemaphoreType.DMA
    vmem = pl.BlockSpec(memory_space=pltpu.VMEM)
    tall = pltpu.VMEM((rows, ff), BF16)
    flat = pltpu.VMEM((rows, width), BF16)
    full = pltpu.VMEM((rows, width), F32)
    small_steps = 1 + lay.bits + (lay.line.bit_length() - 1)
    parts = sum(BACKWARD_PARTS)
    operands = (lengths, *tables, gains, sums, logs, *weights, *saved, tokens, cotangent)
    return pl.pallas_call(
        functools.partial(backward_body, lay),
        in_specs=[pl.BlockSpec(memory_space=pltpu.SMEM)]
        + [ANY, ANY, vmem, vmem]
        + [ANY] * (len(operands) - 5),
        out_specs=[ANY] * 8 + [vmem],
        out_shape=[
            struct((rows, width), BF16),
            struct((rows, width), BF16),
            struct((rows, width), BF16),
            struct((shard, n), BF16),
            struct((shard, width), BF16),
            struct((shard, ff), BF16),
            struct((shard, ff), BF16),
            struct((down, width), BF16),
            struct((8, width), F32),
        ],
        scratch_shapes=[
            pltpu.VMEM((rows, PAIR), F32),
            pltpu.VMEM((rows, PAIR), F32),
            pltpu.VMEM(logs.shape, F32),
            tall,
            tall,
            tall,
            pltpu.VMEM((4, min(TILE, width), n), BF16),
            pltpu.VMEM((width, width), BF16),
            full,
            full,
            full,
            flat,
            pltpu.VMEM((2 * rows, width), BF16),
            pltpu.VMEM((2 * rows, width), BF16),
            flat,
            flat,
            pltpu.VMEM((rows, side), BF16),
            pltpu.VMEM((rows, side), BF16),
            pltpu.VMEM((rows, narrow), BF16),
            pltpu.VMEM((rows, narrow), BF16),
            pltpu.VMEM((rows, narrow), BF16),
            pltpu.VMEM((rows, narrow), BF16),
            pltpu.VMEM((half, down, narrow), BF16),
            pltpu.VMEM((count, shard, side), BF16),
            pltpu.VMEM((count, shard, side), BF16),
            pltpu.VMEM((4 * count, shard, narrow), BF16),
            pltpu.VMEM((half, down, narrow), BF16),
            pltpu.VMEM((half, shard, side), BF16),
            pltpu.VMEM((half, shard, side), BF16),
            pltpu.VMEM((4 * half, shard, narrow), BF16),
            pltpu.VMEM((half - 1, down, narrow), BF16),
            pltpu.VMEM((half - 1, shard, side), BF16),
            pltpu.VMEM((half - 1, shard, side), BF16),
            pltpu.VMEM((4 * (half - 1), shard, narrow), BF16),
            pltpu.VMEM((2 * small_steps, 8, width), F32),
            pltpu.VMEM((PAIR, rows), F32),
            dma((17 + half,)),
            dma((4,)),
            dma((6,)),
            dma((6,)),
            dma((3,)),
            dma((parts * count,)),
            dma((parts * count,)),
            dma((2 * parts,)),
            dma((2 * parts,)),
            pltpu.SemaphoreType.REGULAR((2 * parts,)),
            dma((parts,)),
            dma((parts,)),
            dma((parts,)),
            dma((small_steps,)),
            dma((small_steps,)),
        ],
        compiler_params=pltpu.CompilerParams(
            collective_id=1, has_side_effects=True, vmem_limit_bytes=63 * 2**20
        ),
        cost_estimate=pl.CostEstimate(
            flops=4 * rows * width * (n + width + 3 * ff),
            bytes_accessed=80 * 2**20,
            transcendentals=0,
        ),
        name="backward",
    )(*operands)


def finish_body(lay, entries, small, *refs):
    count = (len(refs) - 4) // 2
    sources, targets = refs[:count], refs[count : 2 * count]
    gain_one, gain_two, first_norm, value_norm = refs[2 * count :]
    for source, target in zip(sources, targets):
        target[...] = source[...].astype(target.dtype)

    @pl.when(pl.program_id(0) == 0)
    def _():
        rows = gain_one.shape[0]
        at = pl.ds(pl.multiple_of(lax.axis_index("fsdp") * rows, rows), rows)
        gain_one[...] = small[0, at]
        gain_two[...] = small[1, at]
        first_norm[0, 0] = jnp.sum(small[2:3, :]) / entries
        value_norm[0, 0] = jnp.sum(small[3:4, :]) / entries


def finish_kernel(lay, results):
    output, grad_tokens, grad_first, *totals, small = results
    rows, width = output.shape
    moved = [output, grad_tokens, grad_first, *totals]
    kinds = [BF16, F32, F32] + [F32] * len(totals)

    steps = 2

    def spec(item):
        return pl.BlockSpec((item.shape[0] // steps, item.shape[1]), lambda i: (i, 0))

    shard = width // lay.fs
    line = pl.BlockSpec((shard,), lambda i: (0,))
    scalar = pl.BlockSpec((1, 1), lambda i: (0, 0), memory_space=pltpu.SMEM)
    done = pl.pallas_call(
        functools.partial(finish_body, lay, rows * width * lay.dp * lay.fs),
        grid=(steps,),
        in_specs=[pl.BlockSpec(small.shape, lambda i: (0, 0))] + [spec(item) for item in moved],
        out_specs=[spec(item) for item in moved] + [line, line, scalar, scalar],
        out_shape=[struct(item.shape, kind) for item, kind in zip(moved, kinds)]
        + [struct((shard,), F32)] * 2
        + [struct((1, 1), F32)] * 2,
        compiler_params=pltpu.CompilerParams(vmem_limit_bytes=63 * 2**20),
        cost_estimate=pl.CostEstimate(
            flops=0, bytes_accessed=30 * 2**20, transcendentals=0
        ),
        name="finish",
    )(small, *moved)
    output, grad_tokens, grad_first, qkv, out, gate, up, down, gain_one, gain_two, first, value = done
    return (
        output,
        grad_tokens,
        grad_first,
        gain_one,
        qkv,
        out,
        gain_two,
        gate,
        up,
        down,
        first.reshape(()),
        value.reshape(()),
    )


def body(
    lay,
    tokens,
    first_values,
    lengths,
    gain_one,
    w_qkv,
    w_out,
    gain_two,
    w_gate,
    w_up,
    w_down,
    cotangent,
):
    rows, width = tokens.shape
    tables = tuple(jnp.asarray(table) for table in rotary_tables(rows))
    results = forward_kernel(
        lay, lengths, tokens, first_values, tables, gain_one, gain_two, cotangent, w_qkv, w_out, w_gate, w_up, w_down
    )
    weights, heads, logs, saved, gains, sums = (
        results[:5],
        results[5:8],
        results[8],
        results[9:17],
        results[17],
        results[18],
    )
    results = backward_kernel(
        lay, lengths, tables, gains, sums, logs, weights, (*heads, *saved), tokens, cotangent
    )
    return finish_kernel(lay, results)


def solution(mesh):
    both = P(AXES, None)
    rows = P("fsdp", None)
    in_specs = (both, both, P(AXES), P("fsdp"), rows, rows, P("fsdp"), rows, rows, rows, both)
    out_specs = (both, both, both, P("fsdp"), rows, rows, P("fsdp"), rows, rows, rows, P(), P())
    lay = Layout(mesh.shape["dp"], mesh.shape["fsdp"])
    return jax.shard_map(
        functools.partial(body, lay),
        mesh=mesh,
        in_specs=in_specs,
        out_specs=out_specs,
        check_vma=False,
    )
```

```python
import functools
import math

import jax
import jax.numpy as jnp
import numpy as np
from jax import lax
from jax.experimental import pallas as pl
from jax.experimental.pallas import tpu as pltpu
from jax.sharding import PartitionSpec as P

HEAD_DIM = 64
PAIR = 2 * HEAD_DIM
TILE = 256
GAIN_ROWS = 16
norm_eps = 1e-06
F32 = jnp.float32
BF16 = jnp.bfloat16
AXES = ("dp", "fsdp")
ANY = pl.BlockSpec(memory_space=pl.ANY)


def dot_nn(a, b):
    return lax.dot_general(a, b, (((1,), (0,)), ((), ())), preferred_element_type=F32)


def dot_nt(a, b):
    return lax.dot_general(a, b, (((1,), (1,)), ((), ())), preferred_element_type=F32)


def dot_tn(a, b):
    return lax.dot_general(a, b, (((0,), (0,)), ((), ())), preferred_element_type=F32)


def rotary_tables(count):
    half = HEAD_DIM // 2
    frequency = np.exp(
        -(np.arange(half, dtype=np.float32) * np.float32(2.0) / np.float32(HEAD_DIM))
        * np.float32(math.log(10000.0))
    ).astype(np.float32)
    angles = np.arange(count, dtype=np.float32)[:, None] * frequency[None, :]
    cosine = np.cos(angles.astype(np.float64)).astype(np.float32)
    sine = np.sin(angles.astype(np.float64)).astype(np.float32)
    cosine = np.concatenate([cosine] * 4, axis=1)
    sine = np.concatenate([-sine, sine, -sine, sine], axis=1)
    return cosine, sine


def swap_halves(x):
    half = HEAD_DIM // 2
    lane = lax.broadcasted_iota(jnp.int32, x.shape, 1)
    up = pltpu.roll(x, PAIR - half, 1)
    down = pltpu.roll(x, half, 1)
    return jnp.where((lane % HEAD_DIM) < half, up, down)


class Layout:
    def __init__(self, dp, fs):
        self.dp, self.fs = dp, fs
        self.bits = fs.bit_length() - 1
        self.line = dp // 2


def add_low(a, b):
    return (a.astype(F32) + b.astype(F32)).astype(BF16)


def start(copies):
    for copy in copies:
        copy.start()


def wait(copies):
    for copy in copies:
        copy.wait()


def struct(shape, dtype):
    return jax.ShapeDtypeStruct(shape, dtype)


class Place:
    def __init__(self, lay):
        self.bits, self.count = lay.bits, lay.fs
        self.d, self.f = lax.axis_index("dp"), lax.axis_index("fsdp")
        self.c = lax.rem(self.d, 2)
        self.flips = []
        for i in range(self.bits):
            ahead, back = 1 << i, 1 << (self.bits - 1 - i)
            one = ahead * (1 - 2 * lax.rem(self.f // ahead, 2))
            two = back * (1 - 2 * lax.rem(self.f // back, 2))
            self.flips.append(one + self.c * (two - one))

    def shard(self, m):
        return self.f + sum(self.flips[i] for i in range(self.bits) if (m >> i) & 1)

    def partner(self, i):
        return (self.d, self.f + self.flips[i])

    def sibling(self):
        return (self.d + 1 - 2 * self.c, self.f)

    def above(self):
        return (self.d + 2 - 4 * lax.rem(self.d // 2, 2), self.f)

    def group(self):
        others = []
        for m in range(1, self.count):
            others.append((self.d, self.shard(m)))
        return others


def remote(src, dst, send, recv, device):
    return pltpu.make_async_remote_copy(
        src_ref=src,
        dst_ref=dst,
        send_sem=send,
        recv_sem=recv,
        device_id=device,
        device_id_type=pl.DeviceIdType.MESH,
    )


class Gather:
    def __init__(self, place, own, full, first, total, lifted, sems, slot):
        self.place = place
        send, recv, up_send, up_recv, cross_send, cross_recv, more_send, more_recv = sems
        count = place.count
        rows, side = own.shape[0], total // 2
        column = pl.ds(pl.multiple_of(first + place.c * side, 128), side)
        size = rows // 2 if lifted else rows
        parity = lax.rem(place.d // 2, 2) if lifted else 0
        self.link, self.up, self.cross, self.more = [None], [None], [None], [None]

        def spot(piece, which):
            at = pl.multiple_of(place.shard(piece) * rows + which * size, size)
            return full.at[pl.ds(at, size), column]

        for m in range(1, count):
            step = m.bit_length() - 1
            before = m - (1 << step)
            source = spot(before, parity)
            if before == 0:
                source = own.at[pl.ds(pl.multiple_of(parity * size, size), size), column]
            at = slot * count + m
            self.link.append(
                remote(source, spot(before, parity), send.at[at], recv.at[at], place.partner(step))
            )
            here = spot(m, parity)
            self.cross.append(
                remote(here, here, cross_send.at[at], cross_recv.at[at], place.sibling())
            )
            if lifted:
                there = spot(m, 1 - parity)
                self.up.append(remote(here, here, up_send.at[at], up_recv.at[at], place.above()))
                self.more.append(
                    remote(there, there, more_send.at[at], more_recv.at[at], place.sibling())
                )

    def begin(self, m):
        self.link[m].start()

    def arrived(self, m):
        self.link[m].wait_recv()
        for i in range(m.bit_length(), self.place.bits):
            self.link[m + (1 << i)].start()
        self.cross[m].start()

    def lift(self, m):
        self.up[m].start()

    def landed(self, m):
        self.up[m].wait_recv()
        self.more[m].start()

    def complete(self):
        for copy in self.cross[1:] + self.more[1:]:
            copy.wait_recv()

    def drain(self):
        for copy in self.link[1:] + self.cross[1:] + self.up[1:] + self.more[1:]:
            copy.wait_send()


QK, V, OUT, GATE, UP, DOWN = range(6)
BEGIN, ARRIVE, LIFT, LAND = range(4)
NORMALISE, QUERIES, KEYS, VALUES, HEADS, PROJECT, GATES, UPS, SUM_DOWN = range(4, 13)
FORWARD_LIFTED = (QK, V, GATE, DOWN)
FORWARD_ORDER = (
    (BEGIN, QK, 1), (BEGIN, QK, 2), (NORMALISE, 0, 0), (BEGIN, GATE, 1), (ARRIVE, QK, 1),
    (ARRIVE, QK, 2), (LIFT, QK, 2), (BEGIN, V, 1), (LIFT, QK, 1), (BEGIN, OUT, 1), (BEGIN, V, 2),
    (ARRIVE, V, 1), (BEGIN, GATE, 2), (ARRIVE, V, 2), (ARRIVE, GATE, 1), (ARRIVE, QK, 3),
    (LIFT, QK, 3), (LAND, QK, 2), (ARRIVE, V, 3), (ARRIVE, OUT, 1), (BEGIN, OUT, 2), (LIFT, V, 2),
    (ARRIVE, GATE, 2), (LAND, QK, 1), (BEGIN, UP, 1), (LIFT, V, 1), (LAND, QK, 3), (LIFT, V, 3),
    (QUERIES, 0, 0), (LAND, V, 2), (LIFT, GATE, 1), (ARRIVE, GATE, 3), (BEGIN, DOWN, 1),
    (BEGIN, UP, 2), (LIFT, GATE, 2), (BEGIN, DOWN, 2), (KEYS, 0, 0), (LAND, V, 1), (LAND, V, 3),
    (VALUES, 0, 0), (ARRIVE, OUT, 3), (LIFT, GATE, 3), (HEADS, 0, 0), (HEADS, 0, 0),
    (LAND, GATE, 1), (ARRIVE, OUT, 2), (HEADS, 0, 0), (ARRIVE, UP, 1), (HEADS, 0, 0),
    (ARRIVE, DOWN, 1), (ARRIVE, UP, 2), (LAND, GATE, 2), (LIFT, DOWN, 1), (PROJECT, 0, 0),
    (ARRIVE, DOWN, 2), (LIFT, DOWN, 2), (LAND, GATE, 3), (GATES, 0, 0), (ARRIVE, UP, 3),
    (LAND, DOWN, 1), (UPS, 0, 0), (ARRIVE, DOWN, 3), (LIFT, DOWN, 3), (UPS, 0, 1), (LAND, DOWN, 2),
    (SUM_DOWN, 0, 0), (LAND, DOWN, 3),
)


def forward_body(
    lay,
    lengths,
    in_tokens,
    in_first,
    in_cosine,
    in_sine,
    gain_one_in,
    gain_two_in,
    cotangent,
    in_qkv,
    in_out,
    in_gate,
    in_up,
    in_down,
    full_qkv,
    full_out,
    full_gate,
    full_up,
    full_down,
    out_q,
    out_k,
    out_v,
    logs,
    hidden_one2,
    attended2,
    hidden_two2,
    out_after,
    out_gate,
    out_up,
    out_product,
    grad_down,
    gains,
    sums,
    w_qkv,
    w_out,
    w_gate,
    w_up,
    tokens,
    first,
    cosine,
    sine,
    gain_in,
    gain,
    hidden,
    queries,
    keys,
    values,
    attended,
    after,
    activated,
    low_gate,
    low_up,
    product2,
    cot2,
    grad_low,
    turned,
    send,
    recv,
    up_send,
    up_recv,
    cross_send,
    cross_recv,
    more_send,
    more_recv,
    local,
    gain_send,
    gain_recv,
    swap_send,
    swap_recv,
    write,
):
    place = Place(lay)
    count, c = place.count, place.c
    rows, width = tokens.shape
    shard_rows = in_qkv.shape[0]
    ff = in_gate.shape[1]
    sibling = place.sibling()

    barrier = pltpu.get_barrier_semaphore()
    begins = []
    for i, (source, target) in enumerate(
        ((in_tokens, tokens), (in_cosine, cosine), (in_sine, sine), (in_first, first))
    ):
        begins.append(pltpu.make_async_copy(source, target, local.at[10 + i]))
    start(begins)
    known = [sibling, place.above()] + place.group()
    for device in known:
        pl.semaphore_signal(barrier, inc=1, device_id=device, device_id_type=pl.DeviceIdType.MESH)
    pl.semaphore_wait(barrier, len(known))

    sems = (send, recv, up_send, up_recv, cross_send, cross_recv, more_send, more_recv)

    def gather(who, own, full, first_column, total):
        return Gather(place, own, full, first_column, total, who in FORWARD_LIFTED, sems, who)

    gathers = {
        QK: gather(QK, in_qkv, w_qkv, 0, 2 * width),
        V: gather(V, in_qkv, w_qkv, 2 * width, width),
        OUT: gather(OUT, in_out, w_out, 0, width),
        GATE: gather(GATE, in_gate, w_gate, 0, ff),
        UP: gather(UP, in_up, w_up, 0, ff),
        DOWN: gather(DOWN, in_down, full_down, 0, width),
    }

    seen = {}

    def link(step):
        kind, who, turn = step
        one = gathers[who]
        if kind == BEGIN:
            firsts = [1 << i for i in range(place.bits)]
            for m in firsts[turn - 1 : turn] if count == 4 else firsts * (turn == 1):
                one.begin(m)
            return
        if count == 4:
            pieces = [turn]
        else:
            done = seen[who, kind] = seen.get((who, kind), 0) + 1
            pieces = range(1 + (done - 1) * (count - 1) // 3, 1 + done * (count - 1) // 3)
        for m in pieces:
            {ARRIVE: one.arrived, LIFT: one.lift, LAND: one.landed}[kind](m)

    gain_in[...] = jnp.zeros(gain_in.shape, BF16)
    gain_in[0:1, :] = gain_one_in[...].reshape(1, shard_rows)
    gain_in[1:2, :] = gain_two_in[...].reshape(1, shard_rows)
    gain_at = pl.multiple_of(place.f * shard_rows, shard_rows)
    gain_copies = []
    for m, device in enumerate(place.group()):
        gain_copies.append(
            remote(
                gain_in,
                gain.at[:, pl.ds(gain_at, shard_rows)],
                gain_send.at[m],
                gain_recv.at[m],
                device,
            )
        )
    gain_own = pltpu.make_async_copy(
        gain_in, gain.at[:, pl.ds(gain_at, shard_rows)], local.at[4]
    )
    start(gain_copies + [gain_own])
    order = list(FORWARD_ORDER)
    while order[0][0] == BEGIN:
        link(order.pop(0))
    own_rows = pl.ds(gain_at, shard_rows)
    locals_of = {}
    for slot, (name, source, full) in enumerate(
        ((QK, in_qkv, w_qkv), (OUT, in_out, w_out), (GATE, in_gate, w_gate), (UP, in_up, w_up))
    ):
        locals_of[name] = pltpu.make_async_copy(source, full.at[own_rows, :], local.at[slot])
        locals_of[name].start()
    half = width // 2
    down_rows = in_down.shape[0]
    down_at = pl.ds(pl.multiple_of(place.f * down_rows, down_rows), down_rows)
    down_in, down_out = [], []
    for i in range(2):
        stage = grad_low.at[pl.ds(i * down_rows, down_rows), :]
        side = pl.ds(i * half, half)
        down_in.append(pltpu.make_async_copy(in_down.at[:, side], stage, local.at[6 + i]))
        down_out.append(pltpu.make_async_copy(stage, full_down.at[down_at, side], local.at[8 + i]))
    start(down_in)

    writes = []

    def put(source, target):
        copy = pltpu.make_async_copy(source, target, write.at[len(writes)])
        copy.start()
        writes.append(copy)

    swaps = []

    def swap(source, target):
        slot = len(swaps)
        copy = remote(source, target, swap_send.at[slot], swap_recv.at[slot], sibling)
        copy.start()
        swaps.append(copy)
        return copy

    def share(source, target):
        put(source, target.at[pl.ds(0, rows), :])
        return swap(source, target.at[pl.ds(rows, rows), :])

    theirs = pl.multiple_of((1 - c) * half, 128)
    ours = pl.multiple_of(c * half, 128)
    cot_swap = swap(cotangent.at[:, pl.ds(theirs, half)], cot2.at[pl.ds(rows, rows), :])
    cot_own = pltpu.make_async_copy(
        cotangent.at[:, pl.ds(ours, half)], cot2.at[pl.ds(0, rows), :], local.at[5]
    )
    cot_own.start()

    block = min(TILE, rows)
    length = lengths[0]
    pairs = width // PAIR
    hidden_two = low_up.at[:, pl.ds(0, width)]
    two_swap, two_put, product_swaps = [], [], []

    def by_rows(step):
        @pl.loop(0, rows // block)
        def _(i):
            step(pl.ds(pl.multiple_of(i * block, block), block))

    def normalise():
        begins[0].wait()
        inputs = tokens[...].astype(F32)
        inverse = lax.rsqrt(jnp.mean(inputs * inputs, axis=-1, keepdims=True) + norm_eps)
        for copy in gain_copies:
            copy.wait_recv()
        gain_own.wait()
        gains[0:1, :] = gain[0:1, :].astype(F32)
        gains[1:2, :] = gain[1:2, :].astype(F32)
        gains[2:8, :] = jnp.zeros((6, width), F32)
        hidden[...] = (inputs * inverse * gains[0:1, :]).astype(BF16)
        share(hidden, hidden_one2)
        wait(down_in)
        start(down_out)
        sums[...] = jnp.zeros(sums.shape, F32)
        logs[...] = jnp.zeros(logs.shape, F32)

    def rotated(which, out, scale):
        def step(at):
            cos, sin = cosine[at, :], sine[at, :]
            raw = dot_nn(hidden[at, :], w_qkv[:, which * width : (which + 1) * width])
            for p in range(width // PAIR):
                x = raw[:, p * PAIR : (p + 1) * PAIR]
                low = (x * cos + swap_halves(x) * sin).astype(BF16)
                out[at, p * PAIR : (p + 1) * PAIR] = low * jnp.asarray(scale, BF16)

        by_rows(step)

    def mix(at):
        raw = dot_nn(hidden[at, :], w_qkv[:, 2 * width : 3 * width])
        kept = first[at, :].astype(F32)
        mixed = 0.5 * raw + 0.5 * kept
        values[at, :] = mixed.astype(BF16)
        sums[0:1, :] += jnp.sum(kept * kept, axis=0, keepdims=True)
        sums[1:2, :] += jnp.sum(mixed * mixed, axis=0, keepdims=True)

    turn = 2

    def attend(links):
        @pl.loop(0, pairs // turn)
        def _(i):
            for j in range(turn):
                attend_pair(i * turn + j, turned.at[j])
            for after_turn, steps in enumerate(links):
                if steps:

                    @pl.when(i == after_turn)
                    def _():
                        for step in steps:
                            link(step)

    def attend_pair(p, turned):
        at = pl.ds(pl.multiple_of(p * PAIR, PAIR), PAIR)
        q, k = queries[:, at], keys[:, at]
        v_t = values[:, at].T
        lane = lax.broadcasted_iota(jnp.int32, (rows, PAIR), 1)
        for head in range(2):
            inside = (lane // HEAD_DIM) == head
            k_head = jnp.where(inside, k, jnp.zeros_like(k))
            v_head = v_t[head * HEAD_DIM : (head + 1) * HEAD_DIM]
            for b in range(rows // block):
                upto = (b + 1) * block
                scores = dot_nt(k_head[:upto], q[b * block : upto])
                key = lax.broadcasted_iota(jnp.int32, scores.shape, 0)
                query = lax.broadcasted_iota(jnp.int32, (1, block), 1) + b * block
                allowed = key <= jnp.minimum(query, length - 1)
                scores = jnp.where(allowed, scores, -1e30)
                peak = jnp.max(scores, axis=0, keepdims=True)
                expo = jnp.exp(scores - peak)
                total = jnp.sum(expo, axis=0, keepdims=True)
                logs[p, head : head + 1, b * block : upto] = peak + jnp.log(total)
                out = dot_nn(v_head[:, :upto], expo.astype(BF16)) * (1.0 / total)
                turned[head * HEAD_DIM : (head + 1) * HEAD_DIM, b * block : upto] = out
        attended[:, at] = turned[...].T.astype(BF16)

    def project(at):
        x = tokens[at, :].astype(F32) + dot_nn(attended[at, :], w_out[...])
        after[at, :] = x
        scale = lax.rsqrt(jnp.mean(x * x, axis=-1, keepdims=True) + norm_eps)
        low_up[at, 0:width] = (x * scale * gains[1:2, :]).astype(BF16)

    def gate_rows(at):
        raw = dot_nn(low_up[at, 0:width], w_gate[...])
        low_gate[at, :] = raw.astype(BF16)
        activated[at, :] = raw * jax.nn.sigmoid(raw)

    def up_rows(at):
        up_proj = dot_nn(low_up[at, 0:width], w_up[...])
        product2[at, :] = (activated[at, :] * up_proj).astype(BF16)
        low_up[at, :] = up_proj.astype(BF16)

    def compute(kind, part):
        if kind == NORMALISE:
            normalise()
        elif kind == QUERIES:
            wait(begins[1:])
            locals_of[QK].wait()
            gathers[QK].complete()
            rotated(0, queries, HEAD_DIM**-0.5)
            put(queries, out_q)
        elif kind == KEYS:
            rotated(1, keys, 1.0)
            put(keys, out_k)
        elif kind == VALUES:
            gathers[V].complete()
            put(w_qkv, full_qkv)
            by_rows(mix)
            put(values, out_v)
        elif kind == PROJECT:
            share(attended, attended2)
            locals_of[OUT].wait()
            gathers[OUT].complete()
            put(w_out, full_out)
            by_rows(project)
            put(after, out_after)
            two_swap.append(share(hidden_two, hidden_two2))
            two_put.append(writes[-1])
        elif kind == GATES:
            locals_of[GATE].wait()
            gathers[GATE].complete()
            put(w_gate, full_gate)
            by_rows(gate_rows)
            put(low_gate, out_gate)
        elif kind == UPS and part == 0:
            locals_of[UP].wait()
            gathers[UP].complete()
            put(w_up, full_up)
            two_swap[0].wait_send()
            two_put[0].wait()
            steps = []
            while order[0][0] <= LAND:
                steps.append(order.pop(0))
            up_parts(steps)
        elif kind == UPS:
            put(low_up, out_up)
            put(product2.at[pl.ds(0, rows), :], out_product)
        else:
            wait(down_out)
            cot_own.wait()
            cot_swap.wait_recv()
            for copy in product_swaps:
                copy.wait_recv()

            size = ff // TILE // 2 * TILE
            for first_row, last_row in ((0, size), (size, ff)):

                @pl.loop(first_row // TILE, last_row // TILE)
                def _(i):
                    at = pl.ds(pl.multiple_of(i * TILE, TILE), TILE)
                    grad_low[at, :] = dot_tn(product2[:, at], cot2[...]).astype(BF16)

                part = pl.ds(first_row, last_row - first_row)
                put(grad_low.at[part, :], grad_down.at[part, :])

    def up_parts(steps):
        size = rows // 2
        for i in range(2):
            part = pl.ds(i * size, size)
            there = pl.ds(rows + i * size, size)
            slot = len(swaps)
            copy = remote(
                product2.at[part, :], product2.at[there, :], swap_send.at[slot], swap_recv.at[slot], sibling
            )
            swaps.append(copy)
            product_swaps.append(copy)

        @pl.loop(0, 2)
        def _(i):
            up_rows(pl.ds(pl.multiple_of(i * size, size), size))

            @pl.when(i == 0)
            def _():
                product_swaps[0].start()
                for step in steps:
                    link(step)

            @pl.when(i == 1)
            def _():
                product_swaps[1].start()

    while order:
        step = order.pop(0)
        if step[0] <= LAND:
            link(step)
        elif step[0] == HEADS:
            turns = pairs // turn
            links, at = [[] for _ in range(4)], 0
            while order and (order[0][0] <= LAND or order[0][0] == HEADS):
                if order[0][0] == HEADS:
                    order.pop(0)
                    at += 1
                else:
                    links[at].append(order.pop(0))
            spread = [[] for _ in range(turns)]
            for i, steps in enumerate(links):
                spread[(i + 1) * turns // 4 - 1] += steps
            attend(spread)
        else:
            compute(step[0], step[2])

    gathers[DOWN].complete()
    for one in gathers.values():
        one.drain()
    for copy in gain_copies:
        copy.wait_send()
    waited = [cot_swap, *product_swaps]
    for copy in swaps:
        if not any(copy is item for item in waited):
            copy.wait_recv()
        if copy is not two_swap[0]:
            copy.wait_send()
    for copy in writes:
        if copy is not two_put[0]:
            copy.wait()


def forward_kernel(lay, lengths, tokens, first, tables, gain_one, gain_two, cotangent, w_qkv, w_out, w_gate, w_up, w_down):
    count = lay.fs
    rows, width = tokens.shape
    n, ff = w_qkv.shape[1], w_gate.shape[1]
    half = width // 2
    pairs = width // PAIR
    big = struct((rows, width), BF16)
    wide = struct((rows, ff), BF16)
    two = struct((2 * rows, width), BF16)
    dma = pltpu.SemaphoreType.DMA
    vmem = pl.BlockSpec(memory_space=pltpu.VMEM)
    weights = [(width, n), (width, width), (width, ff), (width, ff), (ff, width)]
    out_shape = (
        [struct(shape, BF16) for shape in weights]
        + [big, big, big, struct((pairs, 8, rows), F32)]
        + [two, two, two, struct((rows, width), F32), wide, wide, wide]
        + [struct((ff, half), BF16), struct((8, width), F32), struct((8, width), F32)]
    )
    out_specs = [ANY] * 8 + [vmem] + [ANY] * 8 + [vmem, vmem]
    return pl.pallas_call(
        functools.partial(forward_body, lay),
        in_specs=[pl.BlockSpec(memory_space=pltpu.SMEM)] + [ANY] * 4 + [vmem] * 2 + [ANY] * 6,
        out_specs=out_specs,
        out_shape=out_shape,
        scratch_shapes=[
            pltpu.VMEM((width, n), BF16),
            pltpu.VMEM((width, width), BF16),
            pltpu.VMEM((width, ff), BF16),
            pltpu.VMEM((width, ff), BF16),
            pltpu.VMEM((rows, width), BF16),
            pltpu.VMEM((rows, width), BF16),
            pltpu.VMEM((rows, PAIR), F32),
            pltpu.VMEM((rows, PAIR), F32),
            pltpu.VMEM((GAIN_ROWS, width // count), BF16),
            pltpu.VMEM((GAIN_ROWS, width), BF16),
            pltpu.VMEM((rows, width), BF16),
            pltpu.VMEM((rows, width), BF16),
            pltpu.VMEM((rows, width), BF16),
            pltpu.VMEM((rows, width), BF16),
            pltpu.VMEM((rows, width), BF16),
            pltpu.VMEM((rows, width), F32),
            pltpu.VMEM((rows, ff), F32),
            pltpu.VMEM((rows, ff), BF16),
            pltpu.VMEM((rows, ff), BF16),
            pltpu.VMEM((2 * rows, ff), BF16),
            pltpu.VMEM((2 * rows, half), BF16),
            pltpu.VMEM((ff, half), BF16),
            pltpu.VMEM((2, PAIR, rows), F32),
            *[dma((6 * count,))] * 8,
            dma((14,)),
            dma((count - 1,)),
            dma((count - 1,)),
            dma((6,)),
            dma((6,)),
            dma((18,)),
        ],
        compiler_params=pltpu.CompilerParams(
            collective_id=0, has_side_effects=True, vmem_limit_bytes=62 * 2**20
        ),
        cost_estimate=pl.CostEstimate(
            flops=2 * rows * width * (n + width + 3 * ff),
            bytes_accessed=60 * 2**20,
            transcendentals=0,
        ),
        name="forward",
    )(lengths, tokens, first, *tables, gain_one, gain_two, cotangent, w_qkv, w_out, w_gate, w_up, w_down)


def rms_back(grad, normed, inverse):
    return inverse * (grad - normed * jnp.mean(grad * normed, axis=-1, keepdims=True))


class Line:
    def __init__(self, lay, place):
        size = lay.line
        r = place.d // 2
        self.half = size // 2
        upper = r // self.half
        toward = 1 - 2 * upper
        self.depth = r * toward + upper * (size - 1)
        self.next = (place.d + 2 * toward, place.f)
        self.prev = (place.d - 2 * toward, place.f)
        self.middle = self.depth == self.half - 1
        self.inner = self.depth > 0
        self.others = []
        reach = 1
        while reach < size:
            self.others.append((place.d + 2 * reach * (1 - 2 * lax.rem(r // reach, 2)), place.f))
            reach *= 2


def signal(sem, device):
    pl.semaphore_signal(sem, inc=1, device_id=device, device_id_type=pl.DeviceIdType.MESH)


class Reduce:
    def __init__(
        self, place, line, slot, window, held, sources, first, later, final, column, sems
    ):
        send, recv, z_send, z_recv, credit, f_local, f_send, f_recv = sems
        self.place, self.line, self.held, self.window = place, line, held, window
        self.bits, count = place.bits, place.count
        self.count = count
        base = slot * count
        half = count // 2
        self.steps, self.lands = [], []
        at = 0
        for i in range(self.bits):
            blocks = count >> (i + 1)
            copies, lands = [], []
            for q in range(blocks):
                source = sources[q] if i == 0 else held.at[blocks + q, window]
                land = first.at[q, window] if i == 0 else later.at[at + q, window]
                index = base + q if i == 0 else base + half + at + q
                lands.append(land)
                copies.append(remote(source, land, send.at[index], recv.at[index], place.partner(i)))
            if i > 0:
                at += blocks
            self.steps.append(copies)
            self.lands.append(lands)
        mine, inner, outer = held.at[0, window], first.at[0, window], first.at[1, window]
        two = 2 * slot
        self.hops = {
            "in": remote(mine, inner, z_send.at[two], z_recv.at[two], line.next),
            "middle": remote(mine, outer, z_send.at[two], z_recv.at[two + 1], line.next),
            "back": remote(inner, outer, z_send.at[two + 1], z_recv.at[two + 1], line.prev),
            "out": remote(outer, outer, z_send.at[two + 1], z_recv.at[two + 1], line.prev),
        }
        self.mine, self.inner, self.outer = mine, inner, outer
        spot = final.at[window, column]
        self.ends = []
        for source in (inner, outer):
            self.ends.append(
                (
                    pltpu.make_async_copy(source, spot, f_local.at[slot]),
                    remote(source, spot, f_send.at[slot], f_recv.at[slot], place.sibling()),
                )
            )
        self.from_next, self.from_prev = credit.at[two], credit.at[two + 1]

    def begin(self, q):
        self.steps[0][q].start()

    def block(self, i, q):
        blocks = self.count >> (i + 1)
        self.steps[i][q].wait_recv()
        here = self.held.at[q, self.window]
        here[...] = add_low(here[...], self.lands[i][q][...])
        if i + 1 < self.bits and q >= blocks // 2:
            self.steps[i + 1][q - blocks // 2].start()

    def leaving(self):
        half = self.count // 2
        for q in reversed(range(half // 2, half)):
            self.block(0, q)

    def staying(self):
        for q in reversed(range(self.count // 4)):
            self.block(0, q)
        line = self.line

        @pl.when(line.middle)
        def _():
            signal(self.from_next, line.next)

        @pl.when(jnp.logical_not(line.middle))
        def _():
            signal(self.from_prev, line.next)

        @pl.when(line.inner)
        def _():
            signal(self.from_next, line.prev)

    def rest(self):
        for i in range(1, self.bits):
            for q in reversed(range(self.count >> (i + 1))):
                self.block(i, q)

        @pl.when(jnp.logical_not(self.line.inner))
        def _():
            self.onward()

    def onward(self):
        line = self.line
        pl.semaphore_wait(self.from_next, 1)

        @pl.when(line.middle)
        def _():
            self.hops["middle"].start()

        @pl.when(jnp.logical_not(line.middle))
        def _():
            self.hops["in"].start()

    def inward(self):
        @pl.when(self.line.inner)
        def _():
            self.hops["in"].wait_recv()
            self.mine[...] = add_low(self.mine[...], self.inner[...])
            self.onward()

    def finish(self, which):
        local, cross = self.ends[which]
        local.start()
        cross.start()

    def across(self):
        line = self.line

        @pl.when(line.middle)
        def _():
            self.hops["middle"].wait_recv()
            self.inner[...] = add_low(self.mine[...], self.outer[...])

            @pl.when(line.inner)
            def _():
                pl.semaphore_wait(self.from_prev, 1)
                self.hops["back"].start()

            self.finish(0)

    def outward(self):
        line = self.line
        if line.half == 1:
            return

        @pl.when(jnp.logical_not(line.middle))
        def _():
            self.hops["out"].wait_recv()

            @pl.when(line.inner)
            def _():
                pl.semaphore_wait(self.from_prev, 1)
                self.hops["out"].start()

            self.finish(1)

    def drain(self):
        for copies in self.steps:
            for copy in copies:
                copy.wait_send()
        self.hops["in"].wait_send()

        @pl.when(self.line.inner)
        def _():
            self.hops["out"].wait_send()

        local, cross = self.ends[0]
        local.wait()
        cross.wait_send()
        cross.wait_recv()


W_DOWN, W_GATE, W_UP, W_OUT, W_V, W_K, W_Q = range(7)
BACKWARD_PARTS = (2, 2, 4, 2, 2, 4, 4)
LEAVING, STAYING, REST, INWARD, ACROSS, OUTWARD, SMALL = range(7)
BLOCKS, MLP_TILES, NORM_TWO, ATTEND_GRAD, HEAD_PAIRS, QKV_TILES, NORM_ONE = range(7, 14)
BACKWARD_ORDER = (
    (LEAVING, W_DOWN, 0), (STAYING, W_DOWN, 0), (BLOCKS, W_GATE, 3), (BLOCKS, W_GATE, 2),
    (LEAVING, W_DOWN, 1), (BLOCKS, W_GATE, 1), (REST, W_DOWN, 0), (BLOCKS, W_GATE, 0),
    (BLOCKS, W_UP, 3), (BLOCKS, W_UP, 2), (BLOCKS, W_UP, 1), (BLOCKS, W_UP, 0),
    (STAYING, W_DOWN, 1), (MLP_TILES, 0, 0), (REST, W_DOWN, 1), (INWARD, W_DOWN, 0),
    (LEAVING, W_GATE, 0), (MLP_TILES, 0, 1), (MLP_TILES, 0, 2), (MLP_TILES, 0, 3),
    (LEAVING, W_GATE, 1), (NORM_TWO, 0, 0), (INWARD, W_DOWN, 1), (ACROSS, W_DOWN, 0),
    (ATTEND_GRAD, 0, 0), (STAYING, W_GATE, 0), (REST, W_GATE, 0), (BLOCKS, W_OUT, 3),
    (BLOCKS, W_OUT, 2), (BLOCKS, W_OUT, 1), (BLOCKS, W_OUT, 0), (HEAD_PAIRS, 0, 0),
    (STAYING, W_GATE, 1), (REST, W_GATE, 1), (HEAD_PAIRS, 0, 1), (LEAVING, W_UP, 0),
    (LEAVING, W_UP, 1), (INWARD, W_GATE, 0), (ACROSS, W_DOWN, 1), (OUTWARD, W_DOWN, 0),
    (HEAD_PAIRS, 0, 2), (LEAVING, W_UP, 2), (HEAD_PAIRS, 0, 3), (LEAVING, W_UP, 3),
    (HEAD_PAIRS, 0, 4), (INWARD, W_GATE, 1), (HEAD_PAIRS, 0, 5), (ACROSS, W_GATE, 0),
    (STAYING, W_UP, 0), (REST, W_UP, 0), (OUTWARD, W_DOWN, 1), (HEAD_PAIRS, 0, 6),
    (STAYING, W_UP, 1), (REST, W_UP, 1), (HEAD_PAIRS, 0, 7), (INWARD, W_UP, 0), (ACROSS, W_GATE, 1),
    (STAYING, W_UP, 2), (LEAVING, W_OUT, 0), (REST, W_UP, 2), (STAYING, W_UP, 3), (REST, W_UP, 3),
    (LEAVING, W_OUT, 1), (OUTWARD, W_GATE, 0), (INWARD, W_UP, 1), (BLOCKS, W_V, 3),
    (BLOCKS, W_V, 2), (BLOCKS, W_V, 1), (STAYING, W_OUT, 0), (BLOCKS, W_V, 0), (REST, W_OUT, 0),
    (ACROSS, W_UP, 0), (BLOCKS, W_K, 3), (BLOCKS, W_K, 2), (INWARD, W_UP, 2), (STAYING, W_OUT, 1),
    (BLOCKS, W_K, 1), (REST, W_OUT, 1), (BLOCKS, W_K, 0), (LEAVING, W_V, 0), (ACROSS, W_UP, 1),
    (OUTWARD, W_GATE, 1), (BLOCKS, W_Q, 3), (LEAVING, W_V, 1), (INWARD, W_UP, 3), (BLOCKS, W_Q, 2),
    (BLOCKS, W_Q, 1), (BLOCKS, W_Q, 0), (QKV_TILES, 0, 0), (INWARD, W_OUT, 0), (ACROSS, W_UP, 2),
    (STAYING, W_V, 0), (REST, W_V, 0), (OUTWARD, W_UP, 0), (QKV_TILES, 0, 1), (LEAVING, W_K, 0),
    (INWARD, W_OUT, 1), (LEAVING, W_K, 1), (ACROSS, W_UP, 3), (LEAVING, W_K, 2), (STAYING, W_V, 1),
    (REST, W_V, 1), (LEAVING, W_K, 3), (INWARD, W_V, 0), (ACROSS, W_OUT, 0), (OUTWARD, W_UP, 1),
    (QKV_TILES, 0, 2), (STAYING, W_K, 0), (REST, W_K, 0), (ACROSS, W_OUT, 1), (STAYING, W_K, 1),
    (REST, W_K, 1), (OUTWARD, W_UP, 2), (QKV_TILES, 0, 3), (INWARD, W_V, 1), (INWARD, W_K, 0),
    (LEAVING, W_Q, 0), (ACROSS, W_V, 0), (LEAVING, W_Q, 1), (STAYING, W_K, 2), (REST, W_K, 2),
    (LEAVING, W_Q, 2), (INWARD, W_K, 1), (STAYING, W_K, 3), (REST, W_K, 3), (LEAVING, W_Q, 3),
    (OUTWARD, W_UP, 3), (OUTWARD, W_OUT, 0), (NORM_ONE, 0, 0), (INWARD, W_K, 2), (INWARD, W_K, 3),
    (ACROSS, W_V, 1), (ACROSS, W_K, 0), (ACROSS, W_K, 1), (STAYING, W_Q, 0), (REST, W_Q, 0),
    (STAYING, W_Q, 1), (REST, W_Q, 1), (SMALL, 0, 1), (STAYING, W_Q, 2), (REST, W_Q, 2),
    (ACROSS, W_K, 2), (STAYING, W_Q, 3), (REST, W_Q, 3), (OUTWARD, W_OUT, 1), (OUTWARD, W_V, 0),
    (ACROSS, W_K, 3), (INWARD, W_Q, 0), (OUTWARD, W_V, 1), (SMALL, 0, 2), (INWARD, W_Q, 1),
    (OUTWARD, W_K, 0), (INWARD, W_Q, 2), (SMALL, 0, 3), (ACROSS, W_Q, 0), (OUTWARD, W_K, 1),
    (INWARD, W_Q, 3), (OUTWARD, W_K, 2), (ACROSS, W_Q, 1), (SMALL, 0, 4), (OUTWARD, W_K, 3),
    (ACROSS, W_Q, 2), (OUTWARD, W_Q, 0), (ACROSS, W_Q, 3), (SMALL, 0, 5), (OUTWARD, W_Q, 1),
    (OUTWARD, W_Q, 2), (OUTWARD, W_Q, 3),
)


def backward_body(
    lay,
    lengths,
    in_cosine,
    in_sine,
    gains,
    sums,
    in_logs,
    full_qkv,
    full_out,
    full_gate,
    full_up,
    full_down,
    in_q,
    in_k,
    in_v,
    hidden_one2,
    attended2,
    hidden_two2,
    in_after,
    in_gate,
    in_up,
    in_product,
    in_grad_down,
    tokens,
    cotangent,
    output,
    grad_tokens,
    grad_first,
    sum_qkv,
    sum_out,
    sum_gate,
    sum_up,
    sum_down,
    small,
    cosine,
    sine,
    logs,
    gate,
    up,
    product,
    ring,
    w_out,
    one,
    two,
    three,
    cot,
    left,
    right,
    low,
    attend_grad,
    gate_sib,
    up_sib,
    low_sib,
    q_sib,
    k_sib,
    v_sib,
    held_down,
    held_gate,
    held_up,
    held_narrow,
    first_down,
    first_gate,
    first_up,
    first_narrow,
    later_down,
    later_gate,
    later_up,
    later_narrow,
    small_land,
    turned,
    load_sem,
    ring_sem,
    swap_send,
    swap_recv,
    write_sem,
    send,
    recv,
    z_send,
    z_recv,
    credit,
    f_local,
    f_send,
    f_recv,
    small_send,
    small_recv,
):
    place = Place(lay)
    line = Line(lay, place)
    count, c = place.count, place.c
    sibling = place.sibling()
    rows, width = cot.shape
    ff = gate.shape[1]
    side, narrow = ff // 2, width // 2
    block = min(TILE, rows)
    bits = place.bits

    barrier = pltpu.get_barrier_semaphore()
    partners = [place.partner(i) for i in range(bits)]
    known = [sibling] + partners + line.others + [line.next]
    for device in known:
        signal(barrier, device)

    @pl.when(line.inner)
    def _():
        signal(barrier, line.prev)
        pl.semaphore_wait(barrier, len(known) + 1)

    @pl.when(jnp.logical_not(line.inner))
    def _():
        pl.semaphore_wait(barrier, len(known))

    loads = {}

    def load(name, source, target):
        copy = pltpu.make_async_copy(source, target, load_sem.at[len(loads)])
        copy.start()
        loads[name] = copy

    writes = []

    def put(source, target):
        copy = pltpu.make_async_copy(source, target, write_sem.at[len(writes)])
        copy.start()
        writes.append(copy)
        return copy

    swaps = []

    def swap(source, target, begin=True):
        slot = len(swaps)
        copy = remote(source, target, swap_send.at[slot], swap_recv.at[slot], sibling)
        if begin:
            copy.start()
        swaps.append(copy)
        return copy

    def shard_of(p):
        m = sum(((p >> i) & 1) << (bits - 1 - i) for i in range(bits))
        return place.shard(m)

    sems = (send, recv, z_send, z_recv, credit, f_local, f_send, f_recv)
    half = count // 2
    down_rows = in_grad_down.shape[0] // count
    shard_rows = sum_qkv.shape[0]

    def down_block(p, window=None):
        at = pl.multiple_of(shard_of(p) * down_rows, down_rows)
        if window is None:
            return in_grad_down.at[pl.ds(at, down_rows), :]
        return in_grad_down.at[pl.ds(at + window.start, window.size), :]

    reduces = {}

    def reduce_of(name, held, first, later, final, offset, size):
        parts = BACKWARD_PARTS[name]
        part_rows = held.shape[1] // parts
        for part in range(parts):
            window = pl.ds(part * part_rows, part_rows)
            if name == W_DOWN:
                sources = [down_block(half + q, window) for q in range(half)]
            else:
                sources = [held.at[half + q, window] for q in range(half)]
            column = pl.ds(pl.multiple_of(offset + c * size, 128), size)
            reduces[name, part] = Reduce(
                place, line, len(reduces), window, held, sources, first, later, final, column, sems
            )

    def narrow_of(index, name, final, offset):
        at = index * count
        reduce_of(
            name,
            held_narrow.at[pl.ds(at, count)],
            first_narrow.at[pl.ds(index * half, half)],
            later_narrow.at[pl.ds(index * (half - 1), half - 1)],
            final,
            offset,
            narrow,
        )

    reduce_of(W_DOWN, held_down, first_down, later_down, sum_down, 0, narrow)
    reduce_of(W_GATE, held_gate, first_gate, later_gate, sum_gate, 0, side)
    reduce_of(W_UP, held_up, first_up, later_up, sum_up, 0, side)
    narrow_of(0, W_OUT, sum_out, 0)
    narrow_of(1, W_V, sum_qkv, 2 * width)
    narrow_of(2, W_K, sum_qkv, width)
    narrow_of(3, W_Q, sum_qkv, 0)

    def parts_of(name):
        return [reduces[name, i] for i in range(BACKWARD_PARTS[name])]

    smalls = []

    def small_step():
        slot = len(smalls)
        device = ([sibling] + partners + line.others)[slot]
        copy = remote(
            small_land.at[2 * slot],
            small_land.at[2 * slot + 1],
            small_send.at[slot],
            small_recv.at[slot],
            device,
        )
        small_land[2 * slot] = small[...]
        copy.start()
        smalls.append(copy)

    def small_take():
        smalls[-1].wait_recv()
        small[...] += small_land[2 * len(smalls) - 1]

    small_count = 1 + bits + len(line.others)

    def link(step):
        kind, who, part = step
        if kind == SMALL:
            while True:
                small_take()
                if len(smalls) == small_count:
                    return
                small_step()
                if part < 5:
                    return
        reduce = reduces[who, part]
        {
            LEAVING: reduce.leaving,
            STAYING: reduce.staying,
            REST: reduce.rest,
            INWARD: reduce.inward,
            ACROSS: reduce.across,
            OUTWARD: reduce.outward,
        }[kind]()

    for reduce in parts_of(W_DOWN):
        for q in reversed(range(half)):
            reduce.begin(q)

    tile = min(TILE, side)
    whole_tiles, rest = side // tile, side % tile

    def ring_copy(row, slot, size):
        return pltpu.make_async_copy(
            full_down.at[pl.ds(row, size), :],
            ring.at[slot, pl.ds(0, size), pl.ds(0, width)],
            ring_sem.at[slot],
        )

    theirs = pl.multiple_of((1 - c) * side, 128)
    ours = pl.multiple_of(c * side, 128)
    ring_copy(theirs, 0, tile).start()
    load("gate", in_gate, gate)
    load("up", in_up, up)
    load("cot", cotangent, cot)
    load("product", in_product, product)
    load("after", in_after, one)
    load("left", hidden_two2, left)
    down_loads = []
    for q in range(half):
        copy = pltpu.make_async_copy(down_block(q), held_down.at[q], load_sem.at[17 + q])
        copy.start()
        down_loads.append(copy)
    load("out", full_out, w_out)
    load("right", attended2, right)
    load("cosine", in_cosine, cosine)
    load("sine", in_sine, sine)
    load("logs", in_logs, logs)
    for name in ("gate", "up", "cot", "product", "after"):
        loads[name].wait()
    two[...] = one[...]

    def down_tile(at, slot, size):
        rows_of = ring[slot, 0:size, 0:width]
        grad_product = dot_nt(cot[...], rows_of)
        gate_pre = gate[:, pl.ds(at, size)].astype(F32)
        up_proj = up[:, pl.ds(at, size)].astype(F32)
        sigma = jax.nn.sigmoid(gate_pre)
        gate[:, pl.ds(at, size)] = (
            grad_product * up_proj * sigma * (1.0 + gate_pre * (1.0 - sigma))
        ).astype(BF16)
        up[:, pl.ds(at, size)] = (grad_product * (gate_pre * sigma)).astype(BF16)
        two[...] += dot_nn(product[:, pl.ds(at, size)], rows_of)

    gate_swap = swap(gate.at[:, pl.ds(theirs, side)], gate_sib, begin=False)
    up_swap = swap(up.at[:, pl.ds(theirs, side)], up_sib, begin=False)

    @pl.loop(0, 2)
    def _(turn):
        base = pl.multiple_of(lax.rem(1 - c + turn, 2) * side, 128)

        @pl.loop(0, whole_tiles)
        def _(t):
            slot = lax.rem(t, 2)
            at = pl.multiple_of(base + t * tile, 128)
            ring_copy(at, slot, tile).wait()

            @pl.when(t + 1 < whole_tiles)
            def _():
                ring_copy(pl.multiple_of(at + tile, 128), 1 - slot, tile).start()

            if rest:

                @pl.when(t + 1 == whole_tiles)
                def _():
                    ring_copy(pl.multiple_of(at + tile, 128), 2, rest).start()

            down_tile(at, slot, tile)

        @pl.when(turn == 0)
        def _():
            ring_copy(ours, 0, tile).start()

        if rest:
            at = pl.multiple_of(base + whole_tiles * tile, 128)
            ring_copy(at, 2, rest).wait()
            down_tile(at, 2, rest)

        @pl.when(turn == 0)
        def _():
            gate_swap.start()
            up_swap.start()

    low[...] = two[...].astype(BF16)
    output_put = put(low, output)
    load("q", in_q, product.at[:, pl.ds(0, width)])
    load("k", in_k, product.at[:, pl.ds(width, width)])

    def tile_copies(i):
        at = pl.ds(pl.multiple_of(i * block_w, block_w), block_w)
        slot = lax.rem(i, 2)
        return (
            pltpu.make_async_copy(
                full_gate.at[at, :], ring.at[slot, :, pl.ds(0, ff)], ring_sem.at[slot]
            ),
            pltpu.make_async_copy(
                full_up.at[at, :], ring.at[2 + slot, :, pl.ds(0, ff)], ring_sem.at[2 + slot]
            ),
        )

    block_w = min(TILE, width)
    start(tile_copies(0))
    start(tile_copies(1))

    def shard_at(p):
        flips = [place.flips[bits - 1 - i] * lax.rem(p // (1 << i), 2) for i in range(bits)]
        return place.f + sum(flips)

    def grad_blocks(who, both, own, other, links):
        parts = parts_of(who)
        held = parts[0].held

        @pl.loop(0, count)
        def _(i):
            p = count - 1 - i
            at = pl.ds(pl.multiple_of(shard_at(p) * shard_rows, 128), shard_rows)
            held[p] = (
                dot_tn(both[0:rows, at], own()) + dot_tn(both[rows : 2 * rows, at], other())
            ).astype(BF16)
            for q in range(half):

                @pl.when(p == half + q)
                def _():
                    for part in parts:
                        part.begin(q)

            between(i, links)

    def ours_of(ref, offset, size):
        at = pl.ds(pl.multiple_of(offset + c * size, 128), size)
        return lambda: ref[:, at]

    tiles = width // block_w

    def between(turn, links):
        for after, steps in enumerate(links):
            if steps:

                @pl.when(turn == after)
                def _():
                    for step in steps:
                        link(step)

    def back_tiles(links):
        @pl.loop(0, tiles)
        def _(i):
            wait(tile_copies(i))
            slot = lax.rem(i, 2)
            at = pl.ds(pl.multiple_of(i * block_w, block_w), block_w)
            two[:, at] = dot_nt(gate[...], ring[slot, :, 0:ff]) + dot_nt(
                up[...], ring[2 + slot, :, 0:ff]
            )

            @pl.when(i + 2 < tiles)
            def _():
                start(tile_copies(i + 2))

            between(i, links)

    def back_end():
        output_put.wait()
        small[...] = jnp.zeros(small.shape, F32)
        small[2:4, :] = sums[0:2, :]

        @pl.loop(0, rows // block)
        def _(i):
            at = pl.ds(pl.multiple_of(i * block, block), block)
            x = one[at, :]
            inverse = lax.rsqrt(jnp.mean(x * x, axis=-1, keepdims=True) + norm_eps)
            normed = x * inverse
            grad_hidden = two[at, :]
            small[1:2, :] += jnp.sum(grad_hidden * normed, axis=0, keepdims=True)
            result = cot[at, :].astype(F32) + rms_back(grad_hidden * gains[1:2, :], normed, inverse)
            three[at, :] = result
            low[at, :] = result.astype(BF16)

        low_swap.append(swap(low.at[:, pl.ds(theirs_narrow, narrow)], low_sib))
        gate_swap.wait_send()
        up_swap.wait_send()
        load("v", in_v, up.at[:, pl.ds(width, width)])
        load("tokens", tokens, cot)

    theirs_narrow = pl.multiple_of((1 - c) * narrow, 128)
    low_swap, head_swaps = [], {}

    def qkv_copy(i):
        at = pl.ds(pl.multiple_of(i * block_w, block_w), block_w)
        slot = lax.rem(i, 4)
        return pltpu.make_async_copy(full_qkv.at[at, :], ring.at[slot], ring_sem.at[slot])

    def attended_grad():
        loads["out"].wait()

        @pl.loop(0, rows // block)
        def _(i):
            at = pl.ds(pl.multiple_of(i * block, block), block)
            attend_grad[at, :] = dot_nt(low[at, :], w_out[...]).astype(BF16)

        for i in range(min(4, tiles)):
            qkv_copy(i).start()
        loads["right"].wait()
        low_swap[0].wait_recv()

    length = lengths[0]
    pairs = width // PAIR
    q_grad, k_grad = gate.at[:, pl.ds(0, width)], gate.at[:, pl.ds(width, width)]
    v_grad = up.at[:, pl.ds(0, width)]

    def attend_back(links):
        @pl.loop(0, pairs)
        def _(i):
            p = lax.rem((1 - c) * (pairs // 2) + i, pairs)
            at = pl.ds(pl.multiple_of(p * PAIR, PAIR), PAIR)
            shift = pl.ds(pl.multiple_of(width + p * PAIR, PAIR), PAIR)
            q, k, v, g = product[:, at], product[:, shift], up[:, shift], attend_grad[:, at]
            lane = lax.broadcasted_iota(jnp.int32, (rows, PAIR), 1)
            k_t = k.T
            sums_k, sums_v = [], []
            for head in range(2):
                inside = (lane // HEAD_DIM) == head
                k_head = jnp.where(inside, k, jnp.zeros_like(k))
                v_head = jnp.where(inside, v, jnp.zeros_like(v))
                k_turned = k_t[head * HEAD_DIM : (head + 1) * HEAD_DIM]
                parts_k, parts_v = [], []
                for b in range(rows // block):
                    upto = (b + 1) * block
                    q_block, g_block = q[b * block : upto], g[b * block : upto]
                    scores = dot_nt(k_head[:upto], q_block)
                    key = lax.broadcasted_iota(jnp.int32, scores.shape, 0)
                    query = lax.broadcasted_iota(jnp.int32, (1, block), 1) + b * block
                    log_total = logs[p, head : head + 1, b * block : upto]
                    allowed = key <= jnp.minimum(query, length - 1)
                    soft = jnp.where(allowed, jnp.exp(scores - log_total), 0.0)
                    grad_soft = dot_nt(v_head[:upto], g_block)
                    inner = jnp.sum(soft * grad_soft, axis=0, keepdims=True)
                    grad_scores = (soft * (grad_soft - inner)).astype(BF16)
                    turned[head * HEAD_DIM : (head + 1) * HEAD_DIM, b * block : upto] = dot_nn(
                        k_turned[:, :upto], grad_scores
                    )
                    parts_k.append(dot_nn(grad_scores, q_block))
                    parts_v.append(dot_nn(soft.astype(BF16), g_block))
                for parts, gathered in ((parts_k, sums_k), (parts_v, sums_v)):
                    rows_of = []
                    for r in range(rows // block):
                        piece = parts[r][r * block : (r + 1) * block]
                        for later in parts[r + 1 :]:
                            piece = piece + later[r * block : (r + 1) * block]
                        rows_of.append(piece)
                    gathered.append(jnp.concatenate(rows_of, axis=0))
            first_head = lane < HEAD_DIM
            cos, sin = cosine[...], sine[...]

            def back(x):
                return (x * cos - swap_halves(x) * sin).astype(BF16)

            gate[:, at] = back(turned[...].T * HEAD_DIM**-0.5)
            gate[:, shift] = back(jnp.where(first_head, sums_k[0], sums_k[1]))
            half_v = 0.5 * jnp.where(first_head, sums_v[0], sums_v[1])
            up[:, at] = half_v.astype(BF16)
            between(i, links)

            @pl.when(i == pairs // 2 - 1)
            def _():
                for copy in head_swaps.values():
                    copy.start()

    def qkv_tiles(links):
        @pl.loop(0, tiles)
        def _(i):
            qkv_copy(i).wait()
            slot = lax.rem(i, 4)
            at = pl.ds(pl.multiple_of(i * block_w, block_w), block_w)
            one[:, at] = (
                dot_nt(gate[:, 0:width], ring[slot, :, 0:width])
                + dot_nt(gate[:, width : 2 * width], ring[slot, :, width : 2 * width])
                + dot_nt(up[:, 0:width], ring[slot, :, 2 * width : 3 * width])
            )

            @pl.when(i + 4 < tiles)
            def _():
                qkv_copy(i + 4).start()

            between(i, links)

    def qkv_end():
        loads["tokens"].wait()
        low_swap[0].wait_send()

        @pl.loop(0, rows // block)
        def _(i):
            at = pl.ds(pl.multiple_of(i * block, block), block)
            x = cot[at, :].astype(F32)
            inverse = lax.rsqrt(jnp.mean(x * x, axis=-1, keepdims=True) + norm_eps)
            normed = x * inverse
            grad_hidden = one[at, :]
            small[0:1, :] += jnp.sum(grad_hidden * normed, axis=0, keepdims=True)
            grads = three[at, :] + rms_back(grad_hidden * gains[0:1, :], normed, inverse)
            low[at, :] = grads.astype(BF16)

        put(low, grad_tokens)
        small_step()

    def first_of(who):
        if who == W_GATE:
            loads["left"].wait()
            gate_swap.wait_recv()
        elif who == W_UP:
            up_swap.wait_recv()
        elif who in head_swaps:
            if who == W_V:
                loads["one"].wait()
            head_swaps[who].wait_recv()

    lefts = {
        W_GATE: (left, ours_of(gate, 0, side), lambda: gate_sib[...]),
        W_UP: (left, ours_of(up, 0, side), lambda: up_sib[...]),
        W_OUT: (right, ours_of(low, 0, narrow), lambda: low_sib[...]),
        W_V: (left, ours_of(up, 0, narrow), lambda: v_sib[...]),
        W_K: (left, ours_of(gate, width, narrow), lambda: k_sib[...]),
        W_Q: (left, ours_of(gate, 0, narrow), lambda: q_sib[...]),
    }

    def compute(kind):
        if kind == NORM_TWO:
            back_end()
        elif kind == ATTEND_GRAD:
            attended_grad()
        elif kind == NORM_ONE:
            qkv_end()

    def turns_of(kind, who, turns, every):
        links, at = [[] for _ in range(every)], 0
        while order and (order[0][0] <= SMALL or (order[0][0], order[0][1]) == (kind, who)):
            if order[0][0] == kind:
                order.pop(0)
                at += 1
            else:
                links[at].append(order.pop(0))
        spread = [[] for _ in range(turns)]
        for i, steps in enumerate(links):
            spread[(i + 1) * turns // every - 1] += steps
        return spread

    order = list(BACKWARD_ORDER)
    while order:
        step = order.pop(0)
        if step[0] <= SMALL:
            if step == (LEAVING, W_DOWN, 0):
                for copy in down_loads:
                    copy.wait()
            link(step)
        elif step[0] == HEAD_PAIRS:
            for key in ("q", "k", "v", "cosine", "sine", "logs"):
                loads[key].wait()
            for key, ref, land in ((W_V, v_grad, v_sib), (W_K, k_grad, k_sib), (W_Q, q_grad, q_sib)):
                head_swaps[key] = swap(ref.at[:, pl.ds(theirs_narrow, narrow)], land, begin=False)
            attend_back(turns_of(HEAD_PAIRS, 0, pairs, 8))
            put(v_grad, grad_first)
        elif step[0] == BLOCKS:
            who = step[1]
            first_of(who)
            grad_blocks(who, *lefts[who], turns_of(BLOCKS, who, count, 4))
            if who == W_UP:
                load("one", hidden_one2, left)
        elif step[0] == MLP_TILES:
            back_tiles(turns_of(MLP_TILES, 0, tiles, 4))
        elif step[0] == QKV_TILES:
            qkv_tiles(turns_of(QKV_TILES, 0, tiles, 4))
        else:
            compute(step[0])

    for reduce in reduces.values():
        reduce.drain()
    for copy in smalls:
        copy.wait_send()
    for copy in swaps:
        if not any(copy is item for item in (gate_swap, up_swap, low_swap[0])):
            copy.wait_send()
    for copy in writes:
        if copy is not output_put:
            copy.wait()


def backward_kernel(lay, lengths, tables, gains, sums, logs, weights, saved, tokens, cotangent):
    count = lay.fs
    half = count // 2
    rows, width = tokens.shape
    n, ff = weights[0].shape[1], weights[2].shape[1]
    shard, down = width // count, ff // count
    side, narrow = ff // 2, width // 2
    dma = pltpu.SemaphoreType.DMA
    vmem = pl.BlockSpec(memory_space=pltpu.VMEM)
    tall = pltpu.VMEM((rows, ff), BF16)
    flat = pltpu.VMEM((rows, width), BF16)
    full = pltpu.VMEM((rows, width), F32)
    small_steps = 1 + lay.bits + (lay.line.bit_length() - 1)
    parts = sum(BACKWARD_PARTS)
    operands = (lengths, *tables, gains, sums, logs, *weights, *saved, tokens, cotangent)
    return pl.pallas_call(
        functools.partial(backward_body, lay),
        in_specs=[pl.BlockSpec(memory_space=pltpu.SMEM)]
        + [ANY, ANY, vmem, vmem]
        + [ANY] * (len(operands) - 5),
        out_specs=[ANY] * 8 + [vmem],
        out_shape=[
            struct((rows, width), BF16),
            struct((rows, width), BF16),
            struct((rows, width), BF16),
            struct((shard, n), BF16),
            struct((shard, width), BF16),
            struct((shard, ff), BF16),
            struct((shard, ff), BF16),
            struct((down, width), BF16),
            struct((8, width), F32),
        ],
        scratch_shapes=[
            pltpu.VMEM((rows, PAIR), F32),
            pltpu.VMEM((rows, PAIR), F32),
            pltpu.VMEM(logs.shape, F32),
            tall,
            tall,
            tall,
            pltpu.VMEM((4, min(TILE, width), n), BF16),
            pltpu.VMEM((width, width), BF16),
            full,
            full,
            full,
            flat,
            pltpu.VMEM((2 * rows, width), BF16),
            pltpu.VMEM((2 * rows, width), BF16),
            flat,
            flat,
            pltpu.VMEM((rows, side), BF16),
            pltpu.VMEM((rows, side), BF16),
            pltpu.VMEM((rows, narrow), BF16),
            pltpu.VMEM((rows, narrow), BF16),
            pltpu.VMEM((rows, narrow), BF16),
            pltpu.VMEM((rows, narrow), BF16),
            pltpu.VMEM((half, down, narrow), BF16),
            pltpu.VMEM((count, shard, side), BF16),
            pltpu.VMEM((count, shard, side), BF16),
            pltpu.VMEM((4 * count, shard, narrow), BF16),
            pltpu.VMEM((half, down, narrow), BF16),
            pltpu.VMEM((half, shard, side), BF16),
            pltpu.VMEM((half, shard, side), BF16),
            pltpu.VMEM((4 * half, shard, narrow), BF16),
            pltpu.VMEM((half - 1, down, narrow), BF16),
            pltpu.VMEM((half - 1, shard, side), BF16),
            pltpu.VMEM((half - 1, shard, side), BF16),
            pltpu.VMEM((4 * (half - 1), shard, narrow), BF16),
            pltpu.VMEM((2 * small_steps, 8, width), F32),
            pltpu.VMEM((PAIR, rows), F32),
            dma((17 + half,)),
            dma((4,)),
            dma((6,)),
            dma((6,)),
            dma((3,)),
            dma((parts * count,)),
            dma((parts * count,)),
            dma((2 * parts,)),
            dma((2 * parts,)),
            pltpu.SemaphoreType.REGULAR((2 * parts,)),
            dma((parts,)),
            dma((parts,)),
            dma((parts,)),
            dma((small_steps,)),
            dma((small_steps,)),
        ],
        compiler_params=pltpu.CompilerParams(
            collective_id=1, has_side_effects=True, vmem_limit_bytes=63 * 2**20
        ),
        cost_estimate=pl.CostEstimate(
            flops=4 * rows * width * (n + width + 3 * ff),
            bytes_accessed=80 * 2**20,
            transcendentals=0,
        ),
        name="backward",
    )(*operands)


def finish_body(lay, entries, small, *refs):
    count = (len(refs) - 4) // 2
    sources, targets = refs[:count], refs[count : 2 * count]
    gain_one, gain_two, first_norm, value_norm = refs[2 * count :]
    for source, target in zip(sources, targets):
        target[...] = source[...].astype(target.dtype)

    @pl.when(pl.program_id(0) == 0)
    def _():
        rows = gain_one.shape[0]
        at = pl.ds(pl.multiple_of(lax.axis_index("fsdp") * rows, rows), rows)
        gain_one[...] = small[0, at]
        gain_two[...] = small[1, at]
        first_norm[0, 0] = jnp.sum(small[2:3, :]) / entries
        value_norm[0, 0] = jnp.sum(small[3:4, :]) / entries


def finish_kernel(lay, results):
    output, grad_tokens, grad_first, *totals, small = results
    rows, width = output.shape
    moved = [output, grad_tokens, grad_first, *totals]
    kinds = [BF16, F32, F32] + [F32] * len(totals)

    steps = 2

    def spec(item):
        return pl.BlockSpec((item.shape[0] // steps, item.shape[1]), lambda i: (i, 0))

    shard = width // lay.fs
    line = pl.BlockSpec((shard,), lambda i: (0,))
    scalar = pl.BlockSpec((1, 1), lambda i: (0, 0), memory_space=pltpu.SMEM)
    done = pl.pallas_call(
        functools.partial(finish_body, lay, rows * width * lay.dp * lay.fs),
        grid=(steps,),
        in_specs=[pl.BlockSpec(small.shape, lambda i: (0, 0))] + [spec(item) for item in moved],
        out_specs=[spec(item) for item in moved] + [line, line, scalar, scalar],
        out_shape=[struct(item.shape, kind) for item, kind in zip(moved, kinds)]
        + [struct((shard,), F32)] * 2
        + [struct((1, 1), F32)] * 2,
        compiler_params=pltpu.CompilerParams(vmem_limit_bytes=63 * 2**20),
        cost_estimate=pl.CostEstimate(
            flops=0, bytes_accessed=30 * 2**20, transcendentals=0
        ),
        name="finish",
    )(small, *moved)
    output, grad_tokens, grad_first, qkv, out, gate, up, down, gain_one, gain_two, first, value = done
    return (
        output,
        grad_tokens,
        grad_first,
        gain_one,
        qkv,
        out,
        gain_two,
        gate,
        up,
        down,
        first.reshape(()),
        value.reshape(()),
    )


def body(
    lay,
    tokens,
    first_values,
    lengths,
    gain_one,
    w_qkv,
    w_out,
    gain_two,
    w_gate,
    w_up,
    w_down,
    cotangent,
):
    rows, width = tokens.shape
    tables = tuple(jnp.asarray(table) for table in rotary_tables(rows))
    results = forward_kernel(
        lay, lengths, tokens, first_values, tables, gain_one, gain_two, cotangent, w_qkv, w_out, w_gate, w_up, w_down
    )
    weights, heads, logs, saved, gains, sums = (
        results[:5],
        results[5:8],
        results[8],
        results[9:17],
        results[17],
        results[18],
    )
    results = backward_kernel(
        lay, lengths, tables, gains, sums, logs, weights, (*heads, *saved), tokens, cotangent
    )
    return finish_kernel(lay, results)


def solution(mesh):
    both = P(AXES, None)
    rows = P("fsdp", None)
    in_specs = (both, both, P(AXES), P("fsdp"), rows, rows, P("fsdp"), rows, rows, rows, both)
    out_specs = (both, both, both, P("fsdp"), rows, rows, P("fsdp"), rows, rows, rows, P(), P())
    lay = Layout(mesh.shape["dp"], mesh.shape["fsdp"])
    return jax.shard_map(
        functools.partial(body, lay),
        mesh=mesh,
        in_specs=in_specs,
        out_specs=out_specs,
        check_vma=False,
    )
```
